32 devices in a mesh: section: 4 (over z), pair: 4 (over y, x), dp: 2 (over core).
Axes of the slice: x: 2, y: 2, z: 4, core: 2. Of those that a mesh axis runs over, the one named last changes fastest.
Arguments:
- enc_in: bfloat16 [4, 4096, 768], P(None, ('pair', 'dp')), may hold values from -6 to 6
- dec_in: bfloat16 [4, 8, 768], P(None, ('pair', 'dp')), may hold values from -6 to 6
- lengths: int32 [4, 8], P(None, ('pair', 'dp')), may hold values from 40 to 512, as said below
- weights: bfloat16 [4, 768, 6144], P('section', None, 'pair'), as said below
- gains: float32 [4, 2, 768], P('section'), may hold values from 0.25 to 1.75
- dec_cot: bfloat16 [4, 8, 768], P(None, ('pair', 'dp')), may hold values from -6 to 6
Outputs:
- dec_out: bfloat16 [4, 8, 768], P('section', ('pair', 'dp'))
- enc_grad: bfloat16 [4, 4096, 768], P('section', ('pair', 'dp'))
- dec_grad: bfloat16 [4, 8, 768], P('section', ('pair', 'dp'))
- weight_grad: float32 [4, 768, 6144], P('section', None, 'pair')
- gain_grad: float32 [4, 2, 768], P('section', None, 'pair')
The draws below stay inside these ranges and needn't reach their ends.
Inputs may be any that keep to these rules, and one draw needn't show every extreme that they name: `lengths`: in every micro-batch one passage, at a place drawn from the seed, has length 512 and another has length 40. `weights`: each section's matrices lie side by side as the steps lay them out.
All inputs are finite; a program needn't handle non-finite values.
Results may differ from the reference program's by a relative error of at most 0.025.
Values may be sent and summed in bfloat16 or wider, within the bound.
A program may use at most 576 MiB of HBM per device.

```python
import jax
import jax.numpy as jnp
from jax import lax

D = 768
HEADS = 12
HEAD = 64
FF = 3072
L = 512
LMIN = 40
MB = 4
SEQS = 8
ROWS = 4096
N_SECTION = 4


def draw_weights(key, part):
    key = jax.random.fold_in(key, 7)
    full_shape = (N_SECTION, D, 2 * FF)
    base = jax.random.normal(key, full_shape, jnp.float32)
    section_of = lax.broadcasted_iota(jnp.int32, full_shape, 0)
    block_of = lax.broadcasted_iota(jnp.int32, full_shape, 2) // D
    inner_scale = D ** (-0.5)
    output_scale = inner_scale * L ** 0.5 * 0.5
    attend_scale = jnp.where(block_of == 3, output_scale, jnp.where(block_of == 0, 1.5 * inner_scale, inner_scale))
    cross_scale = jnp.where(block_of == 5, output_scale, jnp.where(block_of == 2, 1.5 * inner_scale, inner_scale))
    feed_scale = jnp.where(block_of >= FF // D, FF ** (-0.5), inner_scale)
    scale_all = jnp.where(section_of == 0, attend_scale, jnp.where(section_of == 2, cross_scale, feed_scale))
    return (base * scale_all).astype(jnp.bfloat16)


def draw_lengths(key, part):
    key = jax.random.fold_in(key, 11)
    key_base, key_long, key_short = jax.random.split(key, 3)
    base = jax.random.randint(key_base, (MB, SEQS), LMIN, L + 1)
    longest = jax.random.randint(key_long, (MB, 1), 0, SEQS)
    shortest = (longest + 1 + jax.random.randint(key_short, (MB, 1), 0, SEQS - 1)) % SEQS
    column = lax.broadcasted_iota(jnp.int32, (MB, SEQS), 1)
    result = jnp.where(column == longest, L, jnp.where(column == shortest, LMIN, base))
    return result.astype(jnp.int32)


def level_of(stream_key, shape, cuts, least, high):
    loudness = 1.0
    for axis_at, parts in cuts:
        steps = jax.random.uniform(jax.random.fold_in(jax.random.fold_in(stream_key, 6), axis_at), (parts,), jnp.float32, least / len(cuts), high / len(cuts))
        loudness = loudness * jnp.repeat(jnp.exp(steps), shape[axis_at] // parts).reshape((-1,) + (1,) * (len(shape) - 1 - axis_at))
    return loudness


def centred(rng, extent, width, reach, shards=(), held_as=jnp.bfloat16):
    gain = level_of(rng, extent, shards, -0.22, 0.18) if shards else 1.0
    drawn = jax.random.normal(rng, extent, jnp.float32) * width * gain
    return jnp.minimum(jnp.maximum(drawn, -reach), reach).astype(held_as)


def setup_inputs(seed: int = 0) -> dict:
    seeds = jax.random.split(jax.random.key(seed), 7)
    return {
        "enc_in": centred(seeds[0], (MB, ROWS, D), 1.0, 6.0, ((1, 8),)),
        "dec_in": centred(seeds[1], (MB, SEQS, D), 1.0, 6.0, ((1, 8),)),
        "lengths": draw_lengths(jax.random.fold_in(seeds[6], 71), 0),
        "weights": draw_weights(jax.random.fold_in(seeds[6], 71), 0),
        "gains": jnp.clip(1.0 + 0.15 * jax.random.normal(seeds[4], (N_SECTION, 2, D), jnp.float32), 0.25, 1.75),
        "dec_cot": centred(seeds[5], (MB, SEQS, D), 1.0, 6.0, ((1, 8),)),
    }


@jax.custom_vjp
def low(v):
    return lax.optimization_barrier(v.astype(jnp.bfloat16)).astype(jnp.float32)

@jax.custom_vjp
def low_back(v):
    return v

def low_keep(v):
    return (low(v), None)

def low_pass(kept, grad):
    return (grad,)

def back_keep(v):
    return (v, None)

def back_low(kept, grad):
    return (low(grad),)
low.defvjp(low_keep, low_pass)
low_back.defvjp(back_keep, back_low)
EPSILON = 1e-06
NEGATIVE = -1e+30
HIGHEST = lax.Precision.HIGHEST

def norm_scale(values_in, gain_row):
    return values_in * lax.rsqrt(lax.optimization_barrier(jnp.mean(values_in * values_in, axis=-1, keepdims=True)) + EPSILON) * gain_row

def matmul(left, right):
    return jnp.matmul(left, right, precision=HIGHEST)

def column_block(weight_cols, index):
    return weight_cols[:, index * D:(index + 1) * D]

def self_attend(packed):
    queries, key_rows, value_rows, length = packed
    split_shape = (L, HEADS, HEAD)
    scores = low_back(jnp.einsum('qhd,khd->hqk', queries.reshape(split_shape), key_rows.reshape(split_shape), precision=HIGHEST) * HEAD ** (-0.5))
    live_mask = jnp.arange(L) < length
    scores = jnp.where(live_mask[None, None, :], scores, NEGATIVE)
    soft_probs = low(jax.nn.softmax(scores, axis=-1))
    mixed = jnp.einsum('hqk,khd->qhd', soft_probs, value_rows.reshape(split_shape), precision=HIGHEST)
    return mixed.reshape(L, D)

def encoder_section(enc_x, lengths_blk, weight_cols, gain_pair):
    enc_normed = low(norm_scale(enc_x, gain_pair[0]))
    queries = low(low_back(matmul(enc_normed, column_block(weight_cols, 0))))
    key_rows = low(low_back(matmul(enc_normed, column_block(weight_cols, 1))))
    value_rows = low(low_back(matmul(enc_normed, column_block(weight_cols, 2))))
    attended = low(low_back(lax.map(jax.checkpoint(self_attend), (queries, key_rows, value_rows, lengths_blk))))
    return low(low_back(enc_x + low_back(matmul(attended, column_block(weight_cols, 3).T))))

def feed(rows_in, weight_cols, gain_pair):
    normed = low(norm_scale(rows_in, gain_pair[0]))
    hidden = low_back(matmul(normed, weight_cols[:, :FF]))
    activated = low(jax.nn.gelu(hidden, approximate=True))
    middle = rows_in + low_back(matmul(activated, weight_cols[:, FF:].T))
    return norm_scale(middle, gain_pair[1])

def cross_section(encoded, dec_x, lengths_blk, weight_cols, gain_pair):
    seq_count = dec_x.shape[0]
    normed_self = low(norm_scale(dec_x, gain_pair[0]))
    self_values = low(low_back(matmul(normed_self, column_block(weight_cols, 0))))
    middle = dec_x + low_back(matmul(self_values, column_block(weight_cols, 1).T))
    normed_cross = low(norm_scale(middle, gain_pair[1]))
    queries = low(low_back(matmul(normed_cross, column_block(weight_cols, 2)))).reshape(seq_count, HEADS, HEAD)
    key_rows = low(low_back(matmul(encoded, column_block(weight_cols, 3)))).reshape(seq_count, L, HEADS, HEAD)
    value_rows = low(low_back(matmul(encoded, column_block(weight_cols, 4)))).reshape(seq_count, L, HEADS, HEAD)
    scores = low_back(jnp.einsum('bhd,bkhd->bhk', queries, key_rows, precision=HIGHEST) * HEAD ** (-0.5))
    live_mask = jnp.arange(L)[None, :] < lengths_blk[:, None]
    scores = jnp.where(live_mask[:, None, :], scores, NEGATIVE)
    soft_probs = low(jax.nn.softmax(scores, axis=-1))
    attended = low(low_back(jnp.einsum('bhk,bkhd->bhd', soft_probs, value_rows, precision=HIGHEST).reshape(seq_count, D)))
    return low(low_back(middle + low_back(matmul(attended, column_block(weight_cols, 5).T))))

def forward(enc_x, dec_x, lengths_blk, weights_all, gains_all):
    encoded_first = encoder_section(enc_x, lengths_blk, weights_all[0], gains_all[0])
    encoded = low(low_back(feed(encoded_first, weights_all[1], gains_all[1])))
    decoded = cross_section(encoded, dec_x, lengths_blk, weights_all[2], gains_all[2])
    return feed(decoded, weights_all[3], gains_all[3])

def reference(enc_in, dec_in, lengths, weights, gains, dec_cot):
    block_seqs = 8
    total_seqs = N_SECTION * SEQS
    blocks = total_seqs // block_seqs
    enc_all = enc_in.reshape(blocks, block_seqs, L, D)
    dec_all = dec_in.reshape(blocks, block_seqs, D)
    len_all = lengths.reshape(blocks, block_seqs).astype(jnp.int32)
    cot_all = dec_cot.reshape(blocks, block_seqs, D)
    weights_full = weights.astype(jnp.float32)
    gains_full = gains.astype(jnp.float32)

    def scan_step(carry, item):
        weight_total, gain_total = carry
        enc_block, dec_block, len_block, cot_block = item

        def local_forward(enc_x, dec_x, weights_all, gains_all):
            return forward(enc_x, dec_x, len_block, weights_all, gains_all)
        result, pullback = jax.vjp(local_forward, enc_block.astype(jnp.float32), dec_block.astype(jnp.float32), weights_full, gains_full)
        grad_enc, grad_dec, grad_weights, grad_gains = pullback(cot_block.astype(jnp.float32))
        return ((weight_total + grad_weights, gain_total + grad_gains), (result.astype(jnp.bfloat16), grad_enc.astype(jnp.bfloat16), grad_dec.astype(jnp.bfloat16)))
    start = (jnp.zeros(weights.shape, jnp.float32), jnp.zeros(gains.shape, jnp.float32))
    (weight_total, gain_total), (outs_all, enc_grads, dec_grads) = lax.scan(scan_step, start, (enc_all, dec_all, len_all, cot_all))
    return (outs_all.reshape(N_SECTION, SEQS, D), enc_grads.reshape(N_SECTION, ROWS, D), dec_grads.reshape(N_SECTION, SEQS, D), weight_total, gain_total)
```

```python
import jax
import jax.numpy as jnp
from jax import lax
from jax.experimental import pallas as pl
from jax.experimental.pallas import tpu as pltpu
from jax.sharding import PartitionSpec as P

D = 768
HALF = 384
K = 4
R = HALF // K
MESH = pl.DeviceIdType.MESH


def loop(n, go):
    lax.fori_loop(0, n, go, 0)


def place():
    s, p, d = lax.axis_index("section"), lax.axis_index("pair"), lax.axis_index("dp")
    c = lax.rem(d, 2)
    xn = p + 1 - 2 * lax.rem(p, 2)
    yn = p + 2 - 4 * (p // 2)
    return s, p, d, c, xn, yn, 3 - p, d + 1 - 2 * c


def enter(s, p, d, xn, yn, dn):
    bar = pltpu.get_barrier_semaphore()

    def tell(target):
        pl.semaphore_signal(bar, inc=1, device_id=target, device_id_type=MESH)

    tell((s, xn, d))
    tell((s, yn, d))
    tell((s, p, dn))
    pl.when(s < 3)(lambda: tell((s + 1, p, d)))
    pl.when(s > 0)(lambda: tell((s - 1, p, d)))
    pl.semaphore_wait(bar, 5 - (3 - s) // 3 - s // 3)


X, Y, UP, DOWN = 0, 1, 2, 3


def gather_kernel(w_ref, out_ref, buf, ssem, rsem, csend, crecv, lsem):
    s, p, d, c, xn, yn, dg, dn = place()

    def part(b, k):
        return buf.at[b, pl.ds(pl.multiple_of(c * HALF + k * R, R), R), :]

    targets = {X: (s, xn, d), Y: (s, yn, d), UP: (s + 1, p, d), DOWN: (s - 1, p, d)}

    def copy(link, b, k):
        return pltpu.make_async_remote_copy(
            src_ref=part(b, k), dst_ref=part(b, k), send_sem=ssem.at[link, b, k], recv_sem=rsem.at[b, k],
            device_id=targets[link], device_id_type=MESH)

    def sibling(b, k):
        return pltpu.make_async_remote_copy(
            src_ref=part(b, k), dst_ref=part(b, k), send_sem=csend.at[b, k], recv_sem=crecv.at[b],
            device_id=(s, p, dn), device_id_type=MESH)

    def got(b, k):
        copy(X, b, k).wait_recv()
        sibling(b, k).start()

    def local(j):
        index = jnp.where(s == 0, p + 2 * j, 4 * (1 + j) + p)
        return pltpu.make_async_copy(w_ref.at[:, pl.ds(j * D, D)], buf.at[index], lsem.at[j])

    is0, is1 = s == 0, s == 1
    has = (is0 & (p < 2)) | is1

    @pl.when(has)
    def _():
        local(0).start()
        local(1).start()
        local(0).wait()
        local(1).wait()

    enter(s, p, d, xn, yn, dn)

    @pl.when(is1)
    def _():
        def go(t, _):
            copy(DOWN, 4 * (1 + t // K) + p, lax.rem(t, K)).start()
            return 0
        loop(2 * K, go)
        copy(UP, 4 + p, 0).start()
        copy(X, 4 + p, 0).start()
        copy(Y, 4 + p, 0).start()

    xb = lax.rem(p, 2)

    @pl.when(is0)
    def _():
        def go(t, _):
            h, k = t // K, lax.rem(t, K)
            b = xb + 2 - 2 * h
            @pl.when(p < 2)
            def _():
                @pl.when(t > 1)
                def _():
                    h2, k2 = (t - 2) // K, lax.rem(t - 2, K)
                    copy(Y, xb + 2 - 2 * h2, k2).wait_send()
                    copy(X, xb + 2 - 2 * h2, k2).wait_send()
                copy(Y, b, k).start()
                copy(X, b, k).start()
                pl.when(t < K)(lambda: copy(UP, p, k).start())

            @pl.when(p >= 2)
            def _():
                got(b, k)
                pl.when(t < K)(lambda: copy(UP, p, k).start())
                copy(X, b, k).start()

            @pl.when(t > 1)
            def _():
                h2, k2 = (t - 2) // K, lax.rem(t - 2, K)
                got(3 - xb - 2 * h2, k2)
            return 0
        loop(2 * K, go)
        got(1 - xb, K - 2)
        got(1 - xb, K - 1)

        def w1(t, _):
            b, k = 4 * (1 + t // K) + p, lax.rem(t, K)
            got(b, k)
            copy(X, b, k).start()
            copy(Y, b, k).start()
            return 0
        loop(2 * K, w1)

        def rest(t, _):
            b0, k = 4 * (1 + t // K), lax.rem(t, K)
            got(b0 + xn, k)
            got(b0 + yn, k)
            got(b0 + dg, k)
            return 0
        loop(2 * K, rest)

    @pl.when(s > 0)
    def _():
        def go(t, _):
            @pl.when(t < 3 * K)
            def _():
                b, k = 4 * (t // K) + p, lax.rem(t, K)
                mine = is1 & (t >= K)
                pl.when(jnp.logical_not(mine))(lambda: got(b, k))

                @pl.when(jnp.logical_not(is1 & (t == K)))
                def _():
                    pl.when(s < 3)(lambda: copy(UP, b, k).start())
                    copy(X, b, k).start()
                    copy(Y, b, k).start()

            @pl.when((t > 1) & (t < 3 * K + 2))
            def _():
                b0, k = 4 * ((t - 2) // K), lax.rem(t - 2, K)
                got(b0 + xn, k)
                pl.when(lax.rem(k, 2) == 0)(lambda: copy(Y, b0 + xn, k).start())
                got(b0 + yn, k)
                pl.when(lax.rem(k, 2) == 1)(lambda: copy(X, b0 + yn, k).start())

            @pl.when(t > 3)
            def _():
                b0, k = 4 * ((t - 4) // K), lax.rem(t - 4, K)
                got(b0 + dg, k)
                pl.when(is1 & (b0 > 0))(lambda: copy(DOWN, b0 + dg, k).start())
            return 0

        loop(3 * K + 4, go)

    def sent(b, cond, link):
        def go(k, _):
            copy(link, b, k).wait_send()
            return 0
        pl.when(cond)(lambda: loop(K, go))

    @pl.when(is0)
    def _():
        @pl.when(p < 2)
        def _():
            for k in (K - 2, K - 1):
                copy(X, xb, k).wait_send()
                copy(Y, xb, k).wait_send()
        sent(xb, p >= 2, X)
        sent(xb + 2, p >= 2, X)
        sent(p, p >= 0, UP)

    @pl.when(s > 0)
    def _():
        sent(p, s < 3, UP)
        sent(p, s < 4, X)
        sent(p, s < 4, Y)

    def relayed(b0):
        def go(k, _):
            copy(Y, b0 + xn, 2 * k).wait_send()
            copy(X, b0 + yn, 2 * k + 1).wait_send()
            return 0
        loop(K // 2, go)

    pl.when(s > 0)(lambda: relayed(0))
    for j in range(2):
        b = 4 * (1 + j) + p
        sent(b, (s == 1) | (s == 2), UP)
        sent(b, s < 4, X)
        sent(b, s < 4, Y)
        sent(b, is1, DOWN)
        sent(4 * (1 + j) + dg, is1, DOWN)
        pl.when(s > 0)(lambda j=j: relayed(4 * (1 + j)))

    def whole(b, _):
        mine = (is0 & (p < 2) & (b < 4) & (lax.rem(b, 2) == p)) | (is1 & (b >= 4) & (lax.rem(b, 4) == p))

        @pl.when(jnp.logical_not(mine))
        def _():
            def go(k, _):
                sibling(b, k).wait_send()
                return 0
            loop(K, go)
            other = buf.at[b, pl.ds(pl.multiple_of((1 - c) * HALF, HALF), HALF), :]
            pltpu.make_async_remote_copy(
                src_ref=other, dst_ref=other, send_sem=csend.at[b, 0], recv_sem=crecv.at[b],
                device_id=(s, p, dn), device_id_type=MESH).wait_recv()
        return 0

    loop(12, whole)
    out = pltpu.make_async_copy(buf, out_ref, lsem.at[0])
    out.start()
    out.wait()


def gather(w):
    return pl.pallas_call(
        gather_kernel,
        out_shape=jax.ShapeDtypeStruct((12, D, D), jnp.bfloat16),
        in_specs=[pl.BlockSpec(memory_space=pl.ANY)],
        out_specs=pl.BlockSpec(memory_space=pl.ANY),
        scratch_shapes=[
            pltpu.VMEM((12, D, D), jnp.bfloat16),
            pltpu.SemaphoreType.DMA((4, 12, K)),
            pltpu.SemaphoreType.DMA((12, K)),
            pltpu.SemaphoreType.DMA((12, K)),
            pltpu.SemaphoreType.DMA((12,)),
            pltpu.SemaphoreType.DMA((2,)),
        ],
        compiler_params=pltpu.CompilerParams(collective_id=0, has_side_effects=True, vmem_limit_bytes=60<<20),
        name="gather",
    )(w)


def reduce_kernel(g_ref, fin_out, cb, sr, rr, ox, oy, zu, zd, fin, ssib, rsib, sxy, sz, sfy, sfib, r_rr, r_ox, r_oy, r_zu, r_zd, r_fy, r_fib, lsem):
    s, p, d, c, xn, yn, dg, dn = place()
    is0, is1 = s == 0, s == 1
    XN, YN, UPN, DNN, SIB = (s, xn, d), (s, yn, d), (s + 1, p, d), (s - 1, p, d), (s, p, dn)

    cp = pltpu.make_async_copy(g_ref, cb, lsem.at[0])
    cp.start()
    cp.wait()
    enter(s, p, d, xn, yn, dn)

    def remote(src, dst, ss, rs, to):
        return pltpu.make_async_remote_copy(src_ref=src, dst_ref=dst, send_sem=ss, recv_sem=rs, device_id=to, device_id_type=MESH)

    def mine(b, k):
        return cb.at[b, pl.ds(pl.multiple_of(c * HALF + k * R, R), R), :]

    def other(b, k):
        return cb.at[b, pl.ds(pl.multiple_of((1 - c) * HALF + k * R, R), R), :]

    def srow(b, k):
        return sr.at[b, pl.ds(pl.multiple_of(k * R, R), R), :]

    def sib(b, k):
        return remote(other(b, k), srow(b, k), ssib.at[b, k], rsib.at[b, k], SIB)

    def even(k):
        return lax.rem(k, 2) == 0

    def diag(st, k, y):
        return remote(mine(4 * st + dg, k), rr.at[st, k], sxy.at[0, st, k], r_rr.at[st, k], YN if y else XN)

    def direct(st, k, y):
        return remote(mine(4 * st + (yn if y else xn), k), (oy if y else ox).at[st, k], sxy.at[1, st, k], (r_oy if y else r_ox).at[st, k], YN if y else XN)

    def relay(st, k, y):
        return remote(mine(4 * st + (yn if y else xn), k), (oy if y else ox).at[st, k], sxy.at[2, st, k], (r_oy if y else r_ox).at[st, k], YN if y else XN)

    def both(k, f):
        pl.when(even(k))(lambda: f(0))
        pl.when(jnp.logical_not(even(k)))(lambda: f(1))

    def first(st, k):
        for q in (dg, xn, yn, p):
            sib(4 * st + q, k).wait_recv()
            m = mine(4 * st + q, k)
            m[...] = (f32(m[...]) + f32(srow(4 * st + q, k)[...])).astype(jnp.bfloat16)

        def f(odd):
            diag(st, k, not odd).start()
            direct(st, k, not odd).start()
        both(k, f)

    def second(st, k):
        diag(st, k, True).wait_recv()

        def f(odd):
            m = mine(4 * st + (yn if odd else xn), k)
            m[...] = (f32(m[...]) + f32(rr[st, k])).astype(jnp.bfloat16)
            relay(st, k, odd).start()
        both(k, f)

    def up(st, k):
        return remote(mine(4 * st + p, k), zd.at[st, k], sz.at[st, k], r_zd.at[st, k], UPN)

    def down(st, k):
        return remote(mine(4 * st + p, k), zu.at[st, k], sz.at[st, k], r_zu.at[st, k], DNN)

    def third(st, k):
        direct(st, k, True).wait_recv()
        direct(st, k, False).wait_recv()
        m = mine(4 * st + p, k)
        return m, f32(m[...]) + f32(ox[st, k]) + f32(oy[st, k])

    def finrow(j, k):
        return fin.at[j, pl.ds(pl.multiple_of(c * HALF + k * R, R), R), :]

    def fsib(j, k):
        return remote(finrow(j, k), finrow(j, k), sfib.at[j, k], r_fib.at[j, k], SIB)

    def finy(k):
        return remote(finrow(0, k), finrow(1, k), sfy.at[k], r_fy.at[k], YN)

    def last1(st, k):
        m, total = third(st, k)

        @pl.when((s == 3) | is0)
        def _():
            m[...] = total.astype(jnp.bfloat16)
            pl.when(s == 3)(lambda: down(st, k).start())
            pl.when(is0)(lambda: up(st, k).start())

        @pl.when(s == 2)
        def _():
            down(st, k).wait_recv()
            m[...] = (total + f32(zu[st, k])).astype(jnp.bfloat16)
            down(st, k).start()

        @pl.when(is1)
        def _():
            down(st, k).wait_recv()
            up(st, k).wait_recv()
            finrow(st - 1, k)[...] = (total + f32(zu[st, k]) + f32(zd[st, k])).astype(jnp.bfloat16)
            fsib(st - 1, k).start()

    def last0(k):
        m, total = third(0, k)

        @pl.when(s == 3)
        def _():
            m[...] = total.astype(jnp.bfloat16)
            down(0, k).start()

        @pl.when((s == 1) | (s == 2))
        def _():
            down(0, k).wait_recv()
            m[...] = (total + f32(zu[0, k])).astype(jnp.bfloat16)
            down(0, k).start()

        @pl.when(is0)
        def _():
            down(0, k).wait_recv()
            finrow(0, k)[...] = (total + f32(zu[0, k])).astype(jnp.bfloat16)
            pl.when(p < 2)(lambda: fsib(0, k).start())
            pl.when(p >= 2)(lambda: finy(k).start())

    def send_sib(t, _):
        st, k = lax.rem(t // K + 1, 3), lax.rem(t, K)
        for q in (dg, xn, yn, p):
            sib(4 * st + q, k).start()
        return 0

    loop(3 * K, send_sib)

    lag1 = 6 - s - 3 * ((3 - s) // 3)
    lag0 = 6 - s

    def step(t, _):
        pl.when(t < 3 * K)(lambda: first(lax.rem(t // K + 1, 3), lax.rem(t, K)))
        pl.when((t >= 1) & (t < 3 * K + 1))(lambda: second(lax.rem((t - 1) // K + 1, 3), lax.rem(t - 1, K)))
        t1 = t - lag1
        pl.when((t1 >= 0) & (t1 < 2 * K))(lambda: last1(1 + t1 // K, lax.rem(t1, K)))
        t0 = t - lag0
        pl.when((t0 >= 2 * K) & (t0 < 3 * K))(lambda: last0(t0 - 2 * K))
        return 0

    loop(3 * K + 7, step)

    @pl.when(is0 & (p < 2))
    def _():
        def go(k, _):
            finy(k).wait_recv()
            fsib(1, k).start()
            return 0
        loop(K, go)

    @pl.when(is1 | (is0 & (p < 2)))
    def _():
        def go(t, _):
            j, k = t // K, lax.rem(t, K)
            fsib(j, k).wait()
            return 0
        loop(2 * K, go)

    @pl.when(is0 & (p >= 2))
    def _():
        def go(k, _):
            finy(k).wait_send()
            return 0
        loop(K, go)

    def drain(t, _):
        st, k = t // K, lax.rem(t, K)
        for q in range(4):
            sib(4 * st + q, k).wait_send()
        diag(st, k, True).wait_send()
        direct(st, k, True).wait_send()
        relay(st, k, True).wait_send()
        pl.when((st > 0) & (s != 1))(lambda: down(st, k).wait_send())
        pl.when((st == 0) & (s > 0))(lambda: down(st, k).wait_send())
        return 0

    loop(3 * K, drain)
    cp = pltpu.make_async_copy(fin, fin_out, lsem.at[0])
    cp.start()
    cp.wait()


def reduce(g):
    bf = jnp.bfloat16
    dma = pltpu.SemaphoreType.DMA
    return pl.pallas_call(
        reduce_kernel,
        out_shape=jax.ShapeDtypeStruct((2, D, D), bf),
        in_specs=[pl.BlockSpec(memory_space=pl.ANY)],
        out_specs=pl.BlockSpec(memory_space=pl.ANY),
        scratch_shapes=[
            pltpu.VMEM((12, D, D), bf), pltpu.VMEM((12, HALF, D), bf),
            pltpu.VMEM((3, K, R, D), bf), pltpu.VMEM((3, K, R, D), bf), pltpu.VMEM((3, K, R, D), bf),
            pltpu.VMEM((3, K, R, D), bf), pltpu.VMEM((3, K, R, D), bf), pltpu.VMEM((2, D, D), bf),
            dma((12, K)), dma((12, K)), dma((3, 3, K)), dma((3, K)), dma((K,)), dma((2, K)),
            dma((3, K)), dma((3, K)), dma((3, K)), dma((3, K)), dma((3, K)), dma((K,)), dma((2, K)), dma((1,)),
        ],
        compiler_params=pltpu.CompilerParams(collective_id=1, has_side_effects=True, vmem_limit_bytes=60 << 20),
        name="reduce",
    )(g)


HEADS = 12
HEAD = 64
FF = 3072
L = 512
EPSILON = 1e-06
NEGATIVE = -1e30
ALL = ("section", "pair", "dp")


def f32(v):
    return v.astype(jnp.float32)


def bf16(v):
    return v.astype(jnp.bfloat16)


def norm(v, g):
    return v * lax.rsqrt(jnp.mean(v * v, axis=-1, keepdims=True) + EPSILON) * g


def norm_back(v, g, c):
    r = lax.rsqrt(jnp.mean(v * v, axis=-1, keepdims=True) + EPSILON)
    gc = g * c
    return r * gc - v * (r * r * r) * jnp.mean(v * gc, axis=-1, keepdims=True), jnp.sum(r * v * c, axis=0)


def gelu_both(u):
    a = 0.7978845608028654
    t = jnp.tanh(a * (u + 0.044715 * u * u * u))
    return 0.5 * u * (1.0 + t), 0.5 * (1.0 + t) + 0.5 * u * (1.0 - t * t) * a * (1.0 + 0.134145 * u * u)


def nn(a, b):
    return jnp.dot(a, b, preferred_element_type=jnp.float32)


def nt(a, b):
    return lax.dot_general(a, b, (((1,), (1,)), ((), ())), preferred_element_type=jnp.float32)


def tn(a, b):
    return lax.dot_general(a, b, (((0,), (0,)), ((), ())), preferred_element_type=jnp.float32)


def on(v, s, p):
    here = (lax.axis_index("section") == s) & (lax.axis_index("pair") == p)
    return lax.psum(jnp.where(here, v, jnp.zeros_like(v)), ("section", "pair"))


def spread(rows):
    head = lax.broadcasted_iota(jnp.int32, (16, D), 1) // HEAD == lax.broadcasted_iota(jnp.int32, (16, D), 0)
    return jnp.where(head[None], rows[:, None, :], jnp.zeros((), rows.dtype))


def body(enc_in, dec_in, lengths, weights, gains, dec_cot):
    s, p, d = lax.axis_index("section"), lax.axis_index("pair"), lax.axis_index("dp")
    pairs, dps = lax.axis_size("pair"), lax.axis_size("dp")
    me = (s * pairs + p) * dps + d
    w = weights[0]
    g = lax.all_gather(gains[0], "section")
    blocks = gather(w)
    x = f32(lax.dynamic_index_in_dim(enc_in, s, 0, False))
    dec_x = f32(lax.dynamic_index_in_dim(dec_in, s, 0, False))
    cot = f32(lax.dynamic_index_in_dim(dec_cot, s, 0, False))
    length = lax.dynamic_index_in_dim(lengths, s, 0, False)[0]
    live = lax.broadcasted_iota(jnp.int32, (1, L), 1) < length
    scale = HEAD ** -0.5

    normed = bf16(norm(x, g[0, 0]))

    def heads(v):
        return v.reshape(L, HEADS, HEAD)

    q, v, k, wo = (blocks[i] for i in range(4))
    q, k, v = bf16(nn(normed, q)), bf16(nn(normed, k)), bf16(nn(normed, v))
    scores = jnp.einsum("qhd,khd->hqk", heads(q), heads(k), preferred_element_type=jnp.float32) * scale
    probs = jax.nn.softmax(jnp.where(live[None], scores, NEGATIVE), axis=-1)
    low = bf16(probs)
    att = bf16(jnp.einsum("hqk,khd->qhd", low, heads(v), preferred_element_type=jnp.float32)).reshape(L, D)
    enc0 = bf16(x + nt(att, wo))
    e0 = f32(enc0)
    fnorm = bf16(norm(e0, g[1, 0]))
    up = [blocks[4], blocks[8], blocks[5], blocks[9]]
    dn = [blocks[6], blocks[10], blocks[7], blocks[11]]
    hid, act = [], []
    mid = e0
    for i in range(4):
        hid.append(nn(fnorm, up[i]))
        act.append(bf16(gelu_both(hid[i])[0]))
        mid = mid + nt(act[i], dn[i])
    enc = bf16(norm(mid, g[1, 1]))

    wa, wb = w[:, :D], w[:, D:]
    dec_rows = lax.all_gather(dec_x, ALL, tiled=True)
    cot_rows = lax.all_gather(cot, ALL, tiled=True)
    n = dec_rows.shape[0]
    dnorm = bf16(norm(dec_rows, g[2, 0]))
    self_v = bf16(nn(dnorm, wa))
    self_v = on(self_v, 2, 0)
    dmid = on(dec_rows + nt(self_v, wb), 2, 0)
    cnorm = bf16(norm(dmid, g[2, 1]))
    cq = on(bf16(nn(cnorm, wa)), 2, 1)
    u = on(bf16(nt(spread(cq).reshape(n * 16, D), wb)), 2, 1).reshape(n, 16, D)
    u = lax.dynamic_index_in_dim(u, me, 0, False)
    cs = jnp.where(live, nt(u, enc) * scale, NEGATIVE)
    cp = jax.nn.softmax(cs, axis=-1)
    clow = bf16(cp)
    z = bf16(nn(clow, enc))
    z_all = lax.all_gather(z, ALL)
    head = spread(jnp.ones((1, D), jnp.float32))[0]
    catt = on(bf16(jnp.sum(nn(z_all.reshape(n * 16, D), wa).reshape(n, 16, D) * head, axis=1)), 2, 2)
    decoded = bf16(on(dmid + nt(catt, wb), 2, 2))
    dec32 = f32(decoded)
    tnorm = bf16(norm(dec32, g[3, 0]))
    thid = nn(tnorm, w)
    thid = lax.ppermute(thid, "pair", [(0, 2), (1, 3)])
    ta, td = gelu_both(thid)
    tact = bf16(ta)
    downs = (s == 3) & (p >= 2)
    tmid = dec32 + lax.psum(jnp.where(downs, nt(tact, w), 0.0), ("section", "pair"))
    dec_out = bf16(norm(tmid, g[3, 1]))
    g_tmid, gg31 = norm_back(tmid, g[3, 1], cot_rows)
    g_tb = bf16(g_tmid)
    g_thid = bf16(td * nn(g_tb, w))
    g_thid_up = lax.ppermute(g_thid, "pair", [(2, 0), (3, 1)])
    g_tn = lax.psum(jnp.where((s == 3) & (p < 2), nt(g_thid_up, w), 0.0), ("section", "pair"))
    gp, gg30 = norm_back(dec32, g[3, 0], g_tn)
    g_dec = bf16(g_tmid + gp)
    dw3 = jnp.where(p < 2, tn(tnorm, g_thid_up), tn(g_tb, tact))
    g_catt = on(bf16(nn(g_dec, wb)), 2, 2)
    vv = on(bf16(nt(spread(g_catt).reshape(n * 16, D), wa)), 2, 2).reshape(n, 16, D)
    vv = lax.dynamic_index_in_dim(vv, me, 0, False)
    g_cp = nt(vv, enc)
    g_cs = bf16(cp * (g_cp - jnp.sum(g_cp * cp, axis=-1, keepdims=True)))
    y = bf16(nn(g_cs, enc) * scale)
    g_enc = bf16(tn(g_cs, bf16(f32(u) * scale)) + tn(clow, vv))
    y_all = lax.all_gather(y, ALL)
    g_cq = on(bf16(jnp.sum(nn(y_all.reshape(n * 16, D), wb).reshape(n, 16, D) * head, axis=1)), 2, 1)
    g_cn = on(nt(g_cq, wa), 2, 1)
    gp, gg21 = norm_back(dmid, g[2, 1], g_cn)
    g_dmid = f32(g_dec) + gp
    g_sb = bf16(g_dmid)
    g_sv = on(bf16(nn(g_sb, wb)), 2, 0)
    g_dn = on(nt(g_sv, wa), 2, 0)
    gp, gg20 = norm_back(dec_rows, g[2, 0], g_dn)
    dec_grad = bf16(g_dmid + gp)
    yz = lax.dynamic_index_in_dim(jnp.stack([y_all, z_all]), jnp.clip(p - 1, 0, 1), 0, False).reshape(n * 16, D)
    dw_a = jnp.where(p == 0, tn(dnorm, g_sv), jnp.where(p == 1, tn(cnorm, g_cq), tn(yz, spread(g_catt).reshape(n * 16, D))))
    dw_b = jnp.where(p == 0, tn(g_sb, self_v), jnp.where(p == 1, tn(yz, spread(cq).reshape(n * 16, D)), tn(g_dec, catt)))
    dw2 = jnp.where(p == 3, 0.0, jnp.concatenate([dw_a, dw_b], axis=1))

    g_mid, gg11 = norm_back(mid, g[1, 1], f32(g_enc))
    g_fb = bf16(g_mid)
    g_fn = jnp.zeros((L, D), jnp.float32)
    d_up, d_dn = [], []
    for i in range(4):
        gh = bf16(gelu_both(hid[i])[1] * nn(g_fb, dn[i]))
        d_up.append(bf16(tn(fnorm, gh)))
        d_dn.append(bf16(tn(g_fb, act[i])))
        g_fn = g_fn + nt(gh, up[i])
    gp, gg10 = norm_back(e0, g[1, 0], g_fn)
    g_e0 = bf16(g_mid + gp)
    g_att = bf16(nn(g_e0, wo))
    d_wo = bf16(tn(g_e0, att))
    g_v = bf16(jnp.einsum("hqk,qhd->khd", low, heads(g_att), preferred_element_type=jnp.float32)).reshape(L, D)
    g_p = jnp.einsum("qhd,khd->hqk", heads(g_att), heads(v), preferred_element_type=jnp.float32)
    g_s = bf16(probs * (g_p - jnp.sum(g_p * probs, axis=-1, keepdims=True)))
    g_q = bf16(jnp.einsum("hqk,khd->qhd", g_s, heads(k), preferred_element_type=jnp.float32) * scale).reshape(L, D)
    g_k = bf16(jnp.einsum("hqk,qhd->khd", g_s, heads(q), preferred_element_type=jnp.float32) * scale).reshape(L, D)
    g_n = nt(g_q, blocks[0]) + nt(g_k, blocks[2]) + nt(g_v, blocks[1])
    gp, gg00 = norm_back(x, g[0, 0], g_n)
    enc_grad = bf16(f32(g_e0) + gp)
    grads = jnp.stack([bf16(tn(normed, g_q)), bf16(tn(normed, g_v)), bf16(tn(normed, g_k)), d_wo,
                       d_up[0], d_up[2], d_dn[0], d_dn[2], d_up[1], d_up[3], d_dn[1], d_dn[3]])
    fin = reduce(grads)
    if dps > 2:
        groups = [[i for i in range(dps) if i % 2 == c] for c in range(2)]
        fin = bf16(lax.psum(fin, "dp", axis_index_groups=groups))
    full = f32(jnp.concatenate([fin[0], fin[1]], axis=1))
    dw = jnp.where(s == 0, jnp.where(p < 2, full, 0.0), jnp.where(s == 1, full, jnp.where(s == 2, dw2, dw3)))
    zero = jnp.zeros((D,), jnp.float32)
    part = lax.psum(jnp.stack([gg00, zero, gg10, gg11]).reshape(2, 2, D), ALL)
    gg = jnp.concatenate([part, jnp.stack([gg20, gg21, gg30, gg31]).reshape(2, 2, D)])
    gg = lax.dynamic_index_in_dim(gg, s, 0, False)
    width = D // pairs
    gg = lax.dynamic_slice_in_dim(gg, p * width, width, 1)
    own = lambda a: lax.dynamic_index_in_dim(a, me, 0, False)[None, None]
    return own(dec_out), enc_grad[None], own(dec_grad), dw[None], gg[None]


def solution(mesh):
    rows, both = P(None, ("pair", "dp"), None), P("section", ("pair", "dp"), None)
    return jax.shard_map(
        body, mesh=mesh,
        in_specs=(rows, rows, P(None, ("pair", "dp")), P("section", None, "pair"), P("section", None, None), rows),
        out_specs=(both, both, both, P("section", None, "pair"), P("section", None, "pair")),
        check_vma=False)
```

```python
import functools

import jax
import jax.numpy as jnp
from jax import lax
from jax.experimental import pallas as pl
from jax.experimental.pallas import tpu as pltpu
from jax.sharding import PartitionSpec as P

D = 768
HALF = 384
HEADS = 12
HEAD = 64
L = 512
EPSILON = 1e-06
NEGATIVE = -1e30
K = 4
R = HALF // K
MESH = pl.DeviceIdType.MESH
X, Y, UP, DOWN = 0, 1, 2, 3
BF = jnp.bfloat16
F32 = jnp.float32


def f32(v):
    return v.astype(F32)


def bf16(v):
    return v.astype(BF)


def loop(n, go, start=0):
    def step(i, carry):
        go(i)
        return carry

    lax.fori_loop(start, n, step, 0)


def norm(v, g):
    return v * lax.rsqrt(jnp.mean(v * v, axis=-1, keepdims=True) + EPSILON) * g


def norm_back(v, g, c):
    r = lax.rsqrt(jnp.mean(v * v, axis=-1, keepdims=True) + EPSILON)
    gc = g * c
    back = r * gc - v * (r * r * r) * jnp.mean(v * gc, axis=-1, keepdims=True)
    return back, jnp.sum(r * v * c, axis=0, keepdims=True)


def gelu_both(u):
    a = 0.7978845608028654
    t = jnp.tanh(a * (u + 0.044715 * u * u * u))
    return 0.5 * u * (1.0 + t), 0.5 * (1.0 + t) + 0.5 * u * (1.0 - t * t) * a * (1.0 + 0.134145 * u * u)


def nn(a, b):
    return jnp.dot(a, b, preferred_element_type=F32)


def nt(a, b):
    return lax.dot_general(a, b, (((1,), (1,)), ((), ())), preferred_element_type=F32)


def tn(a, b):
    return lax.dot_general(a, b, (((0,), (0,)), ((), ())), preferred_element_type=F32)


def iota(shape, dim):
    return lax.broadcasted_iota(jnp.int32, shape, dim)


def head_mask(rows):
    return iota((rows, D), 1) // HEAD == lax.rem(iota((rows, D), 0), 16)


def pick(slot):
    return bf16(f32(iota((32, L), 1) == iota((32, L), 0) * 16 + slot))


def gather16():
    return bf16(f32(iota((32, L), 1) // 16 == iota((32, L), 0)))


def spread(rows):
    wide = nn(bf16(f32(iota((L, 32), 0) // 16 == iota((L, 32), 1))), rows)
    return bf16(jnp.where(head_mask(L), wide, 0.0))


SCRATCH = dict(
    W=((14, D, D), BF), cb=((6, D, D), BF), og=((2, HALF, D), BF), sr=((12, HALF, D), BF),
    rr=((3, K, R, D), BF), ox=((3, K, R, D), BF), oy=((3, K, R, D), BF), zu=((3, K, R, D), BF), zd=((2, K, R, D), BF),
    A=((8, L, D), BF), enc=((L, D), BF), B=((4, L, D), BF), T=((3, D, L), BF), mid=((L, D), F32), gfn=((L, D), F32), ring=((4, L, L), BF),
    gall=((4, 1, 2 * D), F32), DI=((32, 1, D), F32), CR=((32, 1, D), F32), DM=((32, 1, D), F32), DR=((32, 1, D), F32),
    ROWS=((32, 1, D), F32), ROWS2=((32, 1, 2 * D), F32), dmrow=((1, D), F32), u=((16, D), BF), drow=((1, D), F32),
    AB=((2, 32, D), BF), GP=((32, D), BF), GH=((2, 32, D), BF), PB=((4, 32, D), BF), orow=((1, 2 * D), F32), GT=((4, 1, D), F32),
    fac=((2, 16, D), BF), FB=((2, 16, 16, D), BF), GD=((32, D), F32), GB=((32, 1, 2 * D), F32), gg=((4, 1, 2 * D), F32),
    cp=((16, L), F32), keep=((2, 32, D), BF),
)
SEMS = dict(
    ssem=(4, 12, K), rsem=(12, K), csend=(12, K), crecv=(12,), lsem=(8,), psem=(4,), s2=(4, 4, 2), r2=(4, 2), c2s=(4, 2), c2r=(4, 2),
    spre=(2,), rdi=(1,), scr=(4,), rcr=(1,), sg=(4,), rg=(1,), sdm=(17,), rdm=(2,), su=(16,), ru=(1,), sd1=(8,), rdr=(1,),
    sact=(3,), ract=(3,), sp=(4,), rpb=(4,), sgh=(2,), rgh=(2,), so=(16,), ror=(1,), sgt=(32,), rgt=(4,),
    sfb=(2,), rfb=(2,), sfs=(1,), rfs=(1,), sgd=(1,), rgd=(1,), sdg=(16,), rdg=(1,), sgb=(4, 8), rgb=(1,),
    ssib=(12,), rsib=(12,), sxy=(3, 3, K), sz=(3, K), rrr=(3, K), rox=(3, K), roy=(3, K), rzu=(3, K), rzd=(3, K),
    sfin=(2, K, 3), rfin=(2, K, 2),
)


class Refs:
    pass


def kernel(names, w, xall, dec, cot, gains, lens, *rest):
    o = Refs()
    for name, ref in zip(names, rest, strict=True):
        setattr(o, name, ref)
    s, p, d = lax.axis_index("section"), lax.axis_index("pair"), lax.axis_index("dp")
    c = lax.rem(d, 2)
    base = d - c
    xn = p + 1 - 2 * lax.rem(p, 2)
    yn = p + 2 - 4 * (p // 2)
    dg = 3 - p
    xb = lax.rem(p, 2)
    is0, is1, is2, is3 = s == 0, s == 1, s == 2, s == 3
    lin = (s * 4 + p) * 2 + c
    row = c * 16 + p * 4 + s
    W, A, B, T, cb = o.W, o.A, o.B, o.T, o.cb

    def dev(s_, p_, c_):
        return (s_, p_, base + c_)

    TO = {X: dev(s, xn, c), Y: dev(s, yn, c), UP: dev(s + 1, p, c), DOWN: dev(s - 1, p, c)}
    SIB = dev(s, p, 1 - c)

    def remote(src, dst, ss, rs, to):
        return pltpu.make_async_remote_copy(src_ref=src, dst_ref=dst, send_sem=ss, recv_sem=rs, device_id=to, device_id_type=MESH)

    def local(src, dst, sem):
        return pltpu.make_async_copy(src, dst, sem)

    def when(cond, f):
        pl.when(cond)(f)

    def unless(cond, f):
        pl.when(jnp.logical_not(cond))(f)

    own_here = (is0 & (p < 2)) | is1

    def own_block(j):
        return jnp.where(is0, p + 2 * j, jnp.where(is1, 4 * (1 + j) + p, 12 + j))

    def load_own(j):
        return local(w.at[:, pl.ds(j * D, D)], W.at[own_block(j)], o.lsem.at[j])

    def load_ws(j):
        return local(w.at[:, pl.ds(j * D, D)], cb.at[j], o.lsem.at[j])

    def load_w3():
        return local(w.at[:, pl.ds(pl.multiple_of(c * D, D), D)], cb.at[0], o.lsem.at[0])

    loads_own = own_here | (is2 & (p == 2))

    @pl.when(loads_own)
    def _():
        load_own(0).start()
        load_own(1).start()

    @pl.when(is2 & (p < 2))
    def _():
        load_ws(0).start()
        load_ws(1).start()

    when(is3, lambda: load_w3().start())
    load_x = local(xall.at[s], A.at[0], o.lsem.at[2])
    load_x.start()

    bar = pltpu.get_barrier_semaphore()

    def tell(i):
        @pl.when(i != lin)
        def _():
            pl.semaphore_signal(bar, inc=1, device_id=dev(i // 8, lax.rem(i // 2, 4), lax.rem(i, 2)), device_id_type=MESH)

    loop(32, tell)
    pl.semaphore_wait(bar, 31)

    @pl.when(loads_own)
    def _():
        load_own(0).wait()
        load_own(1).wait()

    @pl.when(is2 & (p < 2))
    def _():
        load_ws(0).wait()
        load_ws(1).wait()

    when(is3, lambda: load_w3().wait())

    def part(b, k):
        return W.at[b, pl.ds(pl.multiple_of(c * HALF + k * R, R), R), :]

    def copy(link, b, k):
        return remote(part(b, k), part(b, k), o.ssem.at[link, b, k], o.rsem.at[b, k], TO[link])

    def sibling(b, k):
        return remote(part(b, k), part(b, k), o.csend.at[b, k], o.crecv.at[b], SIB)

    def got(b, k):
        copy(X, b, k).wait_recv()
        sibling(b, k).start()

    @pl.when(is1)
    def _():
        loop(2 * K, lambda t: copy(DOWN, 4 * (1 + t // K) + p, lax.rem(t, K)).start())
        copy(UP, 4 + p, 0).start()
        copy(X, 4 + p, 0).start()
        copy(Y, 4 + p, 0).start()

    def step0(t):
        @pl.when(t < 2 * K)
        def _():
            k = lax.rem(t, K)
            b = xb + 2 - 2 * (t // K)

            @pl.when(p < 2)
            def _():
                @pl.when(t > 1)
                def _():
                    b2, k2 = xb + 2 - 2 * ((t - 2) // K), lax.rem(t - 2, K)
                    copy(Y, b2, k2).wait_send()
                    copy(X, b2, k2).wait_send()

                copy(Y, b, k).start()
                copy(X, b, k).start()
                when(t < K, lambda: copy(UP, p, k).start())

            @pl.when(p >= 2)
            def _():
                got(b, k)
                when(t < K, lambda: copy(UP, p, k).start())
                copy(X, b, k).start()

        @pl.when((t > 1) & (t < 2 * K + 2))
        def _():
            got(3 - xb - 2 * ((t - 2) // K), lax.rem(t - 2, K))

        @pl.when((t >= 2 * K) & (t < 4 * K))
        def _():
            b, k = 4 * ((t - K) // K) + p, lax.rem(t, K)
            got(b, k)
            copy(X, b, k).start()
            copy(Y, b, k).start()

        @pl.when(t >= 2 * K + 2)
        def _():
            b0, k = 4 * ((t - K - 2) // K), lax.rem(t - 2, K)
            got(b0 + xn, k)
            got(b0 + yn, k)
            got(b0 + dg, k)

    def step1(t):
        @pl.when(t < 3 * K)
        def _():
            b, k = 4 * (t // K) + p, lax.rem(t, K)
            unless(is1 & (t >= K), lambda: got(b, k))

            @pl.when(jnp.logical_not(is1 & (t == K)))
            def _():
                when(s < 3, lambda: copy(UP, b, k).start())
                copy(X, b, k).start()
                copy(Y, b, k).start()

        @pl.when((t > 1) & (t < 3 * K + 2))
        def _():
            b0, k = 4 * ((t - 2) // K), lax.rem(t - 2, K)
            got(b0 + xn, k)
            when(lax.rem(k, 2) == 0, lambda: copy(Y, b0 + xn, k).start())
            got(b0 + yn, k)
            when(lax.rem(k, 2) == 1, lambda: copy(X, b0 + yn, k).start())

        @pl.when(t > 3)
        def _():
            b0, k = 4 * ((t - 4) // K), lax.rem(t - 4, K)
            got(b0 + dg, k)
            when(is1 & (b0 > 0), lambda: copy(DOWN, b0 + dg, k).start())

    def pump(a0, b0, a1, b1):
        when(is0, lambda: loop(b0, step0, a0))
        when(s > 0, lambda: loop(b1, step1, a1))

    def mine_block(b):
        return (is0 & (p < 2) & (b < 4) & (lax.rem(b, 2) == p)) | (is1 & (b >= 4) & (lax.rem(b, 4) == p))

    def ready(b):
        @pl.when(jnp.logical_not(mine_block(b)))
        def _():
            loop(K, lambda k: sibling(b, k).wait_send())
            other = W.at[b, pl.ds(pl.multiple_of((1 - c) * HALF, HALF), HALF), :]
            remote(other, other, o.csend.at[b, 0], o.crecv.at[b], SIB).wait_recv()

    def part2(q, k):
        return W.at[12 + q // 2, pl.ds(pl.multiple_of(lax.rem(q, 2) * HALF + c * 192 + k * 96, 96), 96), :]

    def copy2(link, q, k):
        return remote(part2(q, k), part2(q, k), o.s2.at[link, q, k], o.r2.at[q, k], TO[link])

    def sib2(q, k):
        return remote(part2(q, k), part2(q, k), o.c2s.at[q, k], o.c2r.at[q, k], SIB)

    def got2(q, k):
        copy2(X, q, k).wait_recv()
        sib2(q, k).start()

    ROUTES = {2: [(X, 2), (X, 3), (Y, 0), (Y, 1)], 3: [(Y, 2), (Y, 3)], 0: [(X, 0), (X, 1)], 1: [(Y, 0), (X, 2), (Y, 1), (X, 3)]}

    def w2_first(k):
        for corner, routes in ROUTES.items():
            @pl.when(is2 & (p == corner))
            def _(corner=corner, routes=routes):
                for link, q in routes:
                    if corner != 2:
                        got2(q, k)
                    if corner == q:
                        copy2(UP, q, k).start()
                        copy2(DOWN, q, k).start()
                    copy2(link, q, k).start()

        @pl.when(s != 2)
        def _():
            got2(p, k)
            when(is1, lambda: copy2(DOWN, p, k).start())
            copy2(X, p, k).start()
            copy2(Y, p, k).start()

    def w2_second(k):
        @pl.when(s != 2)
        def _():
            got2(xn, k)
            got2(yn, k)
            if k == 0:
                copy2(Y, xn, k).start()
            else:
                copy2(X, yn, k).start()

        for corner, qs in ((3, (0, 1)), (0, (2, 3))):
            @pl.when(is2 & (p == corner))
            def _(qs=qs):
                for q in qs:
                    got2(q, k)

    def w2_third(k):
        when(s != 2, lambda: got2(dg, k))

    def w2_ready():
        @pl.when(jnp.logical_not(is2 & (p == 2)))
        def _():
            for q in range(4):
                for k in range(2):
                    sib2(q, k).wait()

    def w2_sent():
        for k in range(2):
            for corner, routes in ROUTES.items():
                @pl.when(is2 & (p == corner))
                def _(corner=corner, routes=routes, k=k):
                    copy2(UP, corner, k).wait_send()
                    copy2(DOWN, corner, k).wait_send()
                    for link, q in routes:
                        copy2(link, q, k).wait_send()

            @pl.when(s != 2)
            def _(k=k):
                when(is1, lambda: copy2(DOWN, p, k).wait_send())
                copy2(X, p, k).wait_send()
                copy2(Y, p, k).wait_send()
                if k == 0:
                    copy2(Y, xn, k).wait_send()
                else:
                    copy2(X, yn, k).wait_send()

    def send_gains(i):
        @pl.when(i == s)
        def _():
            local(gains, o.gall.at[s], o.rg.at[0]).start()

        unless(i == s, lambda: remote(gains, o.gall.at[s], o.sg.at[i], o.rg.at[0], dev(i, p, c)).start())

    loop(4, send_gains)
    four = pl.ds(c * 16 + p * 4, 4)

    def send_dec(i):
        @pl.when((p == 0) & (i == c))
        def _():
            local(dec, o.DI.at[four], o.rdi.at[0]).start()

        unless((p == 0) & (i == c), lambda: remote(dec, o.DI.at[four], o.spre.at[i], o.rdi.at[0], dev(2, 0, i)).start())

    when(is2, lambda: loop(2, send_dec))

    def send_cot(i):
        @pl.when((p == 2 + i // 2) & (lax.rem(i, 2) == c))
        def _():
            local(cot, o.CR.at[four], o.rcr.at[0]).start()

        unless((p == 2 + i // 2) & (lax.rem(i, 2) == c),
               lambda: remote(cot, o.CR.at[four], o.scr.at[i], o.rcr.at[0], dev(3, 2 + i // 2, lax.rem(i, 2))).start())

    when(is3, lambda: loop(4, send_cot))

    def gain(sec, r):
        return o.gall[sec][:, r * D:(r + 1) * D]

    def to_core(f):
        loop(16, lambda i: f(i, i // 4, lax.rem(i, 4)))

    def others(f):
        to_core(lambda i, s_, p_: unless((s_ == s) & (p_ == p), lambda: f(i, s_, p_).wait_send()))

    def decoder_start0():
        local(o.DI, o.DI, o.rdi.at[0]).wait()
        rows = o.DI[:, 0, :]
        dn = bf16(norm(rows, gain(2, 0)))
        o.keep[0] = dn
        sv = bf16(nn(dn, cb[0]))
        o.keep[1] = sv
        o.DM[:, 0, :] = rows + nt(sv, cb[1])
        remote(o.DM, o.DM, o.sdm.at[16], o.rdm.at[1], dev(2, 1, c)).start()

        def go(i, s_, p_):
            me = (s_ == s) & (p_ == p)
            src = o.DM.at[c * 16 + p_ * 4 + s_]
            when(me, lambda: local(src, o.dmrow, o.rdm.at[0]).start())
            unless(me, lambda: remote(src, o.dmrow, o.sdm.at[i], o.rdm.at[0], dev(s_, p_, c)).start())

        to_core(go)

    def decoder_start1():
        remote(o.DM, o.DM, o.sdm.at[16], o.rdm.at[1], dev(2, 1, c)).wait_recv()
        cn = bf16(norm(o.DM[:, 0, :], gain(2, 1)))
        o.keep[0] = cn
        q = bf16(nn(cn, cb[0]))
        o.keep[1] = q
        cb[2, 0:L, :] = bf16(nt(spread(q), cb[1]))

        def go(i, s_, p_):
            me = (s_ == s) & (p_ == p)
            src = cb.at[2, pl.ds(pl.multiple_of((c * 16 + p_ * 4 + s_) * 16, 16), 16), :]
            when(me, lambda: local(src, o.u, o.ru.at[0]).start())
            unless(me, lambda: remote(src, o.u, o.su.at[i], o.ru.at[0], dev(s_, p_, c)).start())

        to_core(go)

    x_, q_, k_, v_, att_, enc0_, fnorm_, act_ = range(8)

    def tiles(f, n=2, size=256):
        loop(n, lambda i: f(pl.ds(pl.multiple_of(i * size, size), size)))

    def turned(src, dst):
        for j in range(6):
            dst[j * 128:(j + 1) * 128, :] = src[:, j * 128:(j + 1) * 128].T

    def turned_back(src, dst):
        for j in range(6):
            dst[:, j * 128:(j + 1) * 128] = src[j * 128:(j + 1) * 128, :].T

    live = iota((L, 1), 0) < lens[0]

    def project(rows):
        n = bf16(norm(f32(A[x_, rows, :]), gain(0, 0)))
        A[q_, rows, :] = bf16(bf16(nn(n, W[0])) * 0.125)
        A[v_, rows, :] = bf16(nn(n, W[1]))
        A[k_, rows, :] = bf16(nn(n, W[2]))

    def padded(ref, i, hh):
        rows = ref[pl.ds(pl.multiple_of(i * 128 + hh * 64, 64), 64), :]
        zero = jnp.zeros((64, L), BF)
        return jnp.concatenate([rows, zero] if hh == 0 else [zero, rows], axis=0)

    def lanes(i):
        return pl.ds(pl.multiple_of(i * 128, 128), 128)

    def half_rows(i, hh):
        return pl.ds(pl.multiple_of(i * 128 + hh * 64, 64), 64)

    def spill(i, hh):
        return local(o.ring.at[2 * lax.rem(i, 2) + hh], o.probs.at[2 * i + hh], o.psem.at[2 * lax.rem(i, 2) + hh])

    def fetch(i, hh):
        return local(o.probs.at[2 * i + hh], o.ring.at[2 * lax.rem(i, 2) + hh], o.psem.at[2 * lax.rem(i, 2) + hh])

    def attend(i):
        kp = A[k_, :, lanes(i)]
        for hh in range(2):
            when(i > 1, lambda: spill(i - 2, hh).wait())
            qp = padded(T.at[0], i, hh)
            vt = T[1, half_rows(i, hh), :]
            for t in range(2):
                cols = slice(t * 256, (t + 1) * 256)
                sc = jnp.where(live, nn(kp, qp[:, cols]), NEGATIVE)
                e = jnp.exp(sc - jnp.max(sc, axis=0, keepdims=True))
                pr = bf16(e * (1.0 / jnp.sum(e, axis=0, keepdims=True)))
                o.ring[2 * lax.rem(i, 2) + hh, :, cols] = pr
                T[2, half_rows(i, hh), cols] = bf16(nn(vt, pr))
            spill(i, hh).start()

    def after_attention(rows):
        e0 = bf16(f32(A[x_, rows, :]) + nt(A[att_, rows, :], W[3]))
        A[enc0_, rows, :] = e0
        A[fnorm_, rows, :] = bf16(norm(f32(e0), gain(1, 0)))
        o.mid[rows, :] = f32(e0)

    HID = {0: (4, 6), 1: (8, 10), 2: (5, 7), 3: (9, 11)}

    def feed(i):
        def hidden(rows):
            B[i, rows, :] = bf16(nn(A[fnorm_, rows, :], W[HID[i][0]]))

        def active(rows):
            A[act_, rows, :] = bf16(gelu_both(f32(B[i, rows, :]))[0])

        def out(rows):
            o.mid[rows, :] += nt(A[act_, rows, :], W[HID[i][1]])

        tiles(hidden)
        tiles(active, 8, 64)
        tiles(out)

    pump(0, 10, 0, 8)
    for b in range(4):
        ready(b)
    load_x.wait()
    local(o.gall, o.gall, o.rg.at[0]).wait()
    when(is2 & (p == 0), decoder_start0)
    tiles(project)
    turned(A.at[q_], T.at[0])
    turned(A.at[v_], T.at[1])
    pump(10, 12, 8, 9)
    when(is2 & (p == 1), decoder_start1)
    loop(2, attend)
    pump(12, 13, 9, 10)
    loop(4, attend, 2)
    pump(13, 14, 10, 11)
    loop(6, attend, 4)
    for i in (4, 5):
        for hh in range(2):
            spill(i, hh).wait()
    turned_back(T.at[2], A.at[att_])
    tiles(after_attention)
    pump(14, 16, 11, 12)
    for b in range(4, 8):
        ready(b)
    feed(0)
    pump(16, 17, 12, 14)
    feed(2)
    pump(17, 18, 14, 16)
    for b in range(8, 12):
        ready(b)
    w2_first(0)
    w2_first(1)
    feed(1)
    w2_second(0)
    w2_second(1)
    feed(3)
    w2_third(0)
    w2_third(1)

    def encoded(rows):
        o.enc[rows, :] = bf16(norm(o.mid[rows, :], gain(1, 1)))

    tiles(encoded)
    w2_ready()

    remote(o.u, o.u, o.su.at[0], o.ru.at[0], SIB).wait_recv()
    remote(o.dmrow, o.dmrow, o.sdm.at[0], o.rdm.at[0], SIB).wait_recv()
    enc = o.enc
    live_row = iota((1, L), 1) < lens[0]
    cs = jnp.where(live_row, nt(o.u[...], enc[...]) * 0.125, NEGATIVE)
    e = jnp.exp(cs - jnp.max(cs, axis=-1, keepdims=True))
    cp = e / jnp.sum(e, axis=-1, keepdims=True)
    o.cp[...] = cp
    z = bf16(nn(bf16(cp), enc[...]))
    catt = bf16(jnp.sum(jnp.where(head_mask(16), nn(z, W[12]), 0.0), axis=0, keepdims=True))
    decoded = f32(bf16(o.dmrow[...] + nt(jnp.broadcast_to(catt, (16, D)), W[13])[0:1]))
    o.drow[...] = decoded
    o.fac[1] = z

    def send_row(i):
        p_, c_ = i // 2, lax.rem(i, 2)
        me = is3 & (p_ == p) & (c_ == c)
        when(me, lambda: local(o.drow, o.DR.at[row], o.rdr.at[0]).start())
        unless(me, lambda: remote(o.drow, o.DR.at[row], o.sd1.at[i], o.rdr.at[0], dev(3, p_, c_)).start())

    loop(8, send_row)
    up_dev, down_dev = is3 & (p < 2), is3 & (p >= 2)
    j = 2 * lax.rem(p, 2) + c
    w3 = cb

    def act_copy():
        return remote(o.AB.at[c], o.AB.at[c], o.sact.at[0], o.ract.at[0], TO[Y])

    def gp_copy():
        return remote(o.GP, o.GP, o.sact.at[1], o.ract.at[1], TO[Y])

    def ab_sib():
        return remote(o.AB.at[c], o.AB.at[c], o.sact.at[2], o.ract.at[2], SIB)

    def gh_copy():
        return remote(o.GH.at[c], o.GH.at[c], o.sgh.at[0], o.rgh.at[0], TO[Y])

    def gh_sib():
        return remote(o.GH.at[c], o.GH.at[c], o.sgh.at[1], o.rgh.at[1], SIB)

    def rows_here():
        local(o.DR, o.DR, o.rdr.at[0]).wait()

    @pl.when(up_dev)
    def _():
        rows_here()
        tnorm = bf16(norm(o.DR[:, 0, :], gain(3, 0)))
        o.keep[0] = tnorm
        act, slope = gelu_both(nn(tnorm, w3[0]))
        o.AB[c] = bf16(act)
        act_copy().start()
        o.GP[...] = bf16(slope)
        gp_copy().start()

    def pb_copy(i):
        return remote(o.PB.at[j], o.PB.at[j], o.sp.at[i], o.rpb.at[j], dev(3, 2 + i // 2, lax.rem(i, 2)))

    def pb_from(i):
        return remote(o.PB.at[i], o.PB.at[i], o.sp.at[i], o.rpb.at[i], SIB)

    def out_copy(i):
        s_, p_ = i // 2, 2 * lax.rem(p, 2) + lax.rem(i, 2)
        return remote(o.ROWS2.at[c * 16 + p_ * 4 + s_], o.orow, o.so.at[i], o.ror.at[0], dev(s_, p_, c)), (s_ == s) & (p_ == p), \
            local(o.ROWS2.at[c * 16 + p_ * 4 + s_], o.orow, o.ror.at[0])

    @pl.when(down_dev)
    def _():
        act_copy().wait_recv()
        o.PB[j] = bf16(nt(o.AB[c], w3[0]))
        loop(4, lambda i: unless(i == j, lambda: pb_copy(i).start()))
        ab_sib().start()
        rows_here()
        local(o.CR, o.CR, o.rcr.at[0]).wait()
        loop(4, lambda i: unless(i == j, lambda: pb_from(i).wait_recv()))
        tmid = o.DR[:, 0, :] + (f32(o.PB[0]) + f32(o.PB[1])) + (f32(o.PB[2]) + f32(o.PB[3]))
        g_tmid, gg31 = norm_back(tmid, gain(3, 1), o.CR[:, 0, :])
        g_tb = bf16(g_tmid)
        gp_copy().wait_recv()
        o.GH[c] = bf16(f32(o.GP[...]) * nn(g_tb, w3[0]))
        gh_copy().start()
        o.keep[0] = g_tb
        o.ROWS2[:, 0, :] = jnp.concatenate([norm(tmid, gain(3, 1)), g_tmid], axis=1)

        def go(i):
            far, me, near = out_copy(i)
            when(me, lambda: near.start())
            unless(me, lambda: far.start())

        loop(8, go)
        o.gg[3] = jnp.concatenate([jnp.zeros((1, D), F32), gg31], axis=1)

    def gt_copy(i):
        s_, p_, c_ = i // 8, lax.rem(i // 2, 4), lax.rem(i, 2)
        return remote(o.ROWS.at[c_ * 16 + p_ * 4 + s_], o.GT.at[j], o.sgt.at[i], o.rgt.at[j], dev(s_, p_, c_))

    @pl.when(up_dev)
    def _():
        gh_copy().wait_recv()
        o.ROWS[:, 0, :] = nt(o.GH[c], w3[0])

        def go(i):
            when(i == lin, lambda: local(o.ROWS.at[row], o.GT.at[j], o.rgt.at[j]).start())
            unless(i == lin, lambda: gt_copy(i).start())

        loop(32, go)
        gh_sib().start()

    local(o.orow, o.orow, o.ror.at[0]).wait()
    for i in range(4):
        local(o.GT.at[i], o.GT.at[i], o.rgt.at[i]).wait()
    g_tn = (o.GT[0] + o.GT[1]) + (o.GT[2] + o.GT[3])
    g_tmid = o.orow[:, D:]
    o.dec_out[...] = o.orow[:, :D]
    decoded = o.drow[...]
    gp, gg30 = norm_back(decoded, gain(3, 0), g_tn)
    gd = bf16(g_tmid + gp)
    @pl.when(jnp.logical_not(is3 & (p == 2) & (c == 0)))
    def _():
        o.gg[3] = jnp.zeros((1, 2 * D), F32)

    o.gg[3, :, 0:D] = gg30
    g_catt = bf16(nn(jnp.broadcast_to(gd, (16, D)), W[13]))
    vv = bf16(nt(jnp.where(head_mask(16), g_catt, jnp.zeros((), BF)), W[12]))
    cp = o.cp[...]
    g_cp = nt(vv, enc[...])
    g_cs = bf16(cp * (g_cp - jnp.sum(g_cp * cp, axis=-1, keepdims=True)))
    both_l = jnp.concatenate([g_cs, bf16(cp)], axis=0)
    both_r = jnp.concatenate([bf16(f32(o.u[...]) * 0.125), vv], axis=0)
    z = o.fac[1]
    y = bf16(nn(g_cs, enc[...]) * 0.125)
    slot = iota((16, D), 0)
    gdw = jnp.broadcast_to(gd, (16, D))
    cattw = jnp.broadcast_to(catt, (16, D))
    o.fac[0] = jnp.where(slot < 12, y, gdw)
    o.fac[1] = jnp.where(slot < 12, z, jnp.where(slot == 12, g_catt, jnp.where(slot == 13, gdw, cattw)))

    def fb_copy(i):
        return remote(o.fac.at[i], o.FB.at[c, p * 4 + s], o.sfb.at[i], o.rfb.at[0], dev(2, 1 + i, c))

    for i in range(2):
        me = is2 & (p == 1 + i)
        when(me, lambda i=i: local(o.fac.at[i], o.FB.at[c, p * 4 + s], o.rfb.at[0]).start())
        unless(me, lambda i=i: fb_copy(i).start())

    def load_again(j):
        return local(w.at[:, pl.ds(j * D, D)], W.at[12 + j], o.lsem.at[j])

    when(is2 & (p == 1), lambda: others(lambda i, s_, p_: remote(o.u, o.u, o.su.at[i], o.ru.at[0], dev(s_, p_, c))))

    def gain_copy(sec, i):
        return remote(o.gg.at[sec], o.GB.at[row], o.sgb.at[sec, i], o.rgb.at[0], dev(sec, i // 2, lax.rem(i, 2)))

    def send_gain(sec):
        def go(i):
            me = (s == sec) & (i == p * 2 + c)
            when(me, lambda: local(o.gg.at[sec], o.GB.at[row], o.rgb.at[0]).start())
            unless(me, lambda: gain_copy(sec, i).start())

        loop(8, go)

    send_gain(3)

    def mine(b, k):
        return cb.at[b // 2, pl.ds(pl.multiple_of(lax.rem(b, 2) * HALF + k * R, R), R), :]

    def sib(b, slot):
        return remote(o.og.at[slot], o.sr.at[b], o.ssib.at[b], o.rsib.at[b], SIB)

    ORDER = [6, 4, 7, 5, 10, 8, 11, 9, 3, 1, 2, 0]

    def emit(b, left, right):
        n = ORDER.index(b)
        if n >= 2:
            sib(ORDER[n - 2], n % 2).wait_send()
        other = pl.ds(pl.multiple_of((1 - c) * HALF, HALF), HALF)
        own = pl.ds(pl.multiple_of(c * HALF, HALF), HALF)
        o.og[n % 2] = bf16(nn(left[other, :], right[...]))
        sib(b, n % 2).start()
        cb[b // 2, (b % 2) * HALF:(b % 2 + 1) * HALF, :] = bf16(nn(left[own, :], right[...]))

    def arrived(st):
        for q in range(4):
            sib(4 * st + q, 0).wait_recv()

    def even(k):
        return lax.rem(k, 2) == 0

    def both(k, f):
        when(even(k), lambda: f(0))
        unless(even(k), lambda: f(1))

    def diag(st, k, y):
        return remote(mine(4 * st + dg, k), o.rr.at[st, k], o.sxy.at[0, st, k], o.rrr.at[st, k], TO[Y if y else X])

    def straight(kind, st, k, y):
        return remote(mine(4 * st + (yn if y else xn), k), (o.oy if y else o.ox).at[st, k], o.sxy.at[kind, st, k],
                      (o.roy if y else o.rox).at[st, k], TO[Y if y else X])

    def first(st, k):
        for q in (dg, xn, yn, p):
            m = mine(4 * st + q, k)
            m[...] = bf16(f32(m[...]) + f32(o.sr[4 * st + q, pl.ds(pl.multiple_of(k * R, R), R), :]))

        def f(odd):
            diag(st, k, not odd).start()
            straight(1, st, k, not odd).start()

        both(k, f)

    def second(st, k):
        diag(st, k, True).wait_recv()

        def f(odd):
            m = mine(4 * st + (yn if odd else xn), k)
            m[...] = bf16(f32(m[...]) + f32(o.rr[st, k]))
            straight(2, st, k, odd).start()

        both(k, f)

    def up(st, k):
        return remote(mine(4 * st + p, k), o.zd.at[st - 1, k], o.sz.at[st, k], o.rzd.at[st, k], TO[UP])

    def down(st, k):
        return remote(mine(4 * st + p, k), o.zu.at[st, k], o.sz.at[st, k], o.rzu.at[st, k], TO[DOWN])

    def third(st, k):
        straight(1, st, k, True).wait_recv()
        straight(1, st, k, False).wait_recv()
        m = mine(4 * st + p, k)
        return m, f32(m[...]) + f32(o.ox[st, k]) + f32(o.oy[st, k])

    def out_rows(jj, half, k):
        return o.dw.at[jj, pl.ds(pl.multiple_of(half * HALF + k * R, R), R), :]

    def fin_local(b, jj, k):
        return local(mine(b, k), out_rows(jj, c, k), o.sfin.at[jj, k, 0])

    def fin_sib(b, jj, k):
        return remote(mine(b, k), out_rows(jj, c, k), o.sfin.at[jj, k, 1], o.rfin.at[jj, k, 0], SIB)

    def fin_sib_in(jj, k):
        return remote(out_rows(jj, 1 - c, k), out_rows(jj, 1 - c, k), o.sfin.at[jj, k, 1], o.rfin.at[jj, k, 0], SIB)

    def fin_y(k, cross):
        to = dev(s, yn, 1 - c) if cross else TO[Y]
        return remote(mine(p, k), out_rows(1, c, k), o.sfin.at[1, k, 1 + cross], o.rfin.at[1, k, cross], to)

    def fin_y_in(k, cross):
        half = 1 - c if cross else c
        return remote(out_rows(1, half, k), out_rows(1, half, k), o.sfin.at[1, k, 1 + cross], o.rfin.at[1, k, cross], SIB)

    def last1(st, k):
        m, total = third(st, k)

        @pl.when(is3 | is0)
        def _():
            m[...] = bf16(total)
            when(is3, lambda: down(st, k).start())
            when(is0, lambda: up(st, k).start())

        @pl.when(is2)
        def _():
            down(st, k).wait_recv()
            m[...] = bf16(total + f32(o.zu[st, k]))
            down(st, k).start()

        @pl.when(is1)
        def _():
            down(st, k).wait_recv()
            up(st, k).wait_recv()
            m[...] = bf16(total + f32(o.zu[st, k]) + f32(o.zd[st - 1, k]))
            fin_local(4 * st + p, st - 1, k).start()
            fin_sib(4 * st + p, st - 1, k).start()

    def last0(k):
        m, total = third(0, k)

        @pl.when(is3)
        def _():
            m[...] = bf16(total)
            down(0, k).start()

        @pl.when(is1 | is2)
        def _():
            down(0, k).wait_recv()
            m[...] = bf16(total + f32(o.zu[0, k]))
            down(0, k).start()

        @pl.when(is0)
        def _():
            down(0, k).wait_recv()
            m[...] = bf16(total + f32(o.zu[0, k]))

            @pl.when(p < 2)
            def _():
                fin_local(p, 0, k).start()
                fin_sib(p, 0, k).start()

            @pl.when(p >= 2)
            def _():
                fin_y(k, 0).start()
                fin_y(k, 1).start()

    lag1 = (3 - s) - 3 * ((3 - s) // 3)
    lag0 = 3 - s

    def zstep(n):
        t1 = n - lag1
        when((t1 >= 0) & (t1 < 2 * K), lambda: last1(1 + t1 // K, lax.rem(t1, K)))
        t0 = n - lag0
        when((t0 >= 2 * K) & (t0 < 3 * K), lambda: last0(t0 - 2 * K))

    def zsteps(a, b):
        loop(b, zstep, a)

    def firsts(st):
        arrived(st)
        loop(K, lambda k: first(st, k))

    def seconds(st, a, b):
        loop(b, lambda k: second(st, k), a)

    gg11 = jnp.zeros((1, D), F32)
    for t in range(4):
        rows = slice(t * 128, (t + 1) * 128)
        g_enc = f32(bf16(tn(both_l[:, rows], both_r)))
        gm, part11 = norm_back(o.mid[rows, :], gain(1, 1), g_enc)
        o.mid[rows, :] = gm
        enc[rows, :] = bf16(gm)
        gg11 = gg11 + part11
    turned(enc, T.at[0])
    turned(A.at[fnorm_], T.at[1])

    def feed_back(i, begin):
        ub, db = HID[i]

        def active(rows):
            a, slope = gelu_both(f32(B[i, rows, :]))
            A[act_, rows, :] = bf16(a)
            B[i, rows, :] = bf16(slope)

        def hidden(rows):
            B[i, rows, :] = bf16(f32(B[i, rows, :]) * nn(enc[rows, :], W[db]))

        def out(rows):
            back = nt(B[i, rows, :], W[ub])
            o.gfn[rows, :] = back if begin else o.gfn[rows, :] + back

        tiles(active, 8, 64)
        emit(db, T.at[0], A.at[act_])
        tiles(hidden)
        tiles(out)
        emit(ub, T.at[1], B.at[i])

    for i in range(2):
        for hh in range(2):
            fetch(i, hh).start()
    feed_back(0, True)
    feed_back(2, False)
    firsts(1)
    feed_back(1, False)
    seconds(1, 0, 2)
    feed_back(3, False)
    seconds(1, 2, 4)
    firsts(2)

    gg10 = jnp.zeros((1, D), F32)
    for t in range(4):
        rows = slice(t * 128, (t + 1) * 128)
        gp, part10 = norm_back(f32(A[enc0_, rows, :]), gain(1, 0), o.gfn[rows, :])
        ge0 = bf16(o.mid[rows, :] + gp)
        A[fnorm_, rows, :] = ge0
        gg10 = gg10 + part10

    def grad_attended(rows):
        B[0, rows, :] = bf16(nn(A[fnorm_, rows, :], W[3]))

    tiles(grad_attended)
    o.gg[1] = jnp.concatenate([gg10, gg11], axis=1)
    send_gain(1)
    turned(A.at[fnorm_], T.at[0])
    emit(3, T.at[0], A.at[att_])
    turned(B.at[0], T.at[1])
    turned(A.at[k_], T.at[2])
    zsteps(0, 2)
    seconds(2, 0, 1)

    lane_half = iota((L, 128), 1) // HEAD

    def attend_back(i):
        vp, qp, gp = A[v_, :, lanes(i)], A[q_, :, lanes(i)], B[0, :, lanes(i)]
        g_v = jnp.zeros((L, 128), F32)
        g_k = jnp.zeros((L, 128), F32)
        zero = jnp.zeros((), BF)
        for hh in range(2):
            fetch(i, hh).wait()
            slot = 2 * lax.rem(i, 2) + hh
            gt = padded(T.at[1], i, hh)
            kt = T[2, half_rows(i, hh), :]
            for t in range(2):
                cols = slice(t * 256, (t + 1) * 256)
                pr = o.ring[slot, :, cols]
                prf = f32(pr)
                g_p = nn(vp, gt[:, cols])
                g_s = bf16(prf * (g_p - jnp.sum(prf * g_p, axis=0, keepdims=True)))
                g_v = g_v + nn(pr, jnp.where(lane_half[cols] == hh, gp[cols], zero))
                g_k = g_k + nn(g_s, jnp.where(lane_half[cols] == hh, qp[cols], zero))
                T[0, half_rows(i, hh), cols] = bf16(nn(kt, g_s) * 0.125)
            when(i < 4, lambda: fetch(i + 2, hh).start())
        B[1, :, lanes(i)] = bf16(g_v)
        B[2, :, lanes(i)] = bf16(g_k)

    loop(2, attend_back)
    zsteps(2, 4)
    seconds(2, 1, 2)
    loop(4, attend_back, 2)
    seconds(2, 2, 3)
    zsteps(4, 5)
    loop(6, attend_back, 4)
    seconds(2, 3, 4)
    turned_back(T.at[0], B.at[3])

    def normed_again(rows):
        A[att_, rows, :] = bf16(norm(f32(A[x_, rows, :]), gain(0, 0)))

    tiles(normed_again)
    turned(A.at[att_], T.at[1])
    emit(1, T.at[1], B.at[1])
    emit(2, T.at[1], B.at[2])
    emit(0, T.at[1], B.at[3])
    firsts(0)
    gg00 = jnp.zeros((1, D), F32)

    def grad_normed(rows):
        o.gfn[rows, :] = nt(B[3, rows, :], W[0]) + nt(B[2, rows, :], W[2]) + nt(B[1, rows, :], W[1])

    tiles(grad_normed)
    for t in range(4):
        rows = slice(t * 128, (t + 1) * 128)
        gp, part00 = norm_back(f32(A[x_, rows, :]), gain(0, 0), o.gfn[rows, :])
        A[act_, rows, :] = bf16(f32(A[fnorm_, rows, :]) + gp)
        gg00 = gg00 + part00
    out_enc = local(A.at[act_], o.enc_grad, o.lsem.at[3])
    out_enc.start()
    o.gg[0] = jnp.concatenate([gg00, jnp.zeros((1, D), F32)], axis=1)
    send_gain(0)
    def sent(b, cond, link):
        when(cond, lambda: loop(K, lambda k: copy(link, b, k).wait_send()))

    @pl.when(is0)
    def _():
        @pl.when(p < 2)
        def _():
            for k in (K - 2, K - 1):
                copy(X, xb, k).wait_send()
                copy(Y, xb, k).wait_send()

        sent(xb, p >= 2, X)
        sent(xb + 2, p >= 2, X)
        sent(p, p >= 0, UP)

    def relayed(b0):
        def go(k):
            copy(Y, b0 + xn, 2 * k).wait_send()
            copy(X, b0 + yn, 2 * k + 1).wait_send()

        loop(K // 2, go)

    @pl.when(s > 0)
    def _():
        sent(p, s < 3, UP)
        sent(p, s < 4, X)
        sent(p, s < 4, Y)
        relayed(0)

    for jj in range(2):
        b = 4 * (1 + jj) + p
        sent(b, is1 | is2, UP)
        sent(b, s < 4, X)
        sent(b, s < 4, Y)
        sent(b, is1, DOWN)
        sent(4 * (1 + jj) + dg, is1, DOWN)
        when(s > 0, lambda jj=jj: relayed(4 * (1 + jj)))
    w2_sent()

    @pl.when(is2 & (p < 2))
    def _():
        load_again(0).start()
        load_again(1).start()

    zsteps(5, 7)
    seconds(0, 0, 4)

    def dw_out(jj):
        return local(W.at[4 + jj], o.dw.at[jj], o.lsem.at[4 + jj])

    def dw_done():
        dw_out(0).start()
        dw_out(1).start()

    def outer(jj, left, right):
        for t in range(3):
            cols = slice(t * 256, (t + 1) * 256)
            W[4 + jj, cols, :] = bf16(tn(left[:, cols], right))

    def both_cores(buf, left):
        for cc in range(2):
            outer(cc, left, buf[cc])
        dw_done()

    @pl.when(up_dev)
    def _():
        gh_sib().wait_send()
        pltpu.make_async_copy(o.GH.at[1 - c], o.GH.at[1 - c], o.rgh.at[1]).wait()
        both_cores(o.GH, o.keep[0])

    @pl.when(down_dev)
    def _():
        ab_sib().wait_send()
        pltpu.make_async_copy(o.AB.at[1 - c], o.AB.at[1 - c], o.ract.at[2]).wait()
        both_cores(o.AB, o.keep[0])

    factor_dev = is2 & ((p == 1) | (p == 2))

    def fs_copy():
        return remote(o.FB.at[c], o.FB.at[c], o.sfs.at[0], o.rfs.at[0], SIB)

    @pl.when(factor_dev)
    def _():
        local(o.FB.at[c], o.FB.at[c], o.rfb.at[0]).wait()
        fs_copy().start()

    def gd_copy():
        return remote(o.GD, o.GD, o.sgd.at[0], o.rgd.at[0], dev(2, 0, c))

    def gain2(slot):
        def go(i):
            when(i == p, lambda: local(o.gg.at[2], o.GB.at[slot], o.rgb.at[0]).start())
            unless(i == p, lambda: gain2_copy(slot, i).start())

        loop(4, go)

    def gain2_copy(slot, i):
        return remote(o.gg.at[2], o.GB.at[slot], o.sgb.at[2, i], o.rgb.at[0], dev(2, i, c))

    def all_factors():
        fs_copy().wait_send()
        pltpu.make_async_copy(o.FB.at[1 - c], o.FB.at[1 - c], o.rfs.at[0]).wait()
        return o.FB[...].reshape(L, D)

    @pl.when(is2 & (p == 1))
    def _():
        load_again(0).wait()
        load_again(1).wait()
        ys = all_factors()
        g_q = bf16(nn(gather16(), bf16(jnp.where(head_mask(L), nn(ys, W[13]), 0.0))))
        gp, gg21 = norm_back(o.DM[:, 0, :], gain(2, 1), nt(g_q, W[12]))
        o.GD[...] = nn(pick(13), ys) + gp
        gd_copy().start()
        o.gg[2] = jnp.concatenate([jnp.zeros((1, D), F32), gg21], axis=1)
        gain2(1)
        outer(0, o.keep[0], g_q)
        outer(1, ys, spread(o.keep[1]))
        dw_done()

    @pl.when(is2 & (p == 2))
    def _():
        zs = all_factors()
        g_ca = bf16(nn(pick(12), zs))
        outer(0, zs, spread(g_ca))
        outer(1, bf16(nn(pick(13), zs)), bf16(nn(pick(14), zs)))
        dw_done()

    zsteps(7, 11)

    def dg_copy(i, s_, p_):
        return remote(o.ROWS.at[c * 16 + p_ * 4 + s_], o.dec_grad, o.sdg.at[i], o.rdg.at[0], dev(s_, p_, c))

    @pl.when(is2 & (p == 0))
    def _():
        load_again(0).wait()
        load_again(1).wait()
        gd_copy().wait_recv()
        g_sb = bf16(o.GD[...])
        g_sv = bf16(nn(g_sb, W[13]))
        gp, gg20 = norm_back(o.DI[:, 0, :], gain(2, 0), nt(g_sv, W[12]))
        o.ROWS[:, 0, :] = o.GD[...] + gp

        def go(i, s_, p_):
            me = (s_ == s) & (p_ == p)
            when(me, lambda: local(o.ROWS.at[row], o.dec_grad, o.rdg.at[0]).start())
            unless(me, lambda: dg_copy(i, s_, p_).start())

        to_core(go)
        o.gg[2] = jnp.concatenate([gg20, jnp.zeros((1, D), F32)], axis=1)
        gain2(0)
        outer(0, o.keep[0], g_sv)
        outer(1, g_sb, o.keep[1])
        dw_done()

    zsteps(11, 15)

    @pl.when(is1)
    def _():
        def go(t):
            jj, k = t // K, lax.rem(t, K)
            b = 4 * (1 + jj) + p
            fin_local(b, jj, k).wait()
            fin_sib(b, jj, k).wait_send()
            fin_sib_in(jj, k).wait_recv()

        loop(2 * K, go)

    @pl.when(is0 & (p < 2))
    def _():
        def go(k):
            fin_local(p, 0, k).wait()
            fin_sib(p, 0, k).wait_send()
            fin_sib_in(0, k).wait_recv()
            fin_y_in(k, 0).wait_recv()
            fin_y_in(k, 1).wait_recv()

        loop(K, go)

    @pl.when(is0 & (p >= 2))
    def _():
        def go(k):
            fin_y(k, 0).wait_send()
            fin_y(k, 1).wait_send()

        loop(K, go)

    @pl.when(is3 | (is2 & (p < 3)))
    def _():
        dw_out(0).wait()
        dw_out(1).wait()

    local(o.dec_grad, o.dec_grad, o.rdg.at[0]).wait()
    out_enc.wait()

    @pl.when(s != 2)
    def _():
        local(o.GB, o.GB, o.rgb.at[0]).wait()
        o.gain_out[...] = jnp.sum(o.GB[:, 0, :], axis=0, keepdims=True)

    @pl.when(is2)
    def _():
        two = o.GB.at[pl.ds(0, 2)]
        local(two, two, o.rgb.at[0]).wait()
        o.gain_out[...] = o.GB[0] + o.GB[1]

    loop(4, lambda i: unless(i == s, lambda: remote(gains, o.gall.at[s], o.sg.at[i], o.rg.at[0], dev(i, p, c)).wait_send()))
    when(is2, lambda: loop(2, lambda i: unless((p == 0) & (i == c), lambda: remote(
        dec, o.DI.at[four], o.spre.at[i], o.rdi.at[0], dev(2, 0, i)).wait_send())))
    when(is3, lambda: loop(4, lambda i: unless((p == 2 + i // 2) & (lax.rem(i, 2) == c), lambda: remote(
        cot, o.CR.at[four], o.scr.at[i], o.rcr.at[0], dev(3, 2 + i // 2, lax.rem(i, 2))).wait_send())))

    @pl.when(is2 & (p == 0))
    def _():
        remote(o.DM, o.DM, o.sdm.at[16], o.rdm.at[1], dev(2, 1, c)).wait_send()
        others(lambda i, s_, p_: remote(o.DM.at[0], o.dmrow, o.sdm.at[i], o.rdm.at[0], dev(s_, p_, c)))
        others(dg_copy)
        loop(4, lambda i: unless(i == p, lambda: gain2_copy(0, i).wait_send()))

    @pl.when(is2 & (p == 1))
    def _():
        gd_copy().wait_send()
        loop(4, lambda i: unless(i == p, lambda: gain2_copy(1, i).wait_send()))

    loop(8, lambda i: unless(is3 & (i == p * 2 + c), lambda: remote(
        o.drow, o.DR.at[row], o.sd1.at[i], o.rdr.at[0], dev(3, i // 2, lax.rem(i, 2))).wait_send()))

    @pl.when(up_dev)
    def _():
        act_copy().wait_send()
        gp_copy().wait_send()
        loop(32, lambda i: unless(i == lin, lambda: gt_copy(i).wait_send()))

    @pl.when(down_dev)
    def _():
        gh_copy().wait_send()
        loop(4, lambda i: unless(i == j, lambda: pb_copy(i).wait_send()))

        def go(i):
            far, me, _ = out_copy(i)
            unless(me, lambda: far.wait_send())

        loop(8, go)

    for i in range(2):
        unless(is2 & (p == 1 + i), lambda i=i: fb_copy(i).wait_send())
    for sec in (0, 1, 3):
        loop(8, lambda i, sec=sec: unless((s == sec) & (i == p * 2 + c), lambda: gain_copy(sec, i).wait_send()))

    for n in (10, 11):
        sib(ORDER[n], n % 2).wait_send()

    def drain(t):
        st, k = t // K, lax.rem(t, K)
        diag(st, k, True).wait_send()
        straight(1, st, k, True).wait_send()
        straight(2, st, k, True).wait_send()
        when((st > 0) & (s != 1), lambda: down(st, k).wait_send())
        when((st == 0) & (s > 0), lambda: down(st, k).wait_send())

    loop(3 * K, drain)


OUTS = dict(dw=(2, D, D), enc_grad=(L, D), probs=(HEADS, L, L))
ROWS_OUT = dict(dec_out=(1, D), dec_grad=(1, D), gain_out=(1, 2 * D))


def fused(w, xall, dec, cot, gains, lens):
    names = [*OUTS, *ROWS_OUT, *SCRATCH, *SEMS]
    hbm, vmem = pl.BlockSpec(memory_space=pl.ANY), pl.BlockSpec(memory_space=pltpu.VMEM)
    return pl.pallas_call(
        functools.partial(kernel, names),
        out_shape=[jax.ShapeDtypeStruct(v, BF) for v in OUTS.values()] + [jax.ShapeDtypeStruct(v, F32) for v in ROWS_OUT.values()],
        in_specs=[hbm, hbm, vmem, vmem, vmem, pl.BlockSpec(memory_space=pltpu.SMEM)],
        out_specs=[hbm] * len(OUTS) + [vmem] * len(ROWS_OUT),
        scratch_shapes=[pltpu.VMEM(*v) for v in SCRATCH.values()] + [pltpu.SemaphoreType.DMA(v) for v in SEMS.values()],
        compiler_params=pltpu.CompilerParams(collective_id=0, has_side_effects=True, vmem_limit_bytes=63 << 20),
        name="fused",
    )(w, xall, dec, cot, gains, lens)


def body(enc_in, dec_in, lengths, weights, gains, dec_cot):
    s, p = lax.axis_index("section"), lax.axis_index("pair")
    pairs, dps = lax.axis_size("pair"), lax.axis_size("dp")
    lens = lax.dynamic_index_in_dim(lengths, s, 0, False)
    dw, enc_grad, _, dec_out, dec_grad, gg = fused(weights[0], enc_in, f32(dec_in), f32(dec_cot), gains.reshape(1, 2 * D), lens)
    if dps > 2:
        groups = [[i for i in range(dps) if i % 2 == c] for c in range(2)]
        dw = bf16(lax.psum(dw, "dp", axis_index_groups=groups))
        gg = lax.psum(gg, "dp", axis_index_groups=groups)
    unused = (p >= 2) & (s == 0) | (p == 3) & (s == 2)
    dw = jnp.where(unused, 0.0, f32(jnp.concatenate([dw[0], dw[1]], axis=1)))
    width = D // pairs
    gg = lax.dynamic_slice_in_dim(gg.reshape(2, D), p * width, width, 1)
    return bf16(dec_out)[None], enc_grad[None], bf16(dec_grad)[None], dw[None], gg[None]


def solution(mesh):
    rows, both = P(None, ("pair", "dp"), None), P("section", ("pair", "dp"), None)
    return jax.shard_map(
        body, mesh=mesh,
        in_specs=(rows, rows, P(None, ("pair", "dp")), P("section", None, "pair"), P("section", None, None), rows),
        out_specs=(both, both, both, P("section", None, "pair"), P("section", None, "pair")),
        check_vma=False)
```

```python
import functools

import jax
import jax.numpy as jnp
from jax import lax
from jax.experimental import pallas as pl
from jax.experimental.pallas import tpu as pltpu
from jax.sharding import PartitionSpec as P

D = 768
HALF = 384
HEADS = 12
HEAD = 64
L = 512
EPSILON = 1e-06
NEGATIVE = -1e30
K = 8
R = HALF // K
H = K // 2
LR, LD, PRE = 4, 12, 2
W2 = (4, 8, 12)
MESH = pl.DeviceIdType.MESH
X, Y, UP, DOWN = 0, 1, 2, 3
BF = jnp.bfloat16
F32 = jnp.float32


def f32(v):
    return v.astype(F32)


def bf16(v):
    return v.astype(BF)


def loop(n, go, start=0):
    def step(i, carry):
        go(i)
        return carry

    lax.fori_loop(start, n, step, 0)


def norm(v, g):
    return v * lax.rsqrt(jnp.mean(v * v, axis=-1, keepdims=True) + EPSILON) * g


def norm_back(v, g, c):
    r = lax.rsqrt(jnp.mean(v * v, axis=-1, keepdims=True) + EPSILON)
    gc = g * c
    back = r * gc - v * (r * r * r) * jnp.mean(v * gc, axis=-1, keepdims=True)
    return back, jnp.sum(r * v * c, axis=0, keepdims=True)


def gelu_both(u):
    a = 0.7978845608028654
    t = jnp.tanh(a * (u + 0.044715 * u * u * u))
    return 0.5 * u * (1.0 + t), 0.5 * (1.0 + t) + 0.5 * u * (1.0 - t * t) * a * (1.0 + 0.134145 * u * u)


def nn(a, b):
    return jnp.dot(a, b, preferred_element_type=F32)


def nt(a, b):
    return lax.dot_general(a, b, (((1,), (1,)), ((), ())), preferred_element_type=F32)


def tn(a, b):
    return lax.dot_general(a, b, (((0,), (0,)), ((), ())), preferred_element_type=F32)


def iota(shape, dim):
    return lax.broadcasted_iota(jnp.int32, shape, dim)


def head_mask(rows):
    return iota((rows, D), 1) // HEAD == lax.rem(iota((rows, D), 0), 16)


def pick(slot):
    return bf16(f32(iota((32, L), 1) == iota((32, L), 0) * 16 + slot))


def gather16():
    return bf16(f32(iota((32, L), 1) // 16 == iota((32, L), 0)))


def spread(rows):
    wide = nn(bf16(f32(iota((L, 32), 0) // 16 == iota((L, 32), 1))), rows)
    return bf16(jnp.where(head_mask(L), wide, 0.0))


SCRATCH = dict(
    W=((14, D, D), BF), cb=((6, D, D), BF), og=((2, HALF, D), BF), sr=((12, HALF, D), BF),
    rr=((3, K, R, D), BF), ox=((3, K, R, D), BF), oy=((3, K, R, D), BF), zu=((3, K, R, D), BF), zd=((2, K, R, D), BF),
    A=((8, L, D), BF), enc=((L, D), BF), B=((4, L, D), BF), T=((3, D, L), BF), mid=((L, D), F32), gfn=((L, D), F32), ring=((3, L, L), BF),
    gall=((4, 2, D), F32), dec=((8, 1, D), F32), dgrow=((1, D), F32), DI=((32, 1, D), F32), CR=((32, 1, D), F32), DM=((32, 1, D), F32), DR=((32, 1, D), F32),
    ROWS=((32, 1, D), F32), ROWS2=((32, 1, 2 * D), F32), dmrow=((1, D), F32), u=((16, D), BF), drow=((1, D), F32),
    AB=((2, 32, D), BF), GP=((32, D), BF), GH=((2, 32, D), BF), PB=((4, 32, D), BF), orow=((1, 2 * D), F32), GT=((4, 1, D), F32),
    fac=((2, 16, D), BF), FB=((2, 16, 16, D), BF), GD=((32, D), F32), GB=((32, 1, 2 * D), F32), gg=((4, 1, 2 * D), F32),
    cp=((16, L), F32), keep=((2, 32, D), BF),
)
SEMS = dict(
    ssem=(4, 4, 2, K), rsem=(16, K), csend=(16, K), crecv=(16,), lsem=(8,), psem=(4,),
    spre=(2,), rdi=(1,), scr=(4,), rcr=(1,), sg=(4,), rg=(1,), sdm=(17,), rdm=(2,), su=(16,), ru=(1,), sd1=(8,), rdr=(1,),
    sact=(3,), ract=(3,), sp=(4,), rpb=(4,), sgh=(2,), rgh=(2,), so=(16,), ror=(1,), sgt=(32,), rgt=(4,),
    sfb=(2,), rfb=(2,), sfs=(1,), rfs=(1,), sgd=(1,), rgd=(1,), sdg=(16,), rdg=(1,), sgb=(4, 8), rgb=(1,),
    ssib=(12,), rsib=(12,), sxy=(3, 3, K), sz=(3, K), rrr=(3, K), rox=(3, K), roy=(3, K), rzu=(3, K), rzd=(3, K),
    sfin=(2, K, 3), rfin=(2, K, 2),
)


class Refs:
    pass


def kernel(names, w, xall, dec8, gains, lens, *rest):
    o = Refs()
    for name, ref in zip(names, rest, strict=True):
        setattr(o, name, ref)
    s, p, d = lax.axis_index("section"), lax.axis_index("pair"), lax.axis_index("dp")
    c = lax.rem(d, 2)
    base = d - c
    xn = p + 1 - 2 * lax.rem(p, 2)
    yn = p + 2 - 4 * (p // 2)
    dg = 3 - p
    xb = lax.rem(p, 2)
    is0, is1, is2, is3 = s == 0, s == 1, s == 2, s == 3
    lin = (s * 4 + p) * 2 + c
    row = c * 16 + p * 4 + s
    W, A, B, T, cb = o.W, o.A, o.B, o.T, o.cb

    def dev(s_, p_, c_):
        return (s_, p_, base + c_)

    TO = {X: dev(s, xn, c), Y: dev(s, yn, c), UP: dev(s + 1, p, c), DOWN: dev(s - 1, p, c)}
    SIB = dev(s, p, 1 - c)

    def remote(src, dst, ss, rs, to):
        return pltpu.make_async_remote_copy(src_ref=src, dst_ref=dst, send_sem=ss, recv_sem=rs, device_id=to, device_id_type=MESH)

    def local(src, dst, sem):
        return pltpu.make_async_copy(src, dst, sem)

    def when(cond, f):
        pl.when(cond)(f)

    def unless(cond, f):
        pl.when(jnp.logical_not(cond))(f)

    own_here = (is0 & (p < 2)) | is1

    def own_block(j):
        return jnp.where(is0, p + 2 * j, jnp.where(is1, 4 * (1 + j) + p, 12 + j))

    def load_own(j):
        return local(w.at[:, pl.ds(j * D, D)], W.at[own_block(j)], o.lsem.at[j])

    def load_ws(j):
        return local(w.at[:, pl.ds(j * D, D)], cb.at[j], o.lsem.at[j])

    def load_w3():
        return local(w.at[:, pl.ds(pl.multiple_of(c * D, D), D)], cb.at[0], o.lsem.at[0])

    loads_own = own_here | (is2 & (p == 2))

    @pl.when(loads_own)
    def _():
        load_own(0).start()
        load_own(1).start()

    @pl.when(is2 & (p < 2))
    def _():
        load_ws(0).start()
        load_ws(1).start()

    when(is3, lambda: load_w3().start())
    load_x = local(xall.at[s], A.at[0], o.lsem.at[2])
    load_x.start()

    bar = pltpu.get_barrier_semaphore()

    def tell(i):
        @pl.when(i != lin)
        def _():
            pl.semaphore_signal(bar, inc=1, device_id=dev(i // 8, lax.rem(i // 2, 4), lax.rem(i, 2)), device_id_type=MESH)

    loop(32, tell)
    pl.semaphore_wait(bar, 31)

    @pl.when(loads_own)
    def _():
        load_own(0).wait()
        load_own(1).wait()

    @pl.when(is2 & (p < 2))
    def _():
        load_ws(0).wait()
        load_ws(1).wait()

    when(is3, lambda: load_w3().wait())

    def part(st, q, k):
        e = st // 3
        block = (4 * st + q) * (1 - e) + (12 + q // 2) * e
        start = c * HALF * (1 - e) + (lax.rem(q, 2) * HALF + c * (HALF // 2)) * e + k * R
        return W.at[block, pl.ds(pl.multiple_of(start, 16), R), :]

    def copy(link, st, q, k, kind=0):
        return remote(part(st, q, k), part(st, q, k), o.ssem.at[link, st, kind, k], o.rsem.at[4 * st + q, k], TO[link])

    def sibling(st, q, k):
        return remote(part(st, q, k), part(st, q, k), o.csend.at[4 * st + q, k], o.crecv.at[4 * st + q], SIB)

    def got(st, q, k):
        copy(X, st, q, k).wait_recv()
        sibling(st, q, k).start()

    @pl.when(is1)
    def _():
        loop(2 * K, lambda t: copy(DOWN, 1 + t // K, p, lax.rem(t, K)).start())
        for k in range(PRE):
            for link in (UP, X, Y):
                copy(link, 1, p, k).start()

    def relay(st, k):
        even = lax.rem(k, 2) == 0
        when(even, lambda: copy(Y, st, xn, k, 1).start())
        unless(even, lambda: copy(X, st, yn, k, 1).start())

    def over_z(st, k):
        return ((st == 1) | (st == 2)) & (lax.rem(k, 4) >= 2)

    def step0(t):
        @pl.when(t < 2 * K)
        def _():
            h, k = t // K, lax.rem(t, K)
            b = xb + 2 - 2 * h

            @pl.when(p < 2)
            def _():
                @pl.when(t > 1)
                def _():
                    h2, k2 = (t - 2) // K, lax.rem(t - 2, K)
                    copy(Y, 0, b, k2, h2).wait_send()
                    copy(X, 0, b, k2, h2).wait_send()

                copy(Y, 0, b, k, h).start()
                copy(X, 0, b, k, h).start()
                when(t < K, lambda: copy(UP, 0, p, k).start())

            @pl.when(p >= 2)
            def _():
                got(0, b, k)
                when(t < K, lambda: copy(UP, 0, p, k).start())
                copy(X, 0, b, k, h).start()

        @pl.when((t > 1) & (t < 2 * K + 2))
        def _():
            got(0, 3 - xb - 2 * ((t - 2) // K), lax.rem(t - 2, K))

        @pl.when((t >= 2 * K) & (t < 4 * K + H))
        def _():
            st, k = (t - K) // K, lax.rem(t, K)
            got(st, p, k)
            copy(X, st, p, k).start()
            copy(Y, st, p, k).start()

        @pl.when((t >= 2 * K + LR) & (t < 4 * K + H + LR))
        def _():
            st, k = (t - LR - K) // K, lax.rem(t - LR, K)
            got(st, xn, k)
            got(st, yn, k)
            when(st == 3, lambda: relay(st, k))

        @pl.when(t >= 2 * K + LD)
        def _():
            got((t - LD - K) // K, dg, lax.rem(t - LD, K))

    ROUTES = {2: [(X, 2), (X, 3), (Y, 0), (Y, 1)], 3: [(Y, 2), (Y, 3)], 0: [(X, 0), (X, 1)], 1: [(Y, 0), (X, 2), (Y, 1), (X, 3)]}

    def corner_step(corner, k):
        def go():
            for link, q in ROUTES[corner]:
                if corner != 2:
                    got(3, q, k)
                if corner == q:
                    copy(UP, 3, q, k).start()
                    copy(DOWN, 3, q, k).start()
                copy(link, 3, q, k, q % 2).start()

        when((p == corner) & (k >= 0) & (k < H), go)

    def step2(t):
        corner_step(2, t - W2[0])
        corner_step(0, t - W2[1])
        corner_step(3, t - W2[1])
        corner_step(1, t - W2[2])
        k = t - W2[2] - LR
        for corner, qs in ((3, (0, 1)), (0, (2, 3))):
            @pl.when((p == corner) & (k >= 0) & (k < H))
            def _(qs=qs):
                for q in qs:
                    got(3, q, k)

    def in_stream(t):
        return (t >= 0) & ((t < 3 * K) | ((t < 3 * K + H) & (s != 2)))

    def step1(t):
        @pl.when(in_stream(t))
        def _():
            st, k = t // K, lax.rem(t, K)
            here = is1 & ((st == 1) | (st == 2))
            unless(here, lambda: got(st, p, k))

            @pl.when(jnp.logical_not(is1 & (st == 1) & (k < PRE)))
            def _():
                when((st < 3) & (s < 3), lambda: copy(UP, st, p, k).start())
                when((st == 3) & is1, lambda: copy(DOWN, st, p, k).start())
                copy(X, st, p, k).start()
                copy(Y, st, p, k).start()

        when(is2, lambda: step2(t))

        @pl.when(in_stream(t - LR))
        def _():
            st, k = (t - LR) // K, lax.rem(t - LR, K)
            got(st, xn, k)
            got(st, yn, k)
            unless((s > 1) & over_z(st, k), lambda: relay(st, k))

        @pl.when(in_stream(t - LD))
        def _():
            st, k = (t - LD) // K, lax.rem(t - LD, K)
            got(st, dg, k)
            when(is1 & ((st == 1) | (st == 2)), lambda: copy(DOWN, st, dg, k, 1).start())
            when((is1 | is2) & over_z(st, k), lambda: copy(UP, st, dg, k, 1).start())

    def pump(a0, b0, a1, b1):
        when(is0, lambda: loop(b0, step0, a0))
        when(s > 0, lambda: loop(b1, step1, a1))

    def mine_block(b):
        return (is0 & (p < 2) & (b < 4) & (lax.rem(b, 2) == p)) | (is1 & (b >= 4) & (lax.rem(b, 4) == p))

    def ready(b):
        @pl.when(jnp.logical_not(mine_block(b)))
        def _():
            loop(K, lambda k: sibling(b // 4, b % 4, k).wait_send())
            other = W.at[b, pl.ds(pl.multiple_of((1 - c) * HALF, HALF), HALF), :]
            remote(other, other, o.csend.at[b, 0], o.crecv.at[b], SIB).wait_recv()

    def w2_ready():
        @pl.when(jnp.logical_not(is2 & (p == 2)))
        def _():
            for q in range(4):
                loop(H, lambda k, q=q: sibling(3, q, k).wait_send())
                start = pl.multiple_of((q % 2) * HALF + (1 - c) * (HALF // 2), 16)
                other = W.at[12 + q // 2, pl.ds(start, HALF // 2), :]
                remote(other, other, o.csend.at[12 + q, 0], o.crecv.at[12 + q], SIB).wait_recv()

    def drain(cond, link, st, kind, n, each=1, start=0):
        def go(i):
            copy(link, st, p, start + each * i, kind).wait_send()

        when(cond, lambda: loop(n, go))

    def weights_sent():
        always = s < 4

        @pl.when(is0)
        def _():
            @pl.when(p < 2)
            def _():
                for k in (K - 2, K - 1):
                    copy(X, 0, p, k, 1).wait_send()
                    copy(Y, 0, p, k, 1).wait_send()

            drain(p >= 2, X, 0, 0, K)
            drain(p >= 2, X, 0, 1, K)
            drain(always, UP, 0, 0, K)

        @pl.when(s > 0)
        def _():
            drain(s < 3, UP, 0, 0, K)
            drain(always, X, 0, 0, K)
            drain(always, Y, 0, 0, K)
            drain(always, Y, 0, 1, K // 2, 2, 0)
            drain(always, X, 0, 1, K // 2, 2, 1)

        for st in (1, 2):
            drain(always, X, st, 0, K)
            drain(always, Y, st, 0, K)
            drain(is1, Y, st, 1, K // 2, 2, 0)
            drain(is1, X, st, 1, K // 2, 2, 1)
            drain(s > 1, Y, st, 1, K // 4, 4, 0)
            drain(s > 1, X, st, 1, K // 4, 4, 1)
            drain(is1 | is2, UP, st, 0, K)
            drain(is1 | is2, UP, st, 1, K // 4, 4, 2)
            drain(is1 | is2, UP, st, 1, K // 4, 4, 3)
            drain(is1, DOWN, st, 0, K)
            drain(is1, DOWN, st, 1, K)

        @pl.when(s != 2)
        def _():
            drain(always, X, 3, 0, H)
            drain(always, Y, 3, 0, H)
            drain(always, Y, 3, 1, H // 2, 2, 0)
            drain(always, X, 3, 1, H // 2, 2, 1)
            drain(is1, DOWN, 3, 0, H)

        @pl.when(is2)
        def _():
            drain(always, UP, 3, 0, H)
            drain(always, DOWN, 3, 0, H)
            for corner, routes in ROUTES.items():
                for link, q in routes:
                    drain(p == corner, link, 3, q % 2, H)

    def send_gains(i):
        @pl.when(i == s)
        def _():
            local(gains, o.gall.at[s], o.rg.at[0]).start()

        unless(i == s, lambda: remote(gains, o.gall.at[s], o.sg.at[i], o.rg.at[0], dev(i, p, c)).start())

    loop(4, send_gains)
    o.dec[:, 0, :] = dec8[...]
    dec, cot = o.dec.at[pl.ds(0, 4)], o.dec.at[pl.ds(4, 4)]
    four = pl.ds(c * 16 + p * 4, 4)

    def send_dec(i):
        @pl.when((p == 0) & (i == c))
        def _():
            local(dec, o.DI.at[four], o.rdi.at[0]).start()

        unless((p == 0) & (i == c), lambda: remote(dec, o.DI.at[four], o.spre.at[i], o.rdi.at[0], dev(2, 0, i)).start())

    when(is2, lambda: loop(2, send_dec))

    def send_cot(i):
        @pl.when((p == 2 + i // 2) & (lax.rem(i, 2) == c))
        def _():
            local(cot, o.CR.at[four], o.rcr.at[0]).start()

        unless((p == 2 + i // 2) & (lax.rem(i, 2) == c),
               lambda: remote(cot, o.CR.at[four], o.scr.at[i], o.rcr.at[0], dev(3, 2 + i // 2, lax.rem(i, 2))).start())

    when(is3, lambda: loop(4, send_cot))

    def gain(sec, r):
        return o.gall[sec][r:r + 1, :]

    def to_core(f):
        loop(16, lambda i: f(i, i // 4, lax.rem(i, 4)))

    def others(f):
        to_core(lambda i, s_, p_: unless((s_ == s) & (p_ == p), lambda: f(i, s_, p_).wait_send()))

    def decoder_start0():
        local(o.DI, o.DI, o.rdi.at[0]).wait()
        rows = o.DI[:, 0, :]
        dn = bf16(norm(rows, gain(2, 0)))
        o.keep[0] = dn
        sv = bf16(nn(dn, cb[0]))
        o.keep[1] = sv
        o.DM[:, 0, :] = rows + nt(sv, cb[1])
        remote(o.DM, o.DM, o.sdm.at[16], o.rdm.at[1], dev(2, 1, c)).start()

        def go(i, s_, p_):
            me = (s_ == s) & (p_ == p)
            src = o.DM.at[c * 16 + p_ * 4 + s_]
            when(me, lambda: local(src, o.dmrow, o.rdm.at[0]).start())
            unless(me, lambda: remote(src, o.dmrow, o.sdm.at[i], o.rdm.at[0], dev(s_, p_, c)).start())

        to_core(go)

    def decoder_start1():
        remote(o.DM, o.DM, o.sdm.at[16], o.rdm.at[1], dev(2, 1, c)).wait_recv()
        cn = bf16(norm(o.DM[:, 0, :], gain(2, 1)))
        o.keep[0] = cn
        q = bf16(nn(cn, cb[0]))
        o.keep[1] = q
        cb[2, 0:L, :] = bf16(nt(spread(q), cb[1]))

        def go(i, s_, p_):
            me = (s_ == s) & (p_ == p)
            src = cb.at[2, pl.ds(pl.multiple_of((c * 16 + p_ * 4 + s_) * 16, 16), 16), :]
            when(me, lambda: local(src, o.u, o.ru.at[0]).start())
            unless(me, lambda: remote(src, o.u, o.su.at[i], o.ru.at[0], dev(s_, p_, c)).start())

        to_core(go)

    x_, q_, k_, v_, att_, enc0_, fnorm_, act_ = range(8)

    def turned(src, dst):
        for j in range(6):
            dst[j * 128:(j + 1) * 128, :] = src[:, j * 128:(j + 1) * 128].T

    def turned_back(src, dst):
        for j in range(6):
            dst[:, j * 128:(j + 1) * 128] = src[j * 128:(j + 1) * 128, :].T

    length = lens[s, 0]
    live = iota((L, 1), 0) < length

    HALVES = (slice(0, HALF), slice(HALF, D))
    QUARTERS = [slice(i * 128, (i + 1) * 128) for i in range(4)]

    def project():
        for rows in QUARTERS:
            A[act_, rows, :] = bf16(norm(f32(A[x_, rows, :]), gain(0, 0)))

        for dst, b, scale in ((q_, 0, 0.125), (v_, 1, 1.0), (k_, 2, 1.0)):
            for cols in HALVES:
                A[dst, :, cols] = bf16(f32(bf16(nn(A[act_], W[b, :, cols]))) * scale)

    def padded(ref, i, hh):
        rows = ref[pl.ds(pl.multiple_of(i * 128 + hh * 64, 64), 64), :]
        zero = jnp.zeros((64, L), BF)
        return jnp.concatenate([rows, zero] if hh == 0 else [zero, rows], axis=0)

    def lanes(i):
        return pl.ds(pl.multiple_of(i * 128, 128), 128)

    def half_rows(i, hh):
        return pl.ds(pl.multiple_of(i * 128 + hh * 64, 64), 64)

    def spill(h):
        return local(o.ring.at[lax.rem(h, 3)], o.probs.at[h], o.psem.at[lax.rem(h, 3)])

    def fetch(h):
        return local(o.probs.at[h], o.ring.at[lax.rem(h, 3)], o.psem.at[lax.rem(h, 3)])

    def attend(i):
        kp = A[k_, :, lanes(i)]
        for hh in range(2):
            head = 2 * i + hh
            when(head > 2, lambda: spill(head - 3).wait())
            sc = jnp.where(live, nn(kp, padded(T.at[0], i, hh)), NEGATIVE)
            e = jnp.exp(sc - jnp.max(sc, axis=0, keepdims=True))
            pr = bf16(e * (1.0 / jnp.sum(e, axis=0, keepdims=True)))
            o.ring[lax.rem(head, 3)] = pr
            T[2, half_rows(i, hh), :] = bf16(nn(T[1, half_rows(i, hh), :], pr))
            spill(head).start()

    def after_attention():
        for cols in HALVES:
            A[enc0_, :, cols] = bf16(f32(A[x_, :, cols]) + nt(A[att_], W[3, cols, :]))
        for rows in QUARTERS:
            e0 = f32(A[enc0_, rows, :])
            o.mid[rows, :] = e0
            A[fnorm_, rows, :] = bf16(norm(e0, gain(1, 0)))

    HID = {0: (4, 6), 1: (8, 10), 2: (5, 7), 3: (9, 11)}

    def feed(i):
        ub, db = HID[i]
        for cols in HALVES:
            h = bf16(nn(A[fnorm_], W[ub, :, cols]))
            B[i, :, cols] = h
            A[act_, :, cols] = bf16(gelu_both(f32(h))[0])
        for cols in HALVES:
            o.mid[:, cols] += nt(A[act_], W[db, cols, :])

    pump(0, 2 * K + 2, 0, K + LD)
    for b in range(4):
        ready(b)
    load_x.wait()
    local(o.gall, o.gall, o.rg.at[0]).wait()
    when(is2 & (p == 0), decoder_start0)
    project()
    pump(18, 20, 20, 21)
    turned(A.at[q_], T.at[0])
    turned(A.at[v_], T.at[1])
    pump(20, 22, 21, 22)
    when(is2 & (p == 1), decoder_start1)

    def attend_pump(i):
        attend(i)
        when(is0, lambda: loop(2, lambda t: step0(22 + 2 * i + t)))
        when((s > 0) & (i < 5), lambda: step1(22 + i))

    loop(6, attend_pump)
    for head in (9, 10, 11):
        spill(head).wait()
    turned_back(T.at[2], A.at[att_])
    after_attention()
    pump(34, 36, 27, 28)
    for b in range(4, 8):
        ready(b)
    feed(0)
    pump(36, 40, 28, 32)
    feed(2)
    pump(40, 44, 32, 36)
    for b in range(8, 12):
        ready(b)
    feed(1)
    pump(44, 46, 36, 38)
    feed(3)
    pump(46, 48, 38, 40)

    for rows in QUARTERS:
        o.enc[rows, :] = bf16(norm(o.mid[rows, :], gain(1, 1)))

    w2_ready()

    remote(o.u, o.u, o.su.at[0], o.ru.at[0], SIB).wait_recv()
    remote(o.dmrow, o.dmrow, o.sdm.at[0], o.rdm.at[0], SIB).wait_recv()
    enc = o.enc
    live_row = iota((1, L), 1) < length
    cs = jnp.where(live_row, nt(o.u[...], enc[...]) * 0.125, NEGATIVE)
    e = jnp.exp(cs - jnp.max(cs, axis=-1, keepdims=True))
    cp = e / jnp.sum(e, axis=-1, keepdims=True)
    o.cp[...] = cp
    z = bf16(nn(bf16(cp), enc[...]))
    catt = bf16(jnp.sum(jnp.where(head_mask(16), nn(z, W[12]), 0.0), axis=0, keepdims=True))
    decoded = f32(bf16(o.dmrow[...] + nt(jnp.broadcast_to(catt, (16, D)), W[13])[0:1]))
    o.drow[...] = decoded
    o.fac[1] = z

    def send_row(i):
        p_, c_ = i // 2, lax.rem(i, 2)
        me = is3 & (p_ == p) & (c_ == c)
        when(me, lambda: local(o.drow, o.DR.at[row], o.rdr.at[0]).start())
        unless(me, lambda: remote(o.drow, o.DR.at[row], o.sd1.at[i], o.rdr.at[0], dev(3, p_, c_)).start())

    loop(8, send_row)
    up_dev, down_dev = is3 & (p < 2), is3 & (p >= 2)
    j = 2 * lax.rem(p, 2) + c
    w3 = cb

    def act_copy():
        return remote(o.AB.at[c], o.AB.at[c], o.sact.at[0], o.ract.at[0], TO[Y])

    def gp_copy():
        return remote(o.GP, o.GP, o.sact.at[1], o.ract.at[1], TO[Y])

    def ab_sib():
        return remote(o.AB.at[c], o.AB.at[c], o.sact.at[2], o.ract.at[2], SIB)

    def gh_copy():
        return remote(o.GH.at[c], o.GH.at[c], o.sgh.at[0], o.rgh.at[0], TO[Y])

    def gh_sib():
        return remote(o.GH.at[c], o.GH.at[c], o.sgh.at[1], o.rgh.at[1], SIB)

    def rows_here():
        local(o.DR, o.DR, o.rdr.at[0]).wait()

    @pl.when(up_dev)
    def _():
        rows_here()
        tnorm = bf16(norm(o.DR[:, 0, :], gain(3, 0)))
        o.keep[0] = tnorm
        act, slope = gelu_both(nn(tnorm, w3[0]))
        o.AB[c] = bf16(act)
        act_copy().start()
        o.GP[...] = bf16(slope)
        gp_copy().start()

    def pb_copy(i):
        return remote(o.PB.at[j], o.PB.at[j], o.sp.at[i], o.rpb.at[j], dev(3, 2 + i // 2, lax.rem(i, 2)))

    def pb_from(i):
        return remote(o.PB.at[i], o.PB.at[i], o.sp.at[i], o.rpb.at[i], SIB)

    def out_copy(i):
        s_, p_ = i // 2, 2 * lax.rem(p, 2) + lax.rem(i, 2)
        return remote(o.ROWS2.at[c * 16 + p_ * 4 + s_], o.orow, o.so.at[i], o.ror.at[0], dev(s_, p_, c)), (s_ == s) & (p_ == p), \
            local(o.ROWS2.at[c * 16 + p_ * 4 + s_], o.orow, o.ror.at[0])

    @pl.when(down_dev)
    def _():
        act_copy().wait_recv()
        o.PB[j] = bf16(nt(o.AB[c], w3[0]))
        loop(4, lambda i: unless(i == j, lambda: pb_copy(i).start()))
        ab_sib().start()
        rows_here()
        local(o.CR, o.CR, o.rcr.at[0]).wait()
        loop(4, lambda i: unless(i == j, lambda: pb_from(i).wait_recv()))
        tmid = o.DR[:, 0, :] + (f32(o.PB[0]) + f32(o.PB[1])) + (f32(o.PB[2]) + f32(o.PB[3]))
        g_tmid, gg31 = norm_back(tmid, gain(3, 1), o.CR[:, 0, :])
        g_tb = bf16(g_tmid)
        gp_copy().wait_recv()
        o.GH[c] = bf16(f32(o.GP[...]) * nn(g_tb, w3[0]))
        gh_copy().start()
        o.keep[0] = g_tb
        o.ROWS2[:, 0, :] = jnp.concatenate([norm(tmid, gain(3, 1)), g_tmid], axis=1)

        def go(i):
            far, me, near = out_copy(i)
            when(me, lambda: near.start())
            unless(me, lambda: far.start())

        loop(8, go)
        o.gg[3] = jnp.concatenate([jnp.zeros((1, D), F32), gg31], axis=1)

    def gt_copy(i):
        s_, p_, c_ = i // 8, lax.rem(i // 2, 4), lax.rem(i, 2)
        return remote(o.ROWS.at[c_ * 16 + p_ * 4 + s_], o.GT.at[j], o.sgt.at[i], o.rgt.at[j], dev(s_, p_, c_))

    @pl.when(up_dev)
    def _():
        gh_copy().wait_recv()
        o.ROWS[:, 0, :] = nt(o.GH[c], w3[0])

        def go(i):
            when(i == lin, lambda: local(o.ROWS.at[row], o.GT.at[j], o.rgt.at[j]).start())
            unless(i == lin, lambda: gt_copy(i).start())

        loop(32, go)
        gh_sib().start()

    local(o.orow, o.orow, o.ror.at[0]).wait()
    for i in range(4):
        local(o.GT.at[i], o.GT.at[i], o.rgt.at[i]).wait()
    g_tn = (o.GT[0] + o.GT[1]) + (o.GT[2] + o.GT[3])
    g_tmid = o.orow[:, D:]
    o.dec_out[...] = bf16(o.orow[:, :D])
    decoded = o.drow[...]
    gp, gg30 = norm_back(decoded, gain(3, 0), g_tn)
    gd = bf16(g_tmid + gp)
    @pl.when(jnp.logical_not(is3 & (p == 2) & (c == 0)))
    def _():
        o.gg[3] = jnp.zeros((1, 2 * D), F32)

    o.gg[3, :, 0:D] = gg30
    g_catt = bf16(nn(jnp.broadcast_to(gd, (16, D)), W[13]))
    vv = bf16(nt(jnp.where(head_mask(16), g_catt, jnp.zeros((), BF)), W[12]))
    cp = o.cp[...]
    g_cp = nt(vv, enc[...])
    g_cs = bf16(cp * (g_cp - jnp.sum(g_cp * cp, axis=-1, keepdims=True)))
    both_l = jnp.concatenate([g_cs, bf16(cp)], axis=0)
    both_r = jnp.concatenate([bf16(f32(o.u[...]) * 0.125), vv], axis=0)
    z = o.fac[1]
    y = bf16(nn(g_cs, enc[...]) * 0.125)
    slot = iota((16, D), 0)
    gdw = jnp.broadcast_to(gd, (16, D))
    cattw = jnp.broadcast_to(catt, (16, D))
    o.fac[0] = jnp.where(slot < 12, y, gdw)
    o.fac[1] = jnp.where(slot < 12, z, jnp.where(slot == 12, g_catt, jnp.where(slot == 13, gdw, cattw)))

    def fb_copy(i):
        return remote(o.fac.at[i], o.FB.at[c, p * 4 + s], o.sfb.at[i], o.rfb.at[0], dev(2, 1 + i, c))

    for i in range(2):
        me = is2 & (p == 1 + i)
        when(me, lambda i=i: local(o.fac.at[i], o.FB.at[c, p * 4 + s], o.rfb.at[0]).start())
        unless(me, lambda i=i: fb_copy(i).start())

    def load_again(j):
        return local(w.at[:, pl.ds(j * D, D)], W.at[12 + j], o.lsem.at[j])

    when(is2 & (p == 1), lambda: others(lambda i, s_, p_: remote(o.u, o.u, o.su.at[i], o.ru.at[0], dev(s_, p_, c))))

    def gain_copy(sec, i):
        return remote(o.gg.at[sec], o.GB.at[row], o.sgb.at[sec, i], o.rgb.at[0], dev(sec, i // 2, lax.rem(i, 2)))

    def send_gain(sec):
        def go(i):
            me = (s == sec) & (i == p * 2 + c)
            when(me, lambda: local(o.gg.at[sec], o.GB.at[row], o.rgb.at[0]).start())
            unless(me, lambda: gain_copy(sec, i).start())

        loop(8, go)

    send_gain(3)

    def mine(b, k):
        return cb.at[b // 2, pl.ds(pl.multiple_of(lax.rem(b, 2) * HALF + k * R, R), R), :]

    def sib(b, slot):
        return remote(o.og.at[slot], o.sr.at[b], o.ssib.at[b], o.rsib.at[b], SIB)

    ORDER = [6, 4, 7, 5, 10, 8, 11, 9, 3, 1, 2, 0]

    def emit(b, left, right):
        n = ORDER.index(b)
        if n >= 2:
            sib(ORDER[n - 2], n % 2).wait_send()
        other = pl.ds(pl.multiple_of((1 - c) * HALF, HALF), HALF)
        own = pl.ds(pl.multiple_of(c * HALF, HALF), HALF)
        o.og[n % 2] = bf16(nn(left[other, :], right[...]))
        sib(b, n % 2).start()
        cb[b // 2, (b % 2) * HALF:(b % 2 + 1) * HALF, :] = bf16(nn(left[own, :], right[...]))

    def arrived(st):
        for q in range(4):
            sib(4 * st + q, 0).wait_recv()

    def even(k):
        return lax.rem(k, 2) == 0

    def both(k, f):
        when(even(k), lambda: f(0))
        unless(even(k), lambda: f(1))

    def diag(st, k, y):
        return remote(mine(4 * st + dg, k), o.rr.at[st, k], o.sxy.at[0, st, k], o.rrr.at[st, k], TO[Y if y else X])

    def straight(kind, st, k, y):
        return remote(mine(4 * st + (yn if y else xn), k), (o.oy if y else o.ox).at[st, k], o.sxy.at[kind, st, k],
                      (o.roy if y else o.rox).at[st, k], TO[Y if y else X])

    def first(st, k):
        for q in (dg, xn, yn, p):
            m = mine(4 * st + q, k)
            m[...] = bf16(f32(m[...]) + f32(o.sr[4 * st + q, pl.ds(pl.multiple_of(k * R, R), R), :]))

        def f(odd):
            diag(st, k, not odd).start()
            straight(1, st, k, not odd).start()

        both(k, f)

    def second(st, k):
        diag(st, k, True).wait_recv()

        def f(odd):
            m = mine(4 * st + (yn if odd else xn), k)
            m[...] = bf16(f32(m[...]) + f32(o.rr[st, k]))
            straight(2, st, k, odd).start()

        both(k, f)

    def up(st, k):
        return remote(mine(4 * st + p, k), o.zd.at[st - 1, k], o.sz.at[st, k], o.rzd.at[st, k], TO[UP])

    def down(st, k):
        return remote(mine(4 * st + p, k), o.zu.at[st, k], o.sz.at[st, k], o.rzu.at[st, k], TO[DOWN])

    def third(st, k):
        straight(1, st, k, True).wait_recv()
        straight(1, st, k, False).wait_recv()
        m = mine(4 * st + p, k)
        return m, f32(m[...]) + f32(o.ox[st, k]) + f32(o.oy[st, k])

    def out_rows(jj, half, k):
        return o.dw.at[jj, pl.ds(pl.multiple_of(half * HALF + k * R, R), R), :]

    def fin_local(b, jj, k):
        return local(mine(b, k), out_rows(jj, c, k), o.sfin.at[jj, k, 0])

    def fin_sib(b, jj, k):
        return remote(mine(b, k), out_rows(jj, c, k), o.sfin.at[jj, k, 1], o.rfin.at[jj, k, 0], SIB)

    def fin_sib_in(jj, k):
        return remote(out_rows(jj, 1 - c, k), out_rows(jj, 1 - c, k), o.sfin.at[jj, k, 1], o.rfin.at[jj, k, 0], SIB)

    def fin_y(k, cross):
        to = dev(s, yn, 1 - c) if cross else TO[Y]
        return remote(mine(p, k), out_rows(1, c, k), o.sfin.at[1, k, 1 + cross], o.rfin.at[1, k, cross], to)

    def fin_y_in(k, cross):
        half = 1 - c if cross else c
        return remote(out_rows(1, half, k), out_rows(1, half, k), o.sfin.at[1, k, 1 + cross], o.rfin.at[1, k, cross], SIB)

    def last1(st, k):
        m, total = third(st, k)

        @pl.when(is3 | is0)
        def _():
            m[...] = bf16(total)
            when(is3, lambda: down(st, k).start())
            when(is0, lambda: up(st, k).start())

        @pl.when(is2)
        def _():
            down(st, k).wait_recv()
            m[...] = bf16(total + f32(o.zu[st, k]))
            down(st, k).start()

        @pl.when(is1)
        def _():
            down(st, k).wait_recv()
            up(st, k).wait_recv()
            m[...] = bf16(total + f32(o.zu[st, k]) + f32(o.zd[st - 1, k]))
            fin_local(4 * st + p, st - 1, k).start()
            fin_sib(4 * st + p, st - 1, k).start()

    def last0(k):
        m, total = third(0, k)

        @pl.when(is3)
        def _():
            m[...] = bf16(total)
            down(0, k).start()

        @pl.when(is1 | is2)
        def _():
            down(0, k).wait_recv()
            m[...] = bf16(total + f32(o.zu[0, k]))
            down(0, k).start()

        @pl.when(is0)
        def _():
            down(0, k).wait_recv()
            m[...] = bf16(total + f32(o.zu[0, k]))

            @pl.when(p < 2)
            def _():
                fin_local(p, 0, k).start()
                fin_sib(p, 0, k).start()

            @pl.when(p >= 2)
            def _():
                fin_y(k, 0).start()
                fin_y(k, 1).start()

    lag1 = (3 - s) - 3 * ((3 - s) // 3)
    lag0 = 3 - s

    def zstep(n):
        t1 = n - lag1
        when((t1 >= 0) & (t1 < 2 * K), lambda: last1(1 + t1 // K, lax.rem(t1, K)))
        t0 = n - lag0
        when((t0 >= 2 * K) & (t0 < 3 * K), lambda: last0(t0 - 2 * K))

    L2, L3 = 2, 4

    def rstep(t, low):
        @pl.when(t < 3 * K)
        def _():
            st, k = lax.rem(t // K + 1, 3), lax.rem(t, K)
            when(k == 0, lambda: arrived(st))
            first(st, k)

        u = t - L2
        when((u >= low) & (u < 3 * K), lambda: second(lax.rem(u // K + 1, 3), lax.rem(u, K)))
        when(t - L3 >= low, lambda: zstep(t - L3))

    def rsteps(a, b, low=0):
        loop(b, lambda t: rstep(t, low), a)

    gg11 = jnp.zeros((1, D), F32)
    for rows in QUARTERS:
        g_enc = f32(bf16(tn(both_l[:, rows], both_r)))
        gm, part11 = norm_back(o.mid[rows, :], gain(1, 1), g_enc)
        o.mid[rows, :] = gm
        enc[rows, :] = bf16(gm)
        gg11 = gg11 + part11
    turned(enc, T.at[0])
    turned(A.at[fnorm_], T.at[1])

    def slopes(i):
        for cols in HALVES:
            a, slope = gelu_both(f32(B[i, :, cols]))
            A[act_, :, cols] = bf16(a)
            B[i, :, cols] = bf16(slope * nn(enc[...], W[HID[i][1], :, cols]))

    def back_out(i, begin=False):
        for cols in HALVES:
            back = nt(B[i], W[HID[i][0], cols, :])
            o.gfn[:, cols] = back if begin else o.gfn[:, cols] + back

    def emits(i):
        emit(HID[i][1], T.at[0], A.at[act_])
        emit(HID[i][0], T.at[1], B.at[i])

    for head in range(3):
        fetch(head).start()
    slopes(0)
    emits(0)
    slopes(2)
    emits(2)
    rsteps(0, 2)
    back_out(0, True)
    back_out(2)
    slopes(1)
    emits(1)
    rsteps(2, 5)
    slopes(3)
    emits(3)
    rsteps(5, 8)
    back_out(1)
    back_out(3)
    rsteps(8, 9)

    gg10 = jnp.zeros((1, D), F32)
    for rows in QUARTERS:
        gp, part10 = norm_back(f32(A[enc0_, rows, :]), gain(1, 0), o.gfn[rows, :])
        A[fnorm_, rows, :] = bf16(o.mid[rows, :] + gp)
        gg10 = gg10 + part10

    for cols in HALVES:
        B[0, :, cols] = bf16(nn(A[fnorm_], W[3, :, cols]))
    rsteps(9, 10)
    o.gg[1] = jnp.concatenate([gg10, gg11], axis=1)
    send_gain(1)
    turned(A.at[fnorm_], T.at[0])
    emit(3, T.at[0], A.at[att_])
    rsteps(10, 11)
    turned(B.at[0], T.at[1])
    turned(A.at[k_], T.at[2])
    rsteps(11, 12)

    lane_half = iota((L, 128), 1) // HEAD

    def attend_back(i):
        vp, qp, gp = A[v_, :, lanes(i)], A[q_, :, lanes(i)], B[0, :, lanes(i)]
        g_v = jnp.zeros((L, 128), F32)
        g_k = jnp.zeros((L, 128), F32)
        zero = jnp.zeros((), BF)
        for hh in range(2):
            head = 2 * i + hh
            fetch(head).wait()
            pr = o.ring[lax.rem(head, 3)]
            prf = f32(pr)
            g_p = nn(vp, padded(T.at[1], i, hh))
            g_s = bf16(prf * (g_p - jnp.sum(prf * g_p, axis=0, keepdims=True)))
            g_v = g_v + nn(pr, jnp.where(lane_half == hh, gp, zero))
            g_k = g_k + nn(g_s, jnp.where(lane_half == hh, qp, zero))
            T[0, half_rows(i, hh), :] = bf16(nn(T[2, half_rows(i, hh), :], g_s) * 0.125)
            when(head < 9, lambda: fetch(head + 3).start())
        B[1, :, lanes(i)] = bf16(g_v)
        B[2, :, lanes(i)] = bf16(g_k)

    def attend_back_step(i):
        attend_back(i)
        when(i < 4, lambda: rstep(12 + i, 0))

    loop(6, attend_back_step)
    loop(2 * K, lambda u: second(lax.rem(u // K + 1, 3), lax.rem(u, K)), 2 * K - L2)
    loop(2 * K, zstep, 2 * K - L3)
    turned_back(T.at[0], B.at[3])

    for rows in QUARTERS:
        A[att_, rows, :] = bf16(norm(f32(A[x_, rows, :]), gain(0, 0)))

    turned(A.at[att_], T.at[1])
    emit(1, T.at[1], B.at[1])
    emit(2, T.at[1], B.at[2])
    emit(0, T.at[1], B.at[3])
    rsteps(2 * K, 2 * K + 2, 2 * K)
    gg00 = jnp.zeros((1, D), F32)

    for cols in HALVES:
        o.gfn[:, cols] = nt(B[3], W[0, cols, :]) + nt(B[2], W[2, cols, :]) + nt(B[1], W[1, cols, :])
    for rows in QUARTERS:
        gp, part00 = norm_back(f32(A[x_, rows, :]), gain(0, 0), o.gfn[rows, :])
        A[act_, rows, :] = bf16(f32(A[fnorm_, rows, :]) + gp)
        gg00 = gg00 + part00
    out_enc = local(A.at[act_], o.enc_grad, o.lsem.at[3])
    out_enc.start()
    o.gg[0] = jnp.concatenate([gg00, jnp.zeros((1, D), F32)], axis=1)
    send_gain(0)
    weights_sent()

    @pl.when(is2 & (p < 2))
    def _():
        load_again(0).start()
        load_again(1).start()

    rsteps(2 * K + 2, 3 * K, 2 * K)

    def dw_out(jj):
        return local(W.at[4 + jj], o.dw.at[jj], o.lsem.at[4 + jj])

    def dw_done():
        dw_out(0).start()
        dw_out(1).start()

    def outer(jj, left, right):
        for t in range(3):
            cols = slice(t * 256, (t + 1) * 256)
            W[4 + jj, cols, :] = bf16(tn(left[:, cols], right))

    def both_cores(buf, left):
        for cc in range(2):
            outer(cc, left, buf[cc])
        dw_done()

    @pl.when(up_dev)
    def _():
        gh_sib().wait_send()
        pltpu.make_async_copy(o.GH.at[1 - c], o.GH.at[1 - c], o.rgh.at[1]).wait()
        both_cores(o.GH, o.keep[0])

    @pl.when(down_dev)
    def _():
        ab_sib().wait_send()
        pltpu.make_async_copy(o.AB.at[1 - c], o.AB.at[1 - c], o.ract.at[2]).wait()
        both_cores(o.AB, o.keep[0])

    factor_dev = is2 & ((p == 1) | (p == 2))

    def fs_copy():
        return remote(o.FB.at[c], o.FB.at[c], o.sfs.at[0], o.rfs.at[0], SIB)

    @pl.when(factor_dev)
    def _():
        local(o.FB.at[c], o.FB.at[c], o.rfb.at[0]).wait()
        fs_copy().start()

    def gd_copy():
        return remote(o.GD, o.GD, o.sgd.at[0], o.rgd.at[0], dev(2, 0, c))

    def gain2(slot):
        def go(i):
            when(i == p, lambda: local(o.gg.at[2], o.GB.at[slot], o.rgb.at[0]).start())
            unless(i == p, lambda: gain2_copy(slot, i).start())

        loop(4, go)

    def gain2_copy(slot, i):
        return remote(o.gg.at[2], o.GB.at[slot], o.sgb.at[2, i], o.rgb.at[0], dev(2, i, c))

    def all_factors():
        fs_copy().wait_send()
        pltpu.make_async_copy(o.FB.at[1 - c], o.FB.at[1 - c], o.rfs.at[0]).wait()
        return o.FB[...].reshape(L, D)

    @pl.when(is2 & (p == 1))
    def _():
        load_again(0).wait()
        load_again(1).wait()
        ys = all_factors()
        g_q = bf16(nn(gather16(), bf16(jnp.where(head_mask(L), nn(ys, W[13]), 0.0))))
        gp, gg21 = norm_back(o.DM[:, 0, :], gain(2, 1), nt(g_q, W[12]))
        o.GD[...] = nn(pick(13), ys) + gp
        gd_copy().start()
        o.gg[2] = jnp.concatenate([jnp.zeros((1, D), F32), gg21], axis=1)
        gain2(1)
        outer(0, o.keep[0], g_q)
        outer(1, ys, spread(o.keep[1]))
        dw_done()

    @pl.when(is2 & (p == 2))
    def _():
        zs = all_factors()
        g_ca = bf16(nn(pick(12), zs))
        outer(0, zs, spread(g_ca))
        outer(1, bf16(nn(pick(13), zs)), bf16(nn(pick(14), zs)))
        dw_done()

    rsteps(3 * K, 3 * K + L3, 2 * K)

    def dg_copy(i, s_, p_):
        return remote(o.ROWS.at[c * 16 + p_ * 4 + s_], o.dgrow, o.sdg.at[i], o.rdg.at[0], dev(s_, p_, c))

    @pl.when(is2 & (p == 0))
    def _():
        load_again(0).wait()
        load_again(1).wait()
        gd_copy().wait_recv()
        g_sb = bf16(o.GD[...])
        g_sv = bf16(nn(g_sb, W[13]))
        gp, gg20 = norm_back(o.DI[:, 0, :], gain(2, 0), nt(g_sv, W[12]))
        o.ROWS[:, 0, :] = o.GD[...] + gp

        def go(i, s_, p_):
            me = (s_ == s) & (p_ == p)
            when(me, lambda: local(o.ROWS.at[row], o.dgrow, o.rdg.at[0]).start())
            unless(me, lambda: dg_copy(i, s_, p_).start())

        to_core(go)
        o.gg[2] = jnp.concatenate([gg20, jnp.zeros((1, D), F32)], axis=1)
        gain2(0)
        outer(0, o.keep[0], g_sv)
        outer(1, g_sb, o.keep[1])
        dw_done()

    rsteps(3 * K + L3, 3 * K + L3 + 3, 2 * K)

    @pl.when(is1)
    def _():
        def go(t):
            jj, k = t // K, lax.rem(t, K)
            b = 4 * (1 + jj) + p
            fin_local(b, jj, k).wait()
            fin_sib(b, jj, k).wait_send()
            fin_sib_in(jj, k).wait_recv()

        loop(2 * K, go)

    @pl.when(is0 & (p < 2))
    def _():
        def go(k):
            fin_local(p, 0, k).wait()
            fin_sib(p, 0, k).wait_send()
            fin_sib_in(0, k).wait_recv()
            fin_y_in(k, 0).wait_recv()
            fin_y_in(k, 1).wait_recv()

        loop(K, go)

    @pl.when(is0 & (p >= 2))
    def _():
        def go(k):
            fin_y(k, 0).wait_send()
            fin_y(k, 1).wait_send()

        loop(K, go)

    @pl.when(is3 | (is2 & (p < 3)))
    def _():
        dw_out(0).wait()
        dw_out(1).wait()

    local(o.dgrow, o.dgrow, o.rdg.at[0]).wait()
    o.dec_grad[...] = bf16(o.dgrow[...])
    out_enc.wait()

    def share(total):
        wide = D // 4
        for i in range(4):
            @pl.when(p == i)
            def _(i=i):
                for r in range(2):
                    o.gain_out[r:r + 1, :] = total[:, r * D + i * wide:r * D + (i + 1) * wide]

    @pl.when(s != 2)
    def _():
        local(o.GB, o.GB, o.rgb.at[0]).wait()
        share(jnp.sum(o.GB[:, 0, :], axis=0, keepdims=True))

    @pl.when(is2)
    def _():
        two = o.GB.at[pl.ds(0, 2)]
        local(two, two, o.rgb.at[0]).wait()
        share(o.GB[0] + o.GB[1])

    loop(4, lambda i: unless(i == s, lambda: remote(gains, o.gall.at[s], o.sg.at[i], o.rg.at[0], dev(i, p, c)).wait_send()))
    when(is2, lambda: loop(2, lambda i: unless((p == 0) & (i == c), lambda: remote(
        dec, o.DI.at[four], o.spre.at[i], o.rdi.at[0], dev(2, 0, i)).wait_send())))
    when(is3, lambda: loop(4, lambda i: unless((p == 2 + i // 2) & (lax.rem(i, 2) == c), lambda: remote(
        cot, o.CR.at[four], o.scr.at[i], o.rcr.at[0], dev(3, 2 + i // 2, lax.rem(i, 2))).wait_send())))

    @pl.when(is2 & (p == 0))
    def _():
        remote(o.DM, o.DM, o.sdm.at[16], o.rdm.at[1], dev(2, 1, c)).wait_send()
        others(lambda i, s_, p_: remote(o.DM.at[0], o.dmrow, o.sdm.at[i], o.rdm.at[0], dev(s_, p_, c)))
        others(dg_copy)
        loop(4, lambda i: unless(i == p, lambda: gain2_copy(0, i).wait_send()))

    @pl.when(is2 & (p == 1))
    def _():
        gd_copy().wait_send()
        loop(4, lambda i: unless(i == p, lambda: gain2_copy(1, i).wait_send()))

    loop(8, lambda i: unless(is3 & (i == p * 2 + c), lambda: remote(
        o.drow, o.DR.at[row], o.sd1.at[i], o.rdr.at[0], dev(3, i // 2, lax.rem(i, 2))).wait_send()))

    @pl.when(up_dev)
    def _():
        act_copy().wait_send()
        gp_copy().wait_send()
        loop(32, lambda i: unless(i == lin, lambda: gt_copy(i).wait_send()))

    @pl.when(down_dev)
    def _():
        gh_copy().wait_send()
        loop(4, lambda i: unless(i == j, lambda: pb_copy(i).wait_send()))

        def go(i):
            far, me, _ = out_copy(i)
            unless(me, lambda: far.wait_send())

        loop(8, go)

    for i in range(2):
        unless(is2 & (p == 1 + i), lambda i=i: fb_copy(i).wait_send())
    for sec in (0, 1, 3):
        loop(8, lambda i, sec=sec: unless((s == sec) & (i == p * 2 + c), lambda: gain_copy(sec, i).wait_send()))

    for n in (10, 11):
        sib(ORDER[n], n % 2).wait_send()

    def spent(t):
        st, k = t // K, lax.rem(t, K)
        diag(st, k, True).wait_send()
        straight(1, st, k, True).wait_send()
        straight(2, st, k, True).wait_send()
        when((st > 0) & (s != 1), lambda: down(st, k).wait_send())
        when((st == 0) & (s > 0), lambda: down(st, k).wait_send())

    loop(3 * K, spent)


OUTS = dict(dw=(2, D, D), enc_grad=(L, D), probs=(HEADS, L, L))
ROWS_OUT = dict(dec_out=((1, D), BF), dec_grad=((1, D), BF), gain_out=((2, D // 4), F32))


def fused(w, xall, dec8, gains, lens):
    names = [*OUTS, *ROWS_OUT, *SCRATCH, *SEMS]
    hbm, vmem = pl.BlockSpec(memory_space=pl.ANY), pl.BlockSpec(memory_space=pltpu.VMEM)
    return pl.pallas_call(
        functools.partial(kernel, names),
        out_shape=[jax.ShapeDtypeStruct(v, BF) for v in OUTS.values()] + [jax.ShapeDtypeStruct(*v) for v in ROWS_OUT.values()],
        in_specs=[hbm, hbm, vmem, vmem, pl.BlockSpec(memory_space=pltpu.SMEM)],
        out_specs=[hbm] * len(OUTS) + [vmem] * len(ROWS_OUT),
        scratch_shapes=[pltpu.VMEM(*v) for v in SCRATCH.values()] + [pltpu.SemaphoreType.DMA(v) for v in SEMS.values()],
        compiler_params=pltpu.CompilerParams(collective_id=0, has_side_effects=True, vmem_limit_bytes=(64 << 20) - (128 << 10)),
        name="fused",
    )(w, xall, dec8, gains, lens)


def body(enc_in, dec_in, lengths, weights, gains, dec_cot):
    s, p = lax.axis_index("section"), lax.axis_index("pair")
    dps = lax.axis_size("dp")
    dec8 = f32(jnp.concatenate([dec_in, dec_cot], axis=0).reshape(8, D))
    dw, enc_grad, _, dec_out, dec_grad, gg = fused(weights[0], enc_in, dec8, gains[0], lengths)
    if dps > 2:
        groups = [[i for i in range(dps) if i % 2 == c] for c in range(2)]
        dw = bf16(lax.psum(dw, "dp", axis_index_groups=groups))
        gg = lax.psum(gg, "dp", axis_index_groups=groups)
    unused = (p >= 2) & (s == 0) | (p == 3) & (s == 2)
    dw = jnp.where(unused, 0.0, f32(jnp.concatenate([dw[0], dw[1]], axis=1)))
    return dec_out[None], enc_grad[None], dec_grad[None], dw[None], gg[None]


def solution(mesh):
    rows, both = P(None, ("pair", "dp"), None), P("section", ("pair", "dp"), None)
    return jax.shard_map(
        body, mesh=mesh,
        in_specs=(rows, rows, P(None, ("pair", "dp")), P("section", None, "pair"), P("section", None, None), rows),
        out_specs=(both, both, both, P("section", None, "pair"), P("section", None, "pair")),
        check_vma=False)
```

```python
import functools

import jax
import jax.numpy as jnp
from jax import lax
from jax.experimental import pallas as pl
from jax.experimental.pallas import tpu as pltpu
from jax.sharding import PartitionSpec as P

D = 768
HALF = 384
HEADS = 12
HEAD = 64
L = 512
EPSILON = 1e-06
NEGATIVE = -1e30
K = 8
R = HALF // K
H = K // 2
LR, LD, PRE = 4, 12, 2
W2 = (4, 8, 12)
MESH = pl.DeviceIdType.MESH
X, Y, UP, DOWN = 0, 1, 2, 3
BF = jnp.bfloat16
F32 = jnp.float32


def f32(v):
    return v.astype(F32)


def bf16(v):
    return v.astype(BF)


def loop(n, go, start=0):
    def step(i, carry):
        go(i)
        return carry

    lax.fori_loop(start, n, step, 0)


def norm(v, g):
    return v * lax.rsqrt(jnp.mean(v * v, axis=-1, keepdims=True) + EPSILON) * g


def norm_back(v, g, c):
    r = lax.rsqrt(jnp.mean(v * v, axis=-1, keepdims=True) + EPSILON)
    gc = g * c
    back = r * gc - v * (r * r * r) * jnp.mean(v * gc, axis=-1, keepdims=True)
    return back, jnp.sum(r * v * c, axis=0, keepdims=True)


def gelu_both(u):
    a = 0.7978845608028654
    t = jnp.tanh(a * (u + 0.044715 * u * u * u))
    return 0.5 * u * (1.0 + t), 0.5 * (1.0 + t) + 0.5 * u * (1.0 - t * t) * a * (1.0 + 0.134145 * u * u)


def nn(a, b):
    return jnp.dot(a, b, preferred_element_type=F32)


def nt(a, b):
    return lax.dot_general(a, b, (((1,), (1,)), ((), ())), preferred_element_type=F32)


def tn(a, b):
    return lax.dot_general(a, b, (((0,), (0,)), ((), ())), preferred_element_type=F32)


def iota(shape, dim):
    return lax.broadcasted_iota(jnp.int32, shape, dim)


def head_mask(rows):
    return iota((rows, D), 1) // HEAD == lax.rem(iota((rows, D), 0), 16)


def pick(slot):
    return bf16(f32(iota((32, L), 1) == iota((32, L), 0) * 16 + slot))


def gather16():
    return bf16(f32(iota((32, L), 1) // 16 == iota((32, L), 0)))


def spread(rows):
    wide = nn(bf16(f32(iota((L, 32), 0) // 16 == iota((L, 32), 1))), rows)
    return bf16(jnp.where(head_mask(L), wide, 0.0))


SCRATCH = dict(
    W=((14, D, D), BF), cb=((6, D, D), BF), og=((2, HALF, D), BF), sr=((12, HALF, D), BF),
    rr=((3, K, R, D), BF), ox=((3, K, R, D), BF), oy=((3, K, R, D), BF), zu=((3, K, R, D), BF), zd=((2, K, R, D), BF),
    A=((8, L, D), BF), enc=((L, D), BF), B=((4, L, D), BF), T=((3, D, L), BF), mid=((L, D), F32), gfn=((L, D), F32), ring=((3, L, L), BF),
    gall=((4, 2, D), F32), dec=((8, 1, D), F32), dgrow=((1, D), F32), DI=((32, 1, D), F32), CR=((32, 1, D), F32), DM=((32, 1, D), F32), DR=((32, 1, D), F32),
    ROWS=((32, 1, D), F32), ROWS2=((32, 1, 2 * D), F32), dmrow=((1, D), F32), u=((16, D), BF), drow=((1, D), F32),
    AB=((2, 32, D), BF), GP=((32, D), BF), GH=((2, 32, D), BF), PB=((4, 32, D), BF), orow=((1, 2 * D), F32), GT=((4, 1, D), F32),
    fac=((2, 16, D), BF), FB=((2, 16, 16, D), BF), GD=((32, D), F32), GB=((32, 1, 2 * D), F32), gg=((4, 1, 2 * D), F32),
    cp=((16, L), F32), keep=((2, 32, D), BF),
)
SEMS = dict(
    ssem=(4, 4, 2, K), rsem=(16, K), csend=(16, K), crecv=(16,), lsem=(8,), psem=(4,),
    spre=(2,), rdi=(1,), scr=(4,), rcr=(1,), sg=(4,), rg=(1,), sdm=(17,), rdm=(2,), su=(16,), ru=(1,), sd1=(8,), rdr=(1,),
    sact=(3,), ract=(3,), sp=(4,), rpb=(4,), sgh=(2,), rgh=(2,), so=(16,), ror=(1,), sgt=(32,), rgt=(4,),
    sfb=(2,), rfb=(2,), sfs=(1,), rfs=(1,), sgd=(1,), rgd=(1,), sdg=(16,), rdg=(1,), sgb=(4, 8), rgb=(1,),
    ssib=(12,), rsib=(12,), sxy=(3, 3, K), sz=(3, K), rrr=(3, K), rox=(3, K), roy=(3, K), rzu=(3, K), rzd=(3, K),
    sfin=(2, K, 3), rfin=(2, K, 2),
)


class Refs:
    pass


def kernel(names, w, xall, dec8, gains, lens, *rest):
    o = Refs()
    for name, ref in zip(names, rest, strict=True):
        setattr(o, name, ref)
    s, p, d = lax.axis_index("section"), lax.axis_index("pair"), lax.axis_index("dp")
    c = lax.rem(d, 2)
    base = d - c
    xn = p + 1 - 2 * lax.rem(p, 2)
    yn = p + 2 - 4 * (p // 2)
    dg = 3 - p
    xb = lax.rem(p, 2)
    is0, is1, is2, is3 = s == 0, s == 1, s == 2, s == 3
    lin = (s * 4 + p) * 2 + c
    row = c * 16 + p * 4 + s
    W, A, B, T, cb = o.W, o.A, o.B, o.T, o.cb

    def dev(s_, p_, c_):
        return (s_, p_, base + c_)

    TO = {X: dev(s, xn, c), Y: dev(s, yn, c), UP: dev(s + 1, p, c), DOWN: dev(s - 1, p, c)}
    SIB = dev(s, p, 1 - c)

    def remote(src, dst, ss, rs, to):
        return pltpu.make_async_remote_copy(src_ref=src, dst_ref=dst, send_sem=ss, recv_sem=rs, device_id=to, device_id_type=MESH)

    def local(src, dst, sem):
        return pltpu.make_async_copy(src, dst, sem)

    def when(cond, f):
        pl.when(cond)(f)

    def unless(cond, f):
        pl.when(jnp.logical_not(cond))(f)

    own_here = (is0 & (p < 2)) | is1

    def own_block(j):
        return jnp.where(is0, p + 2 * j, jnp.where(is1, 4 * (1 + j) + p, 12 + j))

    def load_own(j):
        return local(w.at[:, pl.ds(j * D, D)], W.at[own_block(j)], o.lsem.at[j])

    def load_ws(j):
        return local(w.at[:, pl.ds(j * D, D)], cb.at[j], o.lsem.at[j])

    def load_w3():
        return local(w.at[:, pl.ds(pl.multiple_of(c * D, D), D)], cb.at[0], o.lsem.at[0])

    loads_own = own_here | (is2 & (p == 2))

    @pl.when(loads_own)
    def _():
        load_own(0).start()
        load_own(1).start()

    @pl.when(is2 & (p < 2))
    def _():
        load_ws(0).start()
        load_ws(1).start()

    when(is3, lambda: load_w3().start())
    load_x = local(xall.at[s], A.at[0], o.lsem.at[2])
    load_x.start()

    bar = pltpu.get_barrier_semaphore()

    def tell(i):
        @pl.when(i != lin)
        def _():
            pl.semaphore_signal(bar, inc=1, device_id=dev(i // 8, lax.rem(i // 2, 4), lax.rem(i, 2)), device_id_type=MESH)

    loop(32, tell)
    pl.semaphore_wait(bar, 31)

    @pl.when(loads_own)
    def _():
        load_own(0).wait()
        load_own(1).wait()

    @pl.when(is2 & (p < 2))
    def _():
        load_ws(0).wait()
        load_ws(1).wait()

    when(is3, lambda: load_w3().wait())

    def part(st, q, k):
        e = st // 3
        block = (4 * st + q) * (1 - e) + (12 + q // 2) * e
        start = c * HALF * (1 - e) + (lax.rem(q, 2) * HALF + c * (HALF // 2)) * e + k * R
        return W.at[block, pl.ds(pl.multiple_of(start, 16), R), :]

    def copy(link, st, q, k, kind=0):
        return remote(part(st, q, k), part(st, q, k), o.ssem.at[link, st, kind, k], o.rsem.at[4 * st + q, k], TO[link])

    def sibling(st, q, k):
        return remote(part(st, q, k), part(st, q, k), o.csend.at[4 * st + q, k], o.crecv.at[4 * st + q], SIB)

    def got(st, q, k):
        copy(X, st, q, k).wait_recv()
        sibling(st, q, k).start()

    @pl.when(is1)
    def _():
        loop(2 * K, lambda t: copy(DOWN, 1 + t // K, p, lax.rem(t, K)).start())
        for k in range(PRE):
            for link in (UP, X, Y):
                copy(link, 1, p, k).start()

    def relay(st, k):
        even = lax.rem(k, 2) == 0
        when(even, lambda: copy(Y, st, xn, k, 1).start())
        unless(even, lambda: copy(X, st, yn, k, 1).start())

    def over_z(st, k):
        return ((st == 1) | (st == 2)) & (lax.rem(k, 4) >= 2)

    def step0(t):
        @pl.when(t < 2 * K)
        def _():
            h, k = t // K, lax.rem(t, K)
            b = xb + 2 - 2 * h

            @pl.when(p < 2)
            def _():
                @pl.when(t > 1)
                def _():
                    h2, k2 = (t - 2) // K, lax.rem(t - 2, K)
                    copy(Y, 0, b, k2, h2).wait_send()
                    copy(X, 0, b, k2, h2).wait_send()

                copy(Y, 0, b, k, h).start()
                copy(X, 0, b, k, h).start()
                when(t < K, lambda: copy(UP, 0, p, k).start())

            @pl.when(p >= 2)
            def _():
                got(0, b, k)
                when(t < K, lambda: copy(UP, 0, p, k).start())
                copy(X, 0, b, k, h).start()

        @pl.when((t > 1) & (t < 2 * K + 2))
        def _():
            got(0, 3 - xb - 2 * ((t - 2) // K), lax.rem(t - 2, K))

        @pl.when((t >= 2 * K) & (t < 4 * K + H))
        def _():
            st, k = (t - K) // K, lax.rem(t, K)
            got(st, p, k)
            copy(X, st, p, k).start()
            copy(Y, st, p, k).start()

        @pl.when((t >= 2 * K + LR) & (t < 4 * K + H + LR))
        def _():
            st, k = (t - LR - K) // K, lax.rem(t - LR, K)
            got(st, xn, k)
            got(st, yn, k)
            when(st == 3, lambda: relay(st, k))

        @pl.when(t >= 2 * K + LD)
        def _():
            got((t - LD - K) // K, dg, lax.rem(t - LD, K))

    ROUTES = {2: [(X, 2), (X, 3), (Y, 0), (Y, 1)], 3: [(Y, 2), (Y, 3)], 0: [(X, 0), (X, 1)], 1: [(Y, 0), (X, 2), (Y, 1), (X, 3)]}

    def corner_step(corner, k):
        def go():
            for link, q in ROUTES[corner]:
                if corner != 2:
                    got(3, q, k)
                if corner == q:
                    copy(UP, 3, q, k).start()
                    copy(DOWN, 3, q, k).start()
                copy(link, 3, q, k, q % 2).start()

        when((p == corner) & (k >= 0) & (k < H), go)

    def step2(t):
        corner_step(2, t - W2[0])
        corner_step(0, t - W2[1])
        corner_step(3, t - W2[1])
        corner_step(1, t - W2[2])
        k = t - W2[2] - LR
        for corner, qs in ((3, (0, 1)), (0, (2, 3))):
            @pl.when((p == corner) & (k >= 0) & (k < H))
            def _(qs=qs):
                for q in qs:
                    got(3, q, k)

    def in_stream(t):
        return (t >= 0) & ((t < 3 * K) | ((t < 3 * K + H) & (s != 2)))

    def step1(t):
        @pl.when(in_stream(t))
        def _():
            st, k = t // K, lax.rem(t, K)
            here = is1 & ((st == 1) | (st == 2))
            unless(here, lambda: got(st, p, k))

            @pl.when(jnp.logical_not(is1 & (st == 1) & (k < PRE)))
            def _():
                when((st < 3) & (s < 3), lambda: copy(UP, st, p, k).start())
                when((st == 3) & is1, lambda: copy(DOWN, st, p, k).start())
                copy(X, st, p, k).start()
                copy(Y, st, p, k).start()

        when(is2, lambda: step2(t))

        @pl.when(in_stream(t - LR))
        def _():
            st, k = (t - LR) // K, lax.rem(t - LR, K)
            got(st, xn, k)
            got(st, yn, k)
            unless((s > 1) & over_z(st, k), lambda: relay(st, k))

        @pl.when(in_stream(t - LD))
        def _():
            st, k = (t - LD) // K, lax.rem(t - LD, K)
            got(st, dg, k)
            when(is1 & ((st == 1) | (st == 2)), lambda: copy(DOWN, st, dg, k, 1).start())
            when((is1 | is2) & over_z(st, k), lambda: copy(UP, st, dg, k, 1).start())

    def pump(a0, b0, a1, b1):
        when(is0, lambda: loop(b0, step0, a0))
        when(s > 0, lambda: loop(b1, step1, a1))

    def mine_block(b):
        return (is0 & (p < 2) & (b < 4) & (lax.rem(b, 2) == p)) | (is1 & (b >= 4) & (lax.rem(b, 4) == p))

    def ready(b):
        @pl.when(jnp.logical_not(mine_block(b)))
        def _():
            other = W.at[b, pl.ds(pl.multiple_of((1 - c) * HALF, HALF), HALF), :]
            remote(other, other, o.csend.at[b, 0], o.crecv.at[b], SIB).wait_recv()

    def w2_ready():
        @pl.when(jnp.logical_not(is2 & (p == 2)))
        def _():
            for q in range(4):
                start = pl.multiple_of((q % 2) * HALF + (1 - c) * (HALF // 2), 16)
                other = W.at[12 + q // 2, pl.ds(start, HALF // 2), :]
                remote(other, other, o.csend.at[12 + q, 0], o.crecv.at[12 + q], SIB).wait_recv()

    def drain(cond, link, st, kind, n, each=1, start=0):
        def go(i):
            copy(link, st, p, start + each * i, kind).wait_send()

        when(cond, lambda: loop(n, go))

    def weights_sent():
        always = s < 4

        def halves(b):
            unless(mine_block(b), lambda: loop(K, lambda k: sibling(b // 4, lax.rem(b, 4), k).wait_send()))

        loop(12, halves)
        unless(is2 & (p == 2), lambda: loop(4, lambda q: loop(H, lambda k: sibling(3, q, k).wait_send())))

        @pl.when(is0)
        def _():
            @pl.when(p < 2)
            def _():
                for k in (K - 2, K - 1):
                    copy(X, 0, p, k, 1).wait_send()
                    copy(Y, 0, p, k, 1).wait_send()

            drain(p >= 2, X, 0, 0, K)
            drain(p >= 2, X, 0, 1, K)
            drain(always, UP, 0, 0, K)

        @pl.when(s > 0)
        def _():
            drain(s < 3, UP, 0, 0, K)
            drain(always, X, 0, 0, K)
            drain(always, Y, 0, 0, K)
            drain(always, Y, 0, 1, K // 2, 2, 0)
            drain(always, X, 0, 1, K // 2, 2, 1)

        for st in (1, 2):
            drain(always, X, st, 0, K)
            drain(always, Y, st, 0, K)
            drain(is1, Y, st, 1, K // 2, 2, 0)
            drain(is1, X, st, 1, K // 2, 2, 1)
            drain(s > 1, Y, st, 1, K // 4, 4, 0)
            drain(s > 1, X, st, 1, K // 4, 4, 1)
            drain(is1 | is2, UP, st, 0, K)
            drain(is1 | is2, UP, st, 1, K // 4, 4, 2)
            drain(is1 | is2, UP, st, 1, K // 4, 4, 3)
            drain(is1, DOWN, st, 0, K)
            drain(is1, DOWN, st, 1, K)

        @pl.when(s != 2)
        def _():
            drain(always, X, 3, 0, H)
            drain(always, Y, 3, 0, H)
            drain(always, Y, 3, 1, H // 2, 2, 0)
            drain(always, X, 3, 1, H // 2, 2, 1)
            drain(is1, DOWN, 3, 0, H)

        @pl.when(is2)
        def _():
            drain(always, UP, 3, 0, H)
            drain(always, DOWN, 3, 0, H)
            for corner, routes in ROUTES.items():
                for link, q in routes:
                    drain(p == corner, link, 3, q % 2, H)

    def send_gains(i):
        @pl.when(i == s)
        def _():
            local(gains, o.gall.at[s], o.rg.at[0]).start()

        unless(i == s, lambda: remote(gains, o.gall.at[s], o.sg.at[i], o.rg.at[0], dev(i, p, c)).start())

    loop(4, send_gains)
    o.dec[:, 0, :] = dec8[...]
    dec, cot = o.dec.at[pl.ds(0, 4)], o.dec.at[pl.ds(4, 4)]
    four = pl.ds(c * 16 + p * 4, 4)

    def send_dec(i):
        @pl.when((p == 0) & (i == c))
        def _():
            local(dec, o.DI.at[four], o.rdi.at[0]).start()

        unless((p == 0) & (i == c), lambda: remote(dec, o.DI.at[four], o.spre.at[i], o.rdi.at[0], dev(2, 0, i)).start())

    when(is2, lambda: loop(2, send_dec))

    def send_cot(i):
        @pl.when((p == 2 + i // 2) & (lax.rem(i, 2) == c))
        def _():
            local(cot, o.CR.at[four], o.rcr.at[0]).start()

        unless((p == 2 + i // 2) & (lax.rem(i, 2) == c),
               lambda: remote(cot, o.CR.at[four], o.scr.at[i], o.rcr.at[0], dev(3, 2 + i // 2, lax.rem(i, 2))).start())

    when(is3, lambda: loop(4, send_cot))

    def gain(sec, r):
        return o.gall[sec][r:r + 1, :]

    def to_core(f):
        loop(16, lambda i: f(i, i // 4, lax.rem(i, 4)))

    def others(f):
        to_core(lambda i, s_, p_: unless((s_ == s) & (p_ == p), lambda: f(i, s_, p_).wait_send()))

    def decoder_start0():
        local(o.DI, o.DI, o.rdi.at[0]).wait()
        rows = o.DI[:, 0, :]
        dn = bf16(norm(rows, gain(2, 0)))
        o.keep[0] = dn
        sv = bf16(nn(dn, cb[0]))
        o.keep[1] = sv
        o.DM[:, 0, :] = rows + nt(sv, cb[1])
        remote(o.DM, o.DM, o.sdm.at[16], o.rdm.at[1], dev(2, 1, c)).start()

        def go(i, s_, p_):
            me = (s_ == s) & (p_ == p)
            src = o.DM.at[c * 16 + p_ * 4 + s_]
            when(me, lambda: local(src, o.dmrow, o.rdm.at[0]).start())
            unless(me, lambda: remote(src, o.dmrow, o.sdm.at[i], o.rdm.at[0], dev(s_, p_, c)).start())

        to_core(go)

    def decoder_start1():
        remote(o.DM, o.DM, o.sdm.at[16], o.rdm.at[1], dev(2, 1, c)).wait_recv()
        cn = bf16(norm(o.DM[:, 0, :], gain(2, 1)))
        o.keep[0] = cn
        q = bf16(nn(cn, cb[0]))
        o.keep[1] = q
        cb[2, 0:L, :] = bf16(nt(spread(q), cb[1]))

        def go(i, s_, p_):
            me = (s_ == s) & (p_ == p)
            src = cb.at[2, pl.ds(pl.multiple_of((c * 16 + p_ * 4 + s_) * 16, 16), 16), :]
            when(me, lambda: local(src, o.u, o.ru.at[0]).start())
            unless(me, lambda: remote(src, o.u, o.su.at[i], o.ru.at[0], dev(s_, p_, c)).start())

        to_core(go)

    x_, q_, k_, v_, att_, enc0_, fnorm_, act_ = range(8)

    def turned(src, dst):
        for j in range(6):
            dst[j * 128:(j + 1) * 128, :] = src[:, j * 128:(j + 1) * 128].T

    def turned_back(src, dst):
        for j in range(6):
            dst[:, j * 128:(j + 1) * 128] = src[j * 128:(j + 1) * 128, :].T

    length = lens[s, 0]
    live = iota((L, 1), 0) < length

    HALVES = (slice(0, HALF), slice(HALF, D))
    QUARTERS = [slice(i * 128, (i + 1) * 128) for i in range(4)]

    def project():
        for rows in QUARTERS:
            A[act_, rows, :] = bf16(norm(f32(A[x_, rows, :]), gain(0, 0)))

        for dst, b, scale in ((q_, 0, 0.125), (v_, 1, 1.0), (k_, 2, 1.0)):
            for cols in HALVES:
                A[dst, :, cols] = bf16(f32(bf16(nn(A[act_], W[b, :, cols]))) * scale)

    def padded(ref, i, hh):
        rows = ref[pl.ds(pl.multiple_of(i * 128 + hh * 64, 64), 64), :]
        zero = jnp.zeros((64, L), BF)
        return jnp.concatenate([rows, zero] if hh == 0 else [zero, rows], axis=0)

    def lanes(i):
        return pl.ds(pl.multiple_of(i * 128, 128), 128)

    def half_rows(i, hh):
        return pl.ds(pl.multiple_of(i * 128 + hh * 64, 64), 64)

    def spill(h):
        return local(o.ring.at[lax.rem(h, 3)], o.probs.at[h], o.psem.at[lax.rem(h, 3)])

    def fetch(h):
        return local(o.probs.at[h], o.ring.at[lax.rem(h, 3)], o.psem.at[lax.rem(h, 3)])

    def attend(i):
        kp = A[k_, :, lanes(i)]
        for hh in range(2):
            head = 2 * i + hh
            when(head > 2, lambda: spill(head - 3).wait())
            sc = jnp.where(live, nn(kp, padded(T.at[0], i, hh)), NEGATIVE)
            e = jnp.exp(sc - jnp.max(sc, axis=0, keepdims=True))
            pr = bf16(e * (1.0 / jnp.sum(e, axis=0, keepdims=True)))
            o.ring[lax.rem(head, 3)] = pr
            T[2, half_rows(i, hh), :] = bf16(nn(T[1, half_rows(i, hh), :], pr))
            spill(head).start()

    def after_attention():
        for cols in HALVES:
            A[enc0_, :, cols] = bf16(f32(A[x_, :, cols]) + nt(A[att_], W[3, cols, :]))
        for rows in QUARTERS:
            e0 = f32(A[enc0_, rows, :])
            o.mid[rows, :] = e0
            A[fnorm_, rows, :] = bf16(norm(e0, gain(1, 0)))

    HID = {0: (4, 6), 1: (8, 10), 2: (5, 7), 3: (9, 11)}

    def feed(i):
        ub, db = HID[i]
        for cols in HALVES:
            h = bf16(nn(A[fnorm_], W[ub, :, cols]))
            B[i, :, cols] = h
            A[act_, :, cols] = bf16(gelu_both(f32(h))[0])
        for cols in HALVES:
            o.mid[:, cols] += nt(A[act_], W[db, cols, :])

    pump(0, 2 * K + 2, 0, K + LD)
    for b in range(4):
        ready(b)
    load_x.wait()
    local(o.gall, o.gall, o.rg.at[0]).wait()
    when(is2 & (p == 0), decoder_start0)
    project()
    pump(18, 20, 20, 21)
    turned(A.at[q_], T.at[0])
    turned(A.at[v_], T.at[1])
    pump(20, 22, 21, 22)
    when(is2 & (p == 1), decoder_start1)

    def attend_pump(i):
        attend(i)
        when(is0, lambda: loop(2, lambda t: step0(22 + 2 * i + t)))
        when((s > 0) & (i < 5), lambda: step1(22 + i))

    loop(6, attend_pump)
    for head in (9, 10, 11):
        spill(head).wait()
    turned_back(T.at[2], A.at[att_])
    after_attention()
    pump(34, 36, 27, 28)
    for b in range(4, 8):
        ready(b)
    feed(0)
    pump(36, 40, 28, 32)
    feed(2)
    pump(40, 44, 32, 36)
    for b in range(8, 12):
        ready(b)
    feed(1)
    pump(44, 46, 36, 38)
    feed(3)
    pump(46, 48, 38, 40)

    for rows in QUARTERS:
        o.enc[rows, :] = bf16(norm(o.mid[rows, :], gain(1, 1)))

    w2_ready()

    remote(o.u, o.u, o.su.at[0], o.ru.at[0], SIB).wait_recv()
    remote(o.dmrow, o.dmrow, o.sdm.at[0], o.rdm.at[0], SIB).wait_recv()
    enc = o.enc
    live_row = iota((1, L), 1) < length
    cs = jnp.where(live_row, nt(o.u[...], enc[...]) * 0.125, NEGATIVE)
    e = jnp.exp(cs - jnp.max(cs, axis=-1, keepdims=True))
    cp = e / jnp.sum(e, axis=-1, keepdims=True)
    o.cp[...] = cp
    z = bf16(nn(bf16(cp), enc[...]))
    catt = bf16(jnp.sum(jnp.where(head_mask(16), nn(z, W[12]), 0.0), axis=0, keepdims=True))
    decoded = f32(bf16(o.dmrow[...] + nt(jnp.broadcast_to(catt, (16, D)), W[13])[0:1]))
    o.drow[...] = decoded
    o.fac[1] = z

    def send_row(i):
        p_, c_ = i // 2, lax.rem(i, 2)
        me = is3 & (p_ == p) & (c_ == c)
        when(me, lambda: local(o.drow, o.DR.at[row], o.rdr.at[0]).start())
        unless(me, lambda: remote(o.drow, o.DR.at[row], o.sd1.at[i], o.rdr.at[0], dev(3, p_, c_)).start())

    loop(8, send_row)
    up_dev, down_dev = is3 & (p < 2), is3 & (p >= 2)
    j = 2 * lax.rem(p, 2) + c
    w3 = cb

    def act_copy():
        return remote(o.AB.at[c], o.AB.at[c], o.sact.at[0], o.ract.at[0], TO[Y])

    def gp_copy():
        return remote(o.GP, o.GP, o.sact.at[1], o.ract.at[1], TO[Y])

    def ab_sib():
        return remote(o.AB.at[c], o.AB.at[c], o.sact.at[2], o.ract.at[2], SIB)

    def gh_copy():
        return remote(o.GH.at[c], o.GH.at[c], o.sgh.at[0], o.rgh.at[0], TO[Y])

    def gh_sib():
        return remote(o.GH.at[c], o.GH.at[c], o.sgh.at[1], o.rgh.at[1], SIB)

    def rows_here():
        local(o.DR, o.DR, o.rdr.at[0]).wait()

    @pl.when(up_dev)
    def _():
        rows_here()
        tnorm = bf16(norm(o.DR[:, 0, :], gain(3, 0)))
        o.keep[0] = tnorm
        act, slope = gelu_both(nn(tnorm, w3[0]))
        o.AB[c] = bf16(act)
        act_copy().start()
        o.GP[...] = bf16(slope)
        gp_copy().start()

    def pb_copy(i):
        return remote(o.PB.at[j], o.PB.at[j], o.sp.at[i], o.rpb.at[j], dev(3, 2 + i // 2, lax.rem(i, 2)))

    def pb_from(i):
        return remote(o.PB.at[i], o.PB.at[i], o.sp.at[i], o.rpb.at[i], SIB)

    def out_copy(i):
        s_, p_ = i // 2, 2 * lax.rem(p, 2) + lax.rem(i, 2)
        return remote(o.ROWS2.at[c * 16 + p_ * 4 + s_], o.orow, o.so.at[i], o.ror.at[0], dev(s_, p_, c)), (s_ == s) & (p_ == p), \
            local(o.ROWS2.at[c * 16 + p_ * 4 + s_], o.orow, o.ror.at[0])

    @pl.when(down_dev)
    def _():
        act_copy().wait_recv()
        o.PB[j] = bf16(nt(o.AB[c], w3[0]))
        loop(4, lambda i: unless(i == j, lambda: pb_copy(i).start()))
        ab_sib().start()
        rows_here()
        local(o.CR, o.CR, o.rcr.at[0]).wait()
        loop(4, lambda i: unless(i == j, lambda: pb_from(i).wait_recv()))
        tmid = o.DR[:, 0, :] + (f32(o.PB[0]) + f32(o.PB[1])) + (f32(o.PB[2]) + f32(o.PB[3]))
        g_tmid, gg31 = norm_back(tmid, gain(3, 1), o.CR[:, 0, :])
        g_tb = bf16(g_tmid)
        gp_copy().wait_recv()
        o.GH[c] = bf16(f32(o.GP[...]) * nn(g_tb, w3[0]))
        gh_copy().start()
        o.keep[0] = g_tb
        o.ROWS2[:, 0, :] = jnp.concatenate([norm(tmid, gain(3, 1)), g_tmid], axis=1)

        def go(i):
            far, me, near = out_copy(i)
            when(me, lambda: near.start())
            unless(me, lambda: far.start())

        loop(8, go)
        o.gg[3] = jnp.concatenate([jnp.zeros((1, D), F32), gg31], axis=1)

    def gt_copy(i):
        s_, p_, c_ = i // 8, lax.rem(i // 2, 4), lax.rem(i, 2)
        return remote(o.ROWS.at[c_ * 16 + p_ * 4 + s_], o.GT.at[j], o.sgt.at[i], o.rgt.at[j], dev(s_, p_, c_))

    @pl.when(up_dev)
    def _():
        gh_copy().wait_recv()
        o.ROWS[:, 0, :] = nt(o.GH[c], w3[0])

        def go(i):
            when(i == lin, lambda: local(o.ROWS.at[row], o.GT.at[j], o.rgt.at[j]).start())
            unless(i == lin, lambda: gt_copy(i).start())

        loop(32, go)
        gh_sib().start()

    local(o.orow, o.orow, o.ror.at[0]).wait()
    for i in range(4):
        local(o.GT.at[i], o.GT.at[i], o.rgt.at[i]).wait()
    g_tn = (o.GT[0] + o.GT[1]) + (o.GT[2] + o.GT[3])
    g_tmid = o.orow[:, D:]
    o.dec_out[...] = bf16(o.orow[:, :D])
    decoded = o.drow[...]
    gp, gg30 = norm_back(decoded, gain(3, 0), g_tn)
    gd = bf16(g_tmid + gp)
    @pl.when(jnp.logical_not(is3 & (p == 2) & (c == 0)))
    def _():
        o.gg[3] = jnp.zeros((1, 2 * D), F32)

    o.gg[3, :, 0:D] = gg30
    g_catt = bf16(nn(jnp.broadcast_to(gd, (16, D)), W[13]))
    vv = bf16(nt(jnp.where(head_mask(16), g_catt, jnp.zeros((), BF)), W[12]))
    cp = o.cp[...]
    g_cp = nt(vv, enc[...])
    g_cs = bf16(cp * (g_cp - jnp.sum(g_cp * cp, axis=-1, keepdims=True)))
    both_l = jnp.concatenate([g_cs, bf16(cp)], axis=0)
    both_r = jnp.concatenate([bf16(f32(o.u[...]) * 0.125), vv], axis=0)
    z = o.fac[1]
    y = bf16(nn(g_cs, enc[...]) * 0.125)
    slot = iota((16, D), 0)
    gdw = jnp.broadcast_to(gd, (16, D))
    cattw = jnp.broadcast_to(catt, (16, D))
    o.fac[0] = jnp.where(slot < 12, y, gdw)
    o.fac[1] = jnp.where(slot < 12, z, jnp.where(slot == 12, g_catt, jnp.where(slot == 13, gdw, cattw)))

    def fb_copy(i):
        return remote(o.fac.at[i], o.FB.at[c, p * 4 + s], o.sfb.at[i], o.rfb.at[0], dev(2, 1 + i, c))

    for i in range(2):
        me = is2 & (p == 1 + i)
        when(me, lambda i=i: local(o.fac.at[i], o.FB.at[c, p * 4 + s], o.rfb.at[0]).start())
        unless(me, lambda i=i: fb_copy(i).start())

    def load_again(j):
        return local(w.at[:, pl.ds(j * D, D)], W.at[12 + j], o.lsem.at[j])

    when(is2 & (p == 1), lambda: others(lambda i, s_, p_: remote(o.u, o.u, o.su.at[i], o.ru.at[0], dev(s_, p_, c))))

    def gain_copy(sec, i):
        return remote(o.gg.at[sec], o.GB.at[row], o.sgb.at[sec, i], o.rgb.at[0], dev(sec, i // 2, lax.rem(i, 2)))

    def send_gain(sec):
        def go(i):
            me = (s == sec) & (i == p * 2 + c)
            when(me, lambda: local(o.gg.at[sec], o.GB.at[row], o.rgb.at[0]).start())
            unless(me, lambda: gain_copy(sec, i).start())

        loop(8, go)

    send_gain(3)

    def mine(b, k):
        return cb.at[b // 2, pl.ds(pl.multiple_of(lax.rem(b, 2) * HALF + k * R, R), R), :]

    def sib(b, slot):
        return remote(o.og.at[slot], o.sr.at[b], o.ssib.at[b], o.rsib.at[b], SIB)

    ORDER = [6, 4, 7, 5, 10, 8, 11, 9, 3, 1, 2, 0]

    def emit(b, left, right):
        n = ORDER.index(b)
        if n >= 2:
            sib(ORDER[n - 2], n % 2).wait_send()
        other = pl.ds(pl.multiple_of((1 - c) * HALF, HALF), HALF)
        own = pl.ds(pl.multiple_of(c * HALF, HALF), HALF)
        o.og[n % 2] = bf16(nn(left[other, :], right[...]))
        sib(b, n % 2).start()
        cb[b // 2, (b % 2) * HALF:(b % 2 + 1) * HALF, :] = bf16(nn(left[own, :], right[...]))

    def arrived(st):
        for q in range(4):
            sib(4 * st + q, 0).wait_recv()

    def even(k):
        return lax.rem(k, 2) == 0

    def both(k, f):
        when(even(k), lambda: f(0))
        unless(even(k), lambda: f(1))

    def diag(st, k, y):
        return remote(mine(4 * st + dg, k), o.rr.at[st, k], o.sxy.at[0, st, k], o.rrr.at[st, k], TO[Y if y else X])

    def straight(kind, st, k, y):
        return remote(mine(4 * st + (yn if y else xn), k), (o.oy if y else o.ox).at[st, k], o.sxy.at[kind, st, k],
                      (o.roy if y else o.rox).at[st, k], TO[Y if y else X])

    def first(st, k):
        for q in (dg, xn, yn, p):
            m = mine(4 * st + q, k)
            m[...] = bf16(f32(m[...]) + f32(o.sr[4 * st + q, pl.ds(pl.multiple_of(k * R, R), R), :]))

        def f(odd):
            diag(st, k, not odd).start()
            straight(1, st, k, not odd).start()

        both(k, f)

    def second(st, k):
        diag(st, k, True).wait_recv()

        def f(odd):
            m = mine(4 * st + (yn if odd else xn), k)
            m[...] = bf16(f32(m[...]) + f32(o.rr[st, k]))
            straight(2, st, k, odd).start()

        both(k, f)

    def up(st, k):
        return remote(mine(4 * st + p, k), o.zd.at[st - 1, k], o.sz.at[st, k], o.rzd.at[st, k], TO[UP])

    def down(st, k):
        return remote(mine(4 * st + p, k), o.zu.at[st, k], o.sz.at[st, k], o.rzu.at[st, k], TO[DOWN])

    def third(st, k):
        straight(1, st, k, True).wait_recv()
        straight(1, st, k, False).wait_recv()
        m = mine(4 * st + p, k)
        return m, f32(m[...]) + f32(o.ox[st, k]) + f32(o.oy[st, k])

    def out_rows(jj, half, k):
        return o.dw.at[jj, pl.ds(pl.multiple_of(half * HALF + k * R, R), R), :]

    def fin_local(b, jj, k):
        return local(mine(b, k), out_rows(jj, c, k), o.sfin.at[jj, k, 0])

    def fin_sib(b, jj, k):
        return remote(mine(b, k), out_rows(jj, c, k), o.sfin.at[jj, k, 1], o.rfin.at[jj, k, 0], SIB)

    def fin_sib_in(jj, k):
        return remote(out_rows(jj, 1 - c, k), out_rows(jj, 1 - c, k), o.sfin.at[jj, k, 1], o.rfin.at[jj, k, 0], SIB)

    def fin_y(k, cross):
        to = dev(s, yn, 1 - c) if cross else TO[Y]
        return remote(mine(p, k), out_rows(1, c, k), o.sfin.at[1, k, 1 + cross], o.rfin.at[1, k, cross], to)

    def fin_y_in(k, cross):
        half = 1 - c if cross else c
        return remote(out_rows(1, half, k), out_rows(1, half, k), o.sfin.at[1, k, 1 + cross], o.rfin.at[1, k, cross], SIB)

    def last1(st, k):
        m, total = third(st, k)

        @pl.when(is3 | is0)
        def _():
            m[...] = bf16(total)
            when(is3, lambda: down(st, k).start())
            when(is0, lambda: up(st, k).start())

        @pl.when(is2)
        def _():
            down(st, k).wait_recv()
            m[...] = bf16(total + f32(o.zu[st, k]))
            down(st, k).start()

        @pl.when(is1)
        def _():
            down(st, k).wait_recv()
            up(st, k).wait_recv()
            m[...] = bf16(total + f32(o.zu[st, k]) + f32(o.zd[st - 1, k]))
            fin_local(4 * st + p, st - 1, k).start()
            fin_sib(4 * st + p, st - 1, k).start()

    def last0(k):
        m, total = third(0, k)

        @pl.when(is3)
        def _():
            m[...] = bf16(total)
            down(0, k).start()

        @pl.when(is1 | is2)
        def _():
            down(0, k).wait_recv()
            m[...] = bf16(total + f32(o.zu[0, k]))
            down(0, k).start()

        @pl.when(is0)
        def _():
            down(0, k).wait_recv()
            m[...] = bf16(total + f32(o.zu[0, k]))

            @pl.when(p < 2)
            def _():
                fin_local(p, 0, k).start()
                fin_sib(p, 0, k).start()

            @pl.when(p >= 2)
            def _():
                fin_y(k, 0).start()
                fin_y(k, 1).start()

    lag1 = (3 - s) - 3 * ((3 - s) // 3)
    lag0 = 3 - s

    N2 = 6

    def item(t):
        st = jnp.where(t < K, 1, jnp.where((t >= K + N2) & (t < 2 * K + N2), 0, 2))
        k = t - jnp.where(t < K, 0, jnp.where(t < K + N2, K, jnp.where(t < 2 * K + N2, K + N2, 2 * K)))
        return st, k

    def zstep(n):
        t1 = n - lag1
        st1, k1 = item(t1)
        when((t1 >= 0) & (t1 < 3 * K) & (st1 > 0), lambda: last1(st1, k1))
        t0 = n - lag0
        st0, k0 = item(t0)
        when((t0 >= 0) & (t0 < 3 * K) & (st0 == 0), lambda: last0(k0))

    L2, L3 = 2, 5

    def rstep(t):
        @pl.when(t < 3 * K)
        def _():
            st, k = item(t)
            when(k == 0, lambda: arrived(st))
            first(st, k)

        u = t - L2
        when((u >= 0) & (u < 3 * K), lambda: second(*item(u)))
        when(t >= L3, lambda: zstep(t - L3))

    def rsteps(a, b):
        loop(b, rstep, a)

    gg11 = jnp.zeros((1, D), F32)
    for rows in QUARTERS:
        g_enc = f32(bf16(tn(both_l[:, rows], both_r)))
        gm, part11 = norm_back(o.mid[rows, :], gain(1, 1), g_enc)
        o.mid[rows, :] = gm
        enc[rows, :] = bf16(gm)
        gg11 = gg11 + part11
    turned(enc, T.at[0])
    turned(A.at[fnorm_], T.at[1])

    def slopes(i):
        for cols in HALVES:
            a, slope = gelu_both(f32(B[i, :, cols]))
            A[act_, :, cols] = bf16(a)
            B[i, :, cols] = bf16(slope * nn(enc[...], W[HID[i][1], :, cols]))

    def back_out(i, begin=False):
        for cols in HALVES:
            back = nt(B[i], W[HID[i][0], cols, :])
            o.gfn[:, cols] = back if begin else o.gfn[:, cols] + back

    def emits(i):
        emit(HID[i][1], T.at[0], A.at[act_])
        emit(HID[i][0], T.at[1], B.at[i])

    for head in range(3):
        fetch(head).start()
    slopes(0)
    emits(0)
    slopes(2)
    emits(2)
    rsteps(0, 2)
    slopes(1)
    emits(1)
    rsteps(2, 4)
    slopes(3)
    emits(3)
    rsteps(4, 5)
    back_out(0, True)
    back_out(2)
    rsteps(5, 6)
    back_out(1)
    back_out(3)

    gg10 = jnp.zeros((1, D), F32)
    for rows in QUARTERS:
        gp, part10 = norm_back(f32(A[enc0_, rows, :]), gain(1, 0), o.gfn[rows, :])
        A[fnorm_, rows, :] = bf16(o.mid[rows, :] + gp)
        gg10 = gg10 + part10

    for cols in HALVES:
        B[0, :, cols] = bf16(nn(A[fnorm_], W[3, :, cols]))
    rsteps(6, 7)
    o.gg[1] = jnp.concatenate([gg10, gg11], axis=1)
    send_gain(1)
    turned(A.at[fnorm_], T.at[0])
    emit(3, T.at[0], A.at[att_])
    turned(B.at[0], T.at[1])
    turned(A.at[k_], T.at[2])
    rsteps(7, 8)

    lane_half = iota((L, 128), 1) // HEAD

    def attend_back(i):
        vp, qp, gp = A[v_, :, lanes(i)], A[q_, :, lanes(i)], B[0, :, lanes(i)]
        g_v = jnp.zeros((L, 128), F32)
        g_k = jnp.zeros((L, 128), F32)
        zero = jnp.zeros((), BF)
        for hh in range(2):
            head = 2 * i + hh
            fetch(head).wait()
            pr = o.ring[lax.rem(head, 3)]
            prf = f32(pr)
            g_p = nn(vp, padded(T.at[1], i, hh))
            g_s = bf16(prf * (g_p - jnp.sum(prf * g_p, axis=0, keepdims=True)))
            g_v = g_v + nn(pr, jnp.where(lane_half == hh, gp, zero))
            g_k = g_k + nn(g_s, jnp.where(lane_half == hh, qp, zero))
            T[0, half_rows(i, hh), :] = bf16(nn(T[2, half_rows(i, hh), :], g_s) * 0.125)
            when(head < 9, lambda: fetch(head + 3).start())
        B[1, :, lanes(i)] = bf16(g_v)
        B[2, :, lanes(i)] = bf16(g_k)

    def attend_back_step(i):
        attend_back(i)
        rstep(8 + i)

    loop(6, attend_back_step)
    turned_back(T.at[0], B.at[3])

    for rows in QUARTERS:
        A[att_, rows, :] = bf16(norm(f32(A[x_, rows, :]), gain(0, 0)))

    turned(A.at[att_], T.at[1])
    emit(1, T.at[1], B.at[1])
    emit(2, T.at[1], B.at[2])
    emit(0, T.at[1], B.at[3])
    rsteps(K + N2, K + N2 + 4)
    gg00 = jnp.zeros((1, D), F32)

    for cols in HALVES:
        o.gfn[:, cols] = nt(B[3], W[0, cols, :]) + nt(B[2], W[2, cols, :]) + nt(B[1], W[1, cols, :])
    for rows in QUARTERS:
        gp, part00 = norm_back(f32(A[x_, rows, :]), gain(0, 0), o.gfn[rows, :])
        A[act_, rows, :] = bf16(f32(A[fnorm_, rows, :]) + gp)
        gg00 = gg00 + part00
    out_enc = local(A.at[act_], o.enc_grad, o.lsem.at[3])
    out_enc.start()
    o.gg[0] = jnp.concatenate([gg00, jnp.zeros((1, D), F32)], axis=1)
    send_gain(0)
    rsteps(K + N2 + 4, 3 * K + L3 + 3)
    weights_sent()

    @pl.when(is2 & (p < 2))
    def _():
        load_again(0).start()
        load_again(1).start()

    def dw_out(jj):
        return local(W.at[4 + jj], o.dw.at[jj], o.lsem.at[4 + jj])

    def dw_done():
        dw_out(0).start()
        dw_out(1).start()

    def outer(jj, left, right):
        for t in range(3):
            cols = slice(t * 256, (t + 1) * 256)
            W[4 + jj, cols, :] = bf16(tn(left[:, cols], right))

    def both_cores(buf, left):
        for cc in range(2):
            outer(cc, left, buf[cc])
        dw_done()

    @pl.when(up_dev)
    def _():
        gh_sib().wait_send()
        pltpu.make_async_copy(o.GH.at[1 - c], o.GH.at[1 - c], o.rgh.at[1]).wait()
        both_cores(o.GH, o.keep[0])

    @pl.when(down_dev)
    def _():
        ab_sib().wait_send()
        pltpu.make_async_copy(o.AB.at[1 - c], o.AB.at[1 - c], o.ract.at[2]).wait()
        both_cores(o.AB, o.keep[0])

    factor_dev = is2 & ((p == 1) | (p == 2))

    def fs_copy():
        return remote(o.FB.at[c], o.FB.at[c], o.sfs.at[0], o.rfs.at[0], SIB)

    @pl.when(factor_dev)
    def _():
        local(o.FB.at[c], o.FB.at[c], o.rfb.at[0]).wait()
        fs_copy().start()

    def gd_copy():
        return remote(o.GD, o.GD, o.sgd.at[0], o.rgd.at[0], dev(2, 0, c))

    def gain2(slot):
        def go(i):
            when(i == p, lambda: local(o.gg.at[2], o.GB.at[slot], o.rgb.at[0]).start())
            unless(i == p, lambda: gain2_copy(slot, i).start())

        loop(4, go)

    def gain2_copy(slot, i):
        return remote(o.gg.at[2], o.GB.at[slot], o.sgb.at[2, i], o.rgb.at[0], dev(2, i, c))

    def all_factors():
        fs_copy().wait_send()
        pltpu.make_async_copy(o.FB.at[1 - c], o.FB.at[1 - c], o.rfs.at[0]).wait()
        return o.FB[...].reshape(L, D)

    @pl.when(is2 & (p == 1))
    def _():
        load_again(0).wait()
        load_again(1).wait()
        ys = all_factors()
        g_q = bf16(nn(gather16(), bf16(jnp.where(head_mask(L), nn(ys, W[13]), 0.0))))
        gp, gg21 = norm_back(o.DM[:, 0, :], gain(2, 1), nt(g_q, W[12]))
        o.GD[...] = nn(pick(13), ys) + gp
        gd_copy().start()
        o.gg[2] = jnp.concatenate([jnp.zeros((1, D), F32), gg21], axis=1)
        gain2(1)
        outer(0, o.keep[0], g_q)
        outer(1, ys, spread(o.keep[1]))
        dw_done()

    @pl.when(is2 & (p == 2))
    def _():
        zs = all_factors()
        g_ca = bf16(nn(pick(12), zs))
        outer(0, zs, spread(g_ca))
        outer(1, bf16(nn(pick(13), zs)), bf16(nn(pick(14), zs)))
        dw_done()


    def dg_copy(i, s_, p_):
        return remote(o.ROWS.at[c * 16 + p_ * 4 + s_], o.dgrow, o.sdg.at[i], o.rdg.at[0], dev(s_, p_, c))

    @pl.when(is2 & (p == 0))
    def _():
        load_again(0).wait()
        load_again(1).wait()
        gd_copy().wait_recv()
        g_sb = bf16(o.GD[...])
        g_sv = bf16(nn(g_sb, W[13]))
        gp, gg20 = norm_back(o.DI[:, 0, :], gain(2, 0), nt(g_sv, W[12]))
        o.ROWS[:, 0, :] = o.GD[...] + gp

        def go(i, s_, p_):
            me = (s_ == s) & (p_ == p)
            when(me, lambda: local(o.ROWS.at[row], o.dgrow, o.rdg.at[0]).start())
            unless(me, lambda: dg_copy(i, s_, p_).start())

        to_core(go)
        o.gg[2] = jnp.concatenate([gg20, jnp.zeros((1, D), F32)], axis=1)
        gain2(0)
        outer(0, o.keep[0], g_sv)
        outer(1, g_sb, o.keep[1])
        dw_done()


    @pl.when(is1)
    def _():
        def go(t):
            jj, k = t // K, lax.rem(t, K)
            b = 4 * (1 + jj) + p
            fin_local(b, jj, k).wait()
            fin_sib(b, jj, k).wait_send()
            fin_sib_in(jj, k).wait_recv()

        loop(2 * K, go)

    @pl.when(is0 & (p < 2))
    def _():
        def go(k):
            fin_local(p, 0, k).wait()
            fin_sib(p, 0, k).wait_send()
            fin_sib_in(0, k).wait_recv()
            fin_y_in(k, 0).wait_recv()
            fin_y_in(k, 1).wait_recv()

        loop(K, go)

    @pl.when(is0 & (p >= 2))
    def _():
        def go(k):
            fin_y(k, 0).wait_send()
            fin_y(k, 1).wait_send()

        loop(K, go)

    @pl.when(is3 | (is2 & (p < 3)))
    def _():
        dw_out(0).wait()
        dw_out(1).wait()

    local(o.dgrow, o.dgrow, o.rdg.at[0]).wait()
    o.dec_grad[...] = bf16(o.dgrow[...])
    out_enc.wait()

    def share(total):
        wide = D // 4
        for i in range(4):
            @pl.when(p == i)
            def _(i=i):
                for r in range(2):
                    o.gain_out[r:r + 1, :] = total[:, r * D + i * wide:r * D + (i + 1) * wide]

    @pl.when(s != 2)
    def _():
        local(o.GB, o.GB, o.rgb.at[0]).wait()
        share(jnp.sum(o.GB[:, 0, :], axis=0, keepdims=True))

    @pl.when(is2)
    def _():
        two = o.GB.at[pl.ds(0, 2)]
        local(two, two, o.rgb.at[0]).wait()
        share(o.GB[0] + o.GB[1])

    loop(4, lambda i: unless(i == s, lambda: remote(gains, o.gall.at[s], o.sg.at[i], o.rg.at[0], dev(i, p, c)).wait_send()))
    when(is2, lambda: loop(2, lambda i: unless((p == 0) & (i == c), lambda: remote(
        dec, o.DI.at[four], o.spre.at[i], o.rdi.at[0], dev(2, 0, i)).wait_send())))
    when(is3, lambda: loop(4, lambda i: unless((p == 2 + i // 2) & (lax.rem(i, 2) == c), lambda: remote(
        cot, o.CR.at[four], o.scr.at[i], o.rcr.at[0], dev(3, 2 + i // 2, lax.rem(i, 2))).wait_send())))

    @pl.when(is2 & (p == 0))
    def _():
        remote(o.DM, o.DM, o.sdm.at[16], o.rdm.at[1], dev(2, 1, c)).wait_send()
        others(lambda i, s_, p_: remote(o.DM.at[0], o.dmrow, o.sdm.at[i], o.rdm.at[0], dev(s_, p_, c)))
        others(dg_copy)
        loop(4, lambda i: unless(i == p, lambda: gain2_copy(0, i).wait_send()))

    @pl.when(is2 & (p == 1))
    def _():
        gd_copy().wait_send()
        loop(4, lambda i: unless(i == p, lambda: gain2_copy(1, i).wait_send()))

    loop(8, lambda i: unless(is3 & (i == p * 2 + c), lambda: remote(
        o.drow, o.DR.at[row], o.sd1.at[i], o.rdr.at[0], dev(3, i // 2, lax.rem(i, 2))).wait_send()))

    @pl.when(up_dev)
    def _():
        act_copy().wait_send()
        gp_copy().wait_send()
        loop(32, lambda i: unless(i == lin, lambda: gt_copy(i).wait_send()))

    @pl.when(down_dev)
    def _():
        gh_copy().wait_send()
        loop(4, lambda i: unless(i == j, lambda: pb_copy(i).wait_send()))

        def go(i):
            far, me, _ = out_copy(i)
            unless(me, lambda: far.wait_send())

        loop(8, go)

    for i in range(2):
        unless(is2 & (p == 1 + i), lambda i=i: fb_copy(i).wait_send())
    for sec in (0, 1, 3):
        loop(8, lambda i, sec=sec: unless((s == sec) & (i == p * 2 + c), lambda: gain_copy(sec, i).wait_send()))

    for n in (10, 11):
        sib(ORDER[n], n % 2).wait_send()

    def spent(t):
        st, k = t // K, lax.rem(t, K)
        diag(st, k, True).wait_send()
        straight(1, st, k, True).wait_send()
        straight(2, st, k, True).wait_send()
        when((st > 0) & (s != 1), lambda: down(st, k).wait_send())
        when((st == 0) & (s > 0), lambda: down(st, k).wait_send())

    loop(3 * K, spent)


OUTS = dict(dw=(2, D, D), enc_grad=(L, D), probs=(HEADS, L, L))
ROWS_OUT = dict(dec_out=((1, D), BF), dec_grad=((1, D), BF), gain_out=((2, D // 4), F32))


def fused(w, xall, dec8, gains, lens):
    names = [*OUTS, *ROWS_OUT, *SCRATCH, *SEMS]
    hbm, vmem = pl.BlockSpec(memory_space=pl.ANY), pl.BlockSpec(memory_space=pltpu.VMEM)
    return pl.pallas_call(
        functools.partial(kernel, names),
        out_shape=[jax.ShapeDtypeStruct(v, BF) for v in OUTS.values()] + [jax.ShapeDtypeStruct(*v) for v in ROWS_OUT.values()],
        in_specs=[hbm, hbm, vmem, vmem, pl.BlockSpec(memory_space=pltpu.SMEM)],
        out_specs=[hbm] * len(OUTS) + [vmem] * len(ROWS_OUT),
        scratch_shapes=[pltpu.VMEM(*v) for v in SCRATCH.values()] + [pltpu.SemaphoreType.DMA(v) for v in SEMS.values()],
        compiler_params=pltpu.CompilerParams(collective_id=0, has_side_effects=True, vmem_limit_bytes=(64 << 20) - (128 << 10)),
        name="fused",
    )(w, xall, dec8, gains, lens)


def body(enc_in, dec_in, lengths, weights, gains, dec_cot):
    s, p = lax.axis_index("section"), lax.axis_index("pair")
    dps = lax.axis_size("dp")
    dec8 = f32(jnp.concatenate([dec_in, dec_cot], axis=0).reshape(8, D))
    dw, enc_grad, _, dec_out, dec_grad, gg = fused(weights[0], enc_in, dec8, gains[0], lengths)
    if dps > 2:
        groups = [[i for i in range(dps) if i % 2 == c] for c in range(2)]
        dw = bf16(lax.psum(dw, "dp", axis_index_groups=groups))
        gg = lax.psum(gg, "dp", axis_index_groups=groups)
    unused = (p >= 2) & (s == 0) | (p == 3) & (s == 2)
    dw = jnp.where(unused, 0.0, f32(jnp.concatenate([dw[0], dw[1]], axis=1)))
    return dec_out[None], enc_grad[None], dec_grad[None], dw[None], gg[None]


def solution(mesh):
    rows, both = P(None, ("pair", "dp"), None), P("section", ("pair", "dp"), None)
    return jax.shard_map(
        body, mesh=mesh,
        in_specs=(rows, rows, P(None, ("pair", "dp")), P("section", None, "pair"), P("section", None, None), rows),
        out_specs=(both, both, both, P("section", None, "pair"), P("section", None, "pair")),
        check_vma=False)
```

```python
import functools

import jax
import jax.numpy as jnp
from jax import lax
from jax.experimental import pallas as pl
from jax.experimental.pallas import tpu as pltpu
from jax.sharding import PartitionSpec as P

D = 768
HALF = 384
HEADS = 12
HEAD = 64
L = 512
EPSILON = 1e-06
NEGATIVE = -1e30
K = 8
R = HALF // K
H = K // 2
LR, LD, PRE = 4, 12, 2
W2 = (4, 8, 12)
MESH = pl.DeviceIdType.MESH
X, Y, UP, DOWN = 0, 1, 2, 3
BF = jnp.bfloat16
F32 = jnp.float32


def f32(v):
    return v.astype(F32)


def bf16(v):
    return v.astype(BF)


def loop(n, go, start=0):
    def step(i, carry):
        go(i)
        return carry

    lax.fori_loop(start, n, step, 0)


def norm(v, g):
    return v * lax.rsqrt(jnp.mean(v * v, axis=-1, keepdims=True) + EPSILON) * g


def norm_back(v, g, c):
    r = lax.rsqrt(jnp.mean(v * v, axis=-1, keepdims=True) + EPSILON)
    gc = g * c
    back = r * gc - v * (r * r * r) * jnp.mean(v * gc, axis=-1, keepdims=True)
    return back, jnp.sum(r * v * c, axis=0, keepdims=True)


def gelu_both(u):
    a = 0.7978845608028654
    t = jnp.tanh(a * (u + 0.044715 * u * u * u))
    return 0.5 * u * (1.0 + t), 0.5 * (1.0 + t) + 0.5 * u * (1.0 - t * t) * a * (1.0 + 0.134145 * u * u)


def nn(a, b):
    return jnp.dot(a, b, preferred_element_type=F32)


def nt(a, b):
    return lax.dot_general(a, b, (((1,), (1,)), ((), ())), preferred_element_type=F32)


def tn(a, b):
    return lax.dot_general(a, b, (((0,), (0,)), ((), ())), preferred_element_type=F32)


def iota(shape, dim):
    return lax.broadcasted_iota(jnp.int32, shape, dim)


def head_mask(rows):
    return iota((rows, D), 1) // HEAD == lax.rem(iota((rows, D), 0), 16)


def pick(slot):
    return bf16(f32(iota((32, L), 1) == iota((32, L), 0) * 16 + slot))


def gather16():
    return bf16(f32(iota((32, L), 1) // 16 == iota((32, L), 0)))


def spread(rows):
    wide = nn(bf16(f32(iota((L, 32), 0) // 16 == iota((L, 32), 1))), rows)
    return bf16(jnp.where(head_mask(L), wide, 0.0))


SCRATCH = dict(
    W=((14, D, D), BF), cb=((6, D, D), BF), og=((2, HALF, D), BF), sr=((12, HALF, D), BF),
    rr=((3, K, R, D), BF), ox=((3, K, R, D), BF), oy=((3, K, R, D), BF), zu=((3, K, R, D), BF), zd=((2, K, R, D), BF),
    A=((8, L, D), BF), enc=((L, D), BF), B=((4, L, D), BF), T=((3, D, L), BF), mid=((L, D), F32), gfn=((L, D), F32), ring=((3, L, L), BF),
    gall=((4, 2, D), F32), dec=((8, 1, D), F32), dgrow=((1, D), F32), DI=((32, 1, D), F32), CR=((32, 1, D), F32), DM=((32, 1, D), F32), DR=((32, 1, D), F32),
    ROWS=((32, 1, D), F32), ROWS2=((32, 1, 2 * D), F32), dmrow=((1, D), F32), u=((16, D), BF), drow=((1, D), F32),
    AB=((2, 32, D), BF), GP=((32, D), BF), GH=((2, 32, D), BF), PB=((4, 32, D), BF), orow=((1, 2 * D), F32), GT=((4, 1, D), F32),
    fac=((2, 16, D), BF), FB=((2, 16, 16, D), BF), GD=((32, D), F32), GB=((32, 1, 2 * D), F32), gg=((4, 1, 2 * D), F32),
    cp=((16, L), F32), keep=((2, 32, D), BF),
)
SEMS = dict(
    ssem=(4, 4, 2, K), rsem=(16, K), csend=(16, K), crecv=(16,), lsem=(8,), psem=(4,),
    spre=(2,), rdi=(1,), scr=(4,), rcr=(1,), sg=(4,), rg=(1,), sdm=(17,), rdm=(2,), su=(16,), ru=(1,), sd1=(8,), rdr=(1,),
    sact=(3,), ract=(3,), sp=(4,), rpb=(4,), sgh=(2,), rgh=(2,), so=(16,), ror=(1,), sgt=(32,), rgt=(4,),
    sfb=(2,), rfb=(2,), sfs=(1,), rfs=(1,), sgd=(1,), rgd=(1,), sdg=(16,), rdg=(1,), sgb=(4, 8), rgb=(1,),
    ssib=(12,), rsib=(12,), sxy=(3, 3, K), sz=(3, K), rrr=(3, K), rox=(3, K), roy=(3, K), rzu=(3, K), rzd=(3, K),
    sfin=(2, K, 3), rfin=(2, K, 2),
)


class Refs:
    pass


def kernel(names, w, xall, dec8, gains, *rest):
    o = Refs()
    for name, ref in zip(names, rest, strict=True):
        setattr(o, name, ref)
    s, p, d = lax.axis_index("section"), lax.axis_index("pair"), lax.axis_index("dp")
    c = lax.rem(d, 2)
    base = d - c
    xn = p + 1 - 2 * lax.rem(p, 2)
    yn = p + 2 - 4 * (p // 2)
    dg = 3 - p
    xb = lax.rem(p, 2)
    is0, is1, is2, is3 = s == 0, s == 1, s == 2, s == 3
    lin = (s * 4 + p) * 2 + c
    row = c * 16 + p * 4 + s
    W, A, B, T, cb = o.W, o.A, o.B, o.T, o.cb

    def dev(s_, p_, c_):
        return (s_, p_, base + c_)

    TO = {X: dev(s, xn, c), Y: dev(s, yn, c), UP: dev(s + 1, p, c), DOWN: dev(s - 1, p, c)}
    SIB = dev(s, p, 1 - c)

    def remote(src, dst, ss, rs, to):
        return pltpu.make_async_remote_copy(src_ref=src, dst_ref=dst, send_sem=ss, recv_sem=rs, device_id=to, device_id_type=MESH)

    def local(src, dst, sem):
        return pltpu.make_async_copy(src, dst, sem)

    def when(cond, f):
        pl.when(cond)(f)

    def unless(cond, f):
        pl.when(jnp.logical_not(cond))(f)

    own_here = (is0 & (p < 2)) | is1

    def own_block(j):
        return jnp.where(is0, p + 2 * j, jnp.where(is1, 4 * (1 + j) + p, 12 + j))

    def load_own(j):
        return local(w.at[:, pl.ds(j * D, D)], W.at[own_block(j)], o.lsem.at[j])

    def load_ws(j):
        return local(w.at[:, pl.ds(j * D, D)], cb.at[j], o.lsem.at[j])

    def load_w3():
        return local(w.at[:, pl.ds(pl.multiple_of(c * D, D), D)], cb.at[0], o.lsem.at[0])

    loads_own = own_here | (is2 & (p == 2))

    @pl.when(loads_own)
    def _():
        load_own(0).start()
        load_own(1).start()

    @pl.when(is2 & (p < 2))
    def _():
        load_ws(0).start()
        load_ws(1).start()

    when(is3, lambda: load_w3().start())
    load_x = local(xall.at[s], A.at[0], o.lsem.at[2])
    load_x.start()

    bar = pltpu.get_barrier_semaphore()

    def tell(i):
        @pl.when(i != lin)
        def _():
            pl.semaphore_signal(bar, inc=1, device_id=dev(i // 8, lax.rem(i // 2, 4), lax.rem(i, 2)), device_id_type=MESH)

    loop(32, tell)
    pl.semaphore_wait(bar, 31)

    @pl.when(loads_own)
    def _():
        load_own(0).wait()
        load_own(1).wait()

    @pl.when(is2 & (p < 2))
    def _():
        load_ws(0).wait()
        load_ws(1).wait()

    when(is3, lambda: load_w3().wait())

    def part(st, q, k):
        e = st // 3
        block = (4 * st + q) * (1 - e) + (12 + q // 2) * e
        start = c * HALF * (1 - e) + (lax.rem(q, 2) * HALF + c * (HALF // 2)) * e + k * R
        return W.at[block, pl.ds(pl.multiple_of(start, 16), R), :]

    def copy(link, st, q, k, kind=0):
        return remote(part(st, q, k), part(st, q, k), o.ssem.at[link, st, kind, k], o.rsem.at[4 * st + q, k], TO[link])

    def sibling(st, q, k):
        return remote(part(st, q, k), part(st, q, k), o.csend.at[4 * st + q, k], o.crecv.at[4 * st + q], SIB)

    def got(st, q, k):
        copy(X, st, q, k).wait_recv()
        sibling(st, q, k).start()

    @pl.when(is1)
    def _():
        loop(2 * K, lambda t: copy(DOWN, 1 + t // K, p, lax.rem(t, K)).start())
        for k in range(PRE):
            for link in (UP, X, Y):
                copy(link, 1, p, k).start()

    def relay(st, k):
        even = lax.rem(k, 2) == 0
        when(even, lambda: copy(Y, st, xn, k, 1).start())
        unless(even, lambda: copy(X, st, yn, k, 1).start())

    def over_z(st, k):
        return ((st == 1) | (st == 2)) & (lax.rem(k, 4) >= 2)

    def step0(t):
        @pl.when(t < 2 * K)
        def _():
            h, k = t // K, lax.rem(t, K)
            b = xb + 2 - 2 * h

            @pl.when(p < 2)
            def _():
                @pl.when(t > 1)
                def _():
                    h2, k2 = (t - 2) // K, lax.rem(t - 2, K)
                    copy(Y, 0, b, k2, h2).wait_send()
                    copy(X, 0, b, k2, h2).wait_send()

                copy(Y, 0, b, k, h).start()
                copy(X, 0, b, k, h).start()
                when(t < K, lambda: copy(UP, 0, p, k).start())

            @pl.when(p >= 2)
            def _():
                got(0, b, k)
                when(t < K, lambda: copy(UP, 0, p, k).start())
                copy(X, 0, b, k, h).start()

        @pl.when((t > 1) & (t < 2 * K + 2))
        def _():
            got(0, 3 - xb - 2 * ((t - 2) // K), lax.rem(t - 2, K))

        @pl.when((t >= 2 * K) & (t < 4 * K + H))
        def _():
            st, k = (t - K) // K, lax.rem(t, K)
            got(st, p, k)
            copy(X, st, p, k).start()
            copy(Y, st, p, k).start()

        @pl.when((t >= 2 * K + LR) & (t < 4 * K + H + LR))
        def _():
            st, k = (t - LR - K) // K, lax.rem(t - LR, K)
            got(st, xn, k)
            got(st, yn, k)
            when(st == 3, lambda: relay(st, k))

        @pl.when(t >= 2 * K + LD)
        def _():
            got((t - LD - K) // K, dg, lax.rem(t - LD, K))

    ROUTES = {2: [(X, 2), (X, 3), (Y, 0), (Y, 1)], 3: [(Y, 2), (Y, 3)], 0: [(X, 0), (X, 1)], 1: [(Y, 0), (X, 2), (Y, 1), (X, 3)]}

    def corner_step(corner, k):
        def go():
            for link, q in ROUTES[corner]:
                if corner != 2:
                    got(3, q, k)
                if corner == q:
                    copy(UP, 3, q, k).start()
                    copy(DOWN, 3, q, k).start()
                copy(link, 3, q, k, q % 2).start()

        when((p == corner) & (k >= 0) & (k < H), go)

    def step2(t):
        corner_step(2, t - W2[0])
        corner_step(0, t - W2[1])
        corner_step(3, t - W2[1])
        corner_step(1, t - W2[2])
        k = t - W2[2] - LR
        for corner, qs in ((3, (0, 1)), (0, (2, 3))):
            @pl.when((p == corner) & (k >= 0) & (k < H))
            def _(qs=qs):
                for q in qs:
                    got(3, q, k)

    def in_stream(t):
        return (t >= 0) & ((t < 3 * K) | ((t < 3 * K + H) & (s != 2)))

    def step1(t):
        @pl.when(in_stream(t))
        def _():
            st, k = t // K, lax.rem(t, K)
            here = is1 & ((st == 1) | (st == 2))
            unless(here, lambda: got(st, p, k))

            @pl.when(jnp.logical_not(is1 & (st == 1) & (k < PRE)))
            def _():
                when((st < 3) & (s < 3), lambda: copy(UP, st, p, k).start())
                when((st == 3) & is1, lambda: copy(DOWN, st, p, k).start())
                copy(X, st, p, k).start()
                copy(Y, st, p, k).start()

        when(is2, lambda: step2(t))

        @pl.when(in_stream(t - LR))
        def _():
            st, k = (t - LR) // K, lax.rem(t - LR, K)
            got(st, xn, k)
            got(st, yn, k)
            unless((s > 1) & over_z(st, k), lambda: relay(st, k))

        @pl.when(in_stream(t - LD))
        def _():
            st, k = (t - LD) // K, lax.rem(t - LD, K)
            got(st, dg, k)
            when(is1 & ((st == 1) | (st == 2)), lambda: copy(DOWN, st, dg, k, 1).start())
            when((is1 | is2) & over_z(st, k), lambda: copy(UP, st, dg, k, 1).start())

    def pump(a0, b0, a1, b1):
        when(is0, lambda: loop(b0, step0, a0))
        when(s > 0, lambda: loop(b1, step1, a1))

    def mine_block(b):
        return (is0 & (p < 2) & (b < 4) & (lax.rem(b, 2) == p)) | (is1 & (b >= 4) & (lax.rem(b, 4) == p))

    def ready(b):
        @pl.when(jnp.logical_not(mine_block(b)))
        def _():
            other = W.at[b, pl.ds(pl.multiple_of((1 - c) * HALF, HALF), HALF), :]
            remote(other, other, o.csend.at[b, 0], o.crecv.at[b], SIB).wait_recv()

    def w2_ready():
        @pl.when(jnp.logical_not(is2 & (p == 2)))
        def _():
            for q in range(4):
                start = pl.multiple_of((q % 2) * HALF + (1 - c) * (HALF // 2), 16)
                other = W.at[12 + q // 2, pl.ds(start, HALF // 2), :]
                remote(other, other, o.csend.at[12 + q, 0], o.crecv.at[12 + q], SIB).wait_recv()

    def drain(cond, link, st, kind, n, each=1, start=0):
        def go(i):
            copy(link, st, p, start + each * i, kind).wait_send()

        when(cond, lambda: loop(n, go))

    def weights_sent():
        always = s < 4

        def halves(b):
            unless(mine_block(b), lambda: loop(K, lambda k: sibling(b // 4, lax.rem(b, 4), k).wait_send()))

        loop(12, halves)
        unless(is2 & (p == 2), lambda: loop(4, lambda q: loop(H, lambda k: sibling(3, q, k).wait_send())))

        @pl.when(is0)
        def _():
            @pl.when(p < 2)
            def _():
                for k in (K - 2, K - 1):
                    copy(X, 0, p, k, 1).wait_send()
                    copy(Y, 0, p, k, 1).wait_send()

            drain(p >= 2, X, 0, 0, K)
            drain(p >= 2, X, 0, 1, K)
            drain(always, UP, 0, 0, K)

        @pl.when(s > 0)
        def _():
            drain(s < 3, UP, 0, 0, K)
            drain(always, X, 0, 0, K)
            drain(always, Y, 0, 0, K)
            drain(always, Y, 0, 1, K // 2, 2, 0)
            drain(always, X, 0, 1, K // 2, 2, 1)

        for st in (1, 2):
            drain(always, X, st, 0, K)
            drain(always, Y, st, 0, K)
            drain(is1, Y, st, 1, K // 2, 2, 0)
            drain(is1, X, st, 1, K // 2, 2, 1)
            drain(s > 1, Y, st, 1, K // 4, 4, 0)
            drain(s > 1, X, st, 1, K // 4, 4, 1)
            drain(is1 | is2, UP, st, 0, K)
            drain(is1 | is2, UP, st, 1, K // 4, 4, 2)
            drain(is1 | is2, UP, st, 1, K // 4, 4, 3)
            drain(is1, DOWN, st, 0, K)
            drain(is1, DOWN, st, 1, K)

        @pl.when(s != 2)
        def _():
            drain(always, X, 3, 0, H)
            drain(always, Y, 3, 0, H)
            drain(always, Y, 3, 1, H // 2, 2, 0)
            drain(always, X, 3, 1, H // 2, 2, 1)
            drain(is1, DOWN, 3, 0, H)

        @pl.when(is2)
        def _():
            drain(always, UP, 3, 0, H)
            drain(always, DOWN, 3, 0, H)
            for corner, routes in ROUTES.items():
                for link, q in routes:
                    drain(p == corner, link, 3, q % 2, H)

    def send_gains(i):
        @pl.when(i == s)
        def _():
            local(gains, o.gall.at[s], o.rg.at[0]).start()

        unless(i == s, lambda: remote(gains, o.gall.at[s], o.sg.at[i], o.rg.at[0], dev(i, p, c)).start())

    loop(4, send_gains)
    o.dec[:, 0, :] = dec8[0:8, :]
    dec, cot = o.dec.at[pl.ds(0, 4)], o.dec.at[pl.ds(4, 4)]
    four = pl.ds(c * 16 + p * 4, 4)

    def send_dec(i):
        @pl.when((p == 0) & (i == c))
        def _():
            local(dec, o.DI.at[four], o.rdi.at[0]).start()

        unless((p == 0) & (i == c), lambda: remote(dec, o.DI.at[four], o.spre.at[i], o.rdi.at[0], dev(2, 0, i)).start())

    when(is2, lambda: loop(2, send_dec))

    def send_cot(i):
        @pl.when((p == 2 + i // 2) & (lax.rem(i, 2) == c))
        def _():
            local(cot, o.CR.at[four], o.rcr.at[0]).start()

        unless((p == 2 + i // 2) & (lax.rem(i, 2) == c),
               lambda: remote(cot, o.CR.at[four], o.scr.at[i], o.rcr.at[0], dev(3, 2 + i // 2, lax.rem(i, 2))).start())

    when(is3, lambda: loop(4, send_cot))

    def gain(sec, r):
        return o.gall[sec][r:r + 1, :]

    def to_core(f):
        loop(16, lambda i: f(i, i // 4, lax.rem(i, 4)))

    def others(f):
        to_core(lambda i, s_, p_: unless((s_ == s) & (p_ == p), lambda: f(i, s_, p_).wait_send()))

    def decoder_start0():
        local(o.DI, o.DI, o.rdi.at[0]).wait()
        rows = o.DI[:, 0, :]
        dn = bf16(norm(rows, gain(2, 0)))
        o.keep[0] = dn
        sv = bf16(nn(dn, cb[0]))
        o.keep[1] = sv
        o.DM[:, 0, :] = rows + nt(sv, cb[1])
        remote(o.DM, o.DM, o.sdm.at[16], o.rdm.at[1], dev(2, 1, c)).start()

        def go(i, s_, p_):
            me = (s_ == s) & (p_ == p)
            src = o.DM.at[c * 16 + p_ * 4 + s_]
            when(me, lambda: local(src, o.dmrow, o.rdm.at[0]).start())
            unless(me, lambda: remote(src, o.dmrow, o.sdm.at[i], o.rdm.at[0], dev(s_, p_, c)).start())

        to_core(go)

    def decoder_start1():
        remote(o.DM, o.DM, o.sdm.at[16], o.rdm.at[1], dev(2, 1, c)).wait_recv()
        cn = bf16(norm(o.DM[:, 0, :], gain(2, 1)))
        o.keep[0] = cn
        q = bf16(nn(cn, cb[0]))
        o.keep[1] = q
        cb[2, 0:L, :] = bf16(nt(spread(q), cb[1]))

        def go(i, s_, p_):
            me = (s_ == s) & (p_ == p)
            src = cb.at[2, pl.ds(pl.multiple_of((c * 16 + p_ * 4 + s_) * 16, 16), 16), :]
            when(me, lambda: local(src, o.u, o.ru.at[0]).start())
            unless(me, lambda: remote(src, o.u, o.su.at[i], o.ru.at[0], dev(s_, p_, c)).start())

        to_core(go)

    x_, q_, k_, v_, att_, enc0_, fnorm_, act_ = range(8)

    def turned(src, dst):
        for j in range(6):
            dst[j * 128:(j + 1) * 128, :] = src[:, j * 128:(j + 1) * 128].T

    def turned_back(src, dst):
        for j in range(6):
            dst[:, j * 128:(j + 1) * 128] = src[j * 128:(j + 1) * 128, :].T

    length = sum(jnp.where(s == i, dec8[8 + i:9 + i, 0:1], 0.0) for i in range(4))
    live = f32(iota((L, 1), 0)) < length

    HALVES = (slice(0, HALF), slice(HALF, D))
    QUARTERS = [slice(i * 128, (i + 1) * 128) for i in range(4)]

    def project():
        for rows in QUARTERS:
            A[act_, rows, :] = bf16(norm(f32(A[x_, rows, :]), gain(0, 0)))

        for dst, b, scale in ((q_, 0, 0.125), (v_, 1, 1.0), (k_, 2, 1.0)):
            for cols in HALVES:
                A[dst, :, cols] = bf16(f32(bf16(nn(A[act_], W[b, :, cols]))) * scale)

    def padded(ref, i, hh):
        rows = ref[pl.ds(pl.multiple_of(i * 128 + hh * 64, 64), 64), :]
        zero = jnp.zeros((64, L), BF)
        return jnp.concatenate([rows, zero] if hh == 0 else [zero, rows], axis=0)

    def lanes(i):
        return pl.ds(pl.multiple_of(i * 128, 128), 128)

    def half_rows(i, hh):
        return pl.ds(pl.multiple_of(i * 128 + hh * 64, 64), 64)

    def spill(h):
        return local(o.ring.at[lax.rem(h, 3)], o.probs.at[h], o.psem.at[lax.rem(h, 3)])

    def fetch(h):
        return local(o.probs.at[h], o.ring.at[lax.rem(h, 3)], o.psem.at[lax.rem(h, 3)])

    def attend(i):
        kp = A[k_, :, lanes(i)]
        for hh in range(2):
            head = 2 * i + hh
            when(head > 2, lambda: spill(head - 3).wait())
            sc = jnp.where(live, nn(kp, padded(T.at[0], i, hh)), NEGATIVE)
            e = jnp.exp(sc - jnp.max(sc, axis=0, keepdims=True))
            pr = bf16(e * (1.0 / jnp.sum(e, axis=0, keepdims=True)))
            o.ring[lax.rem(head, 3)] = pr
            T[2, half_rows(i, hh), :] = bf16(nn(T[1, half_rows(i, hh), :], pr))
            spill(head).start()

    def after_attention():
        for cols in HALVES:
            A[enc0_, :, cols] = bf16(f32(A[x_, :, cols]) + nt(A[att_], W[3, cols, :]))
        for rows in QUARTERS:
            e0 = f32(A[enc0_, rows, :])
            o.mid[rows, :] = e0
            A[fnorm_, rows, :] = bf16(norm(e0, gain(1, 0)))

    HID = {0: (4, 6), 1: (8, 10), 2: (5, 7), 3: (9, 11)}

    def feed(i):
        ub, db = HID[i]
        for cols in HALVES:
            h = bf16(nn(A[fnorm_], W[ub, :, cols]))
            B[i, :, cols] = h
            A[act_, :, cols] = bf16(gelu_both(f32(h))[0])
        for cols in HALVES:
            o.mid[:, cols] += nt(A[act_], W[db, cols, :])

    pump(0, 2 * K + 2, 0, K + LD)
    for b in range(4):
        ready(b)
    load_x.wait()
    local(o.gall, o.gall, o.rg.at[0]).wait()
    when(is2 & (p == 0), decoder_start0)
    project()
    pump(18, 20, 20, 21)
    turned(A.at[q_], T.at[0])
    turned(A.at[v_], T.at[1])
    pump(20, 22, 21, 22)
    when(is2 & (p == 1), decoder_start1)

    def attend_pump(i):
        attend(i)
        when(is0, lambda: loop(2, lambda t: step0(22 + 2 * i + t)))
        when((s > 0) & (i < 5), lambda: step1(22 + i))

    loop(6, attend_pump)
    for head in (9, 10, 11):
        spill(head).wait()
    turned_back(T.at[2], A.at[att_])
    after_attention()
    pump(34, 36, 27, 28)
    for b in range(4, 8):
        ready(b)
    feed(0)
    pump(36, 40, 28, 32)
    feed(2)
    pump(40, 44, 32, 36)
    for b in range(8, 12):
        ready(b)
    feed(1)
    pump(44, 46, 36, 38)
    feed(3)
    pump(46, 48, 38, 40)

    for rows in QUARTERS:
        o.enc[rows, :] = bf16(norm(o.mid[rows, :], gain(1, 1)))

    w2_ready()

    remote(o.u, o.u, o.su.at[0], o.ru.at[0], SIB).wait_recv()
    remote(o.dmrow, o.dmrow, o.sdm.at[0], o.rdm.at[0], SIB).wait_recv()
    enc = o.enc
    live_row = f32(iota((1, L), 1)) < length
    cs = jnp.where(live_row, nt(o.u[...], enc[...]) * 0.125, NEGATIVE)
    e = jnp.exp(cs - jnp.max(cs, axis=-1, keepdims=True))
    cp = e / jnp.sum(e, axis=-1, keepdims=True)
    o.cp[...] = cp
    z = bf16(nn(bf16(cp), enc[...]))
    catt = bf16(jnp.sum(jnp.where(head_mask(16), nn(z, W[12]), 0.0), axis=0, keepdims=True))
    decoded = f32(bf16(o.dmrow[...] + nt(jnp.broadcast_to(catt, (16, D)), W[13])[0:1]))
    o.drow[...] = decoded
    o.fac[1] = z

    def send_row(i):
        p_, c_ = i // 2, lax.rem(i, 2)
        me = is3 & (p_ == p) & (c_ == c)
        when(me, lambda: local(o.drow, o.DR.at[row], o.rdr.at[0]).start())
        unless(me, lambda: remote(o.drow, o.DR.at[row], o.sd1.at[i], o.rdr.at[0], dev(3, p_, c_)).start())

    loop(8, send_row)
    up_dev, down_dev = is3 & (p < 2), is3 & (p >= 2)
    j = 2 * lax.rem(p, 2) + c
    w3 = cb

    def act_copy():
        return remote(o.AB.at[c], o.AB.at[c], o.sact.at[0], o.ract.at[0], TO[Y])

    def gp_copy():
        return remote(o.GP, o.GP, o.sact.at[1], o.ract.at[1], TO[Y])

    def ab_sib():
        return remote(o.AB.at[c], o.AB.at[c], o.sact.at[2], o.ract.at[2], SIB)

    def gh_copy():
        return remote(o.GH.at[c], o.GH.at[c], o.sgh.at[0], o.rgh.at[0], TO[Y])

    def gh_sib():
        return remote(o.GH.at[c], o.GH.at[c], o.sgh.at[1], o.rgh.at[1], SIB)

    def rows_here():
        local(o.DR, o.DR, o.rdr.at[0]).wait()

    @pl.when(up_dev)
    def _():
        rows_here()
        tnorm = bf16(norm(o.DR[:, 0, :], gain(3, 0)))
        o.keep[0] = tnorm
        act, slope = gelu_both(nn(tnorm, w3[0]))
        o.AB[c] = bf16(act)
        act_copy().start()
        o.GP[...] = bf16(slope)
        gp_copy().start()

    def pb_copy(i):
        return remote(o.PB.at[j], o.PB.at[j], o.sp.at[i], o.rpb.at[j], dev(3, 2 + i // 2, lax.rem(i, 2)))

    def pb_from(i):
        return remote(o.PB.at[i], o.PB.at[i], o.sp.at[i], o.rpb.at[i], SIB)

    def out_copy(i):
        s_, p_ = i // 2, 2 * lax.rem(p, 2) + lax.rem(i, 2)
        return remote(o.ROWS2.at[c * 16 + p_ * 4 + s_], o.orow, o.so.at[i], o.ror.at[0], dev(s_, p_, c)), (s_ == s) & (p_ == p), \
            local(o.ROWS2.at[c * 16 + p_ * 4 + s_], o.orow, o.ror.at[0])

    @pl.when(down_dev)
    def _():
        act_copy().wait_recv()
        o.PB[j] = bf16(nt(o.AB[c], w3[0]))
        loop(4, lambda i: unless(i == j, lambda: pb_copy(i).start()))
        ab_sib().start()
        rows_here()
        local(o.CR, o.CR, o.rcr.at[0]).wait()
        loop(4, lambda i: unless(i == j, lambda: pb_from(i).wait_recv()))
        tmid = o.DR[:, 0, :] + (f32(o.PB[0]) + f32(o.PB[1])) + (f32(o.PB[2]) + f32(o.PB[3]))
        g_tmid, gg31 = norm_back(tmid, gain(3, 1), o.CR[:, 0, :])
        g_tb = bf16(g_tmid)
        gp_copy().wait_recv()
        o.GH[c] = bf16(f32(o.GP[...]) * nn(g_tb, w3[0]))
        gh_copy().start()
        o.keep[0] = g_tb
        o.ROWS2[:, 0, :] = jnp.concatenate([norm(tmid, gain(3, 1)), g_tmid], axis=1)

        def go(i):
            far, me, near = out_copy(i)
            when(me, lambda: near.start())
            unless(me, lambda: far.start())

        loop(8, go)
        o.gg[3] = jnp.concatenate([jnp.zeros((1, D), F32), gg31], axis=1)

    def gt_copy(i):
        s_, p_, c_ = i // 8, lax.rem(i // 2, 4), lax.rem(i, 2)
        return remote(o.ROWS.at[c_ * 16 + p_ * 4 + s_], o.GT.at[j], o.sgt.at[i], o.rgt.at[j], dev(s_, p_, c_))

    @pl.when(up_dev)
    def _():
        gh_copy().wait_recv()
        o.ROWS[:, 0, :] = nt(o.GH[c], w3[0])

        def go(i):
            when(i == lin, lambda: local(o.ROWS.at[row], o.GT.at[j], o.rgt.at[j]).start())
            unless(i == lin, lambda: gt_copy(i).start())

        loop(32, go)
        gh_sib().start()

    local(o.orow, o.orow, o.ror.at[0]).wait()
    for i in range(4):
        local(o.GT.at[i], o.GT.at[i], o.rgt.at[i]).wait()
    g_tn = (o.GT[0] + o.GT[1]) + (o.GT[2] + o.GT[3])
    g_tmid = o.orow[:, D:]
    o.dec_out[...] = bf16(o.orow[:, :D])
    decoded = o.drow[...]
    gp, gg30 = norm_back(decoded, gain(3, 0), g_tn)
    gd = bf16(g_tmid + gp)
    @pl.when(jnp.logical_not(is3 & (p == 2) & (c == 0)))
    def _():
        o.gg[3] = jnp.zeros((1, 2 * D), F32)

    o.gg[3, :, 0:D] = gg30
    g_catt = bf16(nn(jnp.broadcast_to(gd, (16, D)), W[13]))
    vv = bf16(nt(jnp.where(head_mask(16), g_catt, jnp.zeros((), BF)), W[12]))
    cp = o.cp[...]
    g_cp = nt(vv, enc[...])
    g_cs = bf16(cp * (g_cp - jnp.sum(g_cp * cp, axis=-1, keepdims=True)))
    both_l = jnp.concatenate([g_cs, bf16(cp)], axis=0)
    both_r = jnp.concatenate([bf16(f32(o.u[...]) * 0.125), vv], axis=0)
    z = o.fac[1]
    y = bf16(nn(g_cs, enc[...]) * 0.125)
    slot = iota((16, D), 0)
    gdw = jnp.broadcast_to(gd, (16, D))
    cattw = jnp.broadcast_to(catt, (16, D))
    o.fac[0] = jnp.where(slot < 12, y, gdw)
    o.fac[1] = jnp.where(slot < 12, z, jnp.where(slot == 12, g_catt, jnp.where(slot == 13, gdw, cattw)))

    def fb_copy(i):
        return remote(o.fac.at[i], o.FB.at[c, p * 4 + s], o.sfb.at[i], o.rfb.at[0], dev(2, 1 + i, c))

    for i in range(2):
        me = is2 & (p == 1 + i)
        when(me, lambda i=i: local(o.fac.at[i], o.FB.at[c, p * 4 + s], o.rfb.at[0]).start())
        unless(me, lambda i=i: fb_copy(i).start())

    def load_again(j):
        return local(w.at[:, pl.ds(j * D, D)], W.at[12 + j], o.lsem.at[j])

    when(is2 & (p == 1), lambda: others(lambda i, s_, p_: remote(o.u, o.u, o.su.at[i], o.ru.at[0], dev(s_, p_, c))))

    def gain_copy(sec, i):
        return remote(o.gg.at[sec], o.GB.at[row], o.sgb.at[sec, i], o.rgb.at[0], dev(sec, i // 2, lax.rem(i, 2)))

    def send_gain(sec):
        def go(i):
            me = (s == sec) & (i == p * 2 + c)
            when(me, lambda: local(o.gg.at[sec], o.GB.at[row], o.rgb.at[0]).start())
            unless(me, lambda: gain_copy(sec, i).start())

        loop(8, go)

    send_gain(3)

    def mine(b, k):
        return cb.at[b // 2, pl.ds(pl.multiple_of(lax.rem(b, 2) * HALF + k * R, R), R), :]

    def sib(b, slot):
        return remote(o.og.at[slot], o.sr.at[b], o.ssib.at[b], o.rsib.at[b], SIB)

    ORDER = [6, 4, 7, 5, 10, 8, 11, 9, 3, 1, 2, 0]

    def emit(b, left, right):
        n = ORDER.index(b)
        if n >= 2:
            sib(ORDER[n - 2], n % 2).wait_send()
        other = pl.ds(pl.multiple_of((1 - c) * HALF, HALF), HALF)
        own = pl.ds(pl.multiple_of(c * HALF, HALF), HALF)
        o.og[n % 2] = bf16(nn(left[other, :], right[...]))
        sib(b, n % 2).start()
        cb[b // 2, (b % 2) * HALF:(b % 2 + 1) * HALF, :] = bf16(nn(left[own, :], right[...]))

    def arrived(st):
        for q in range(4):
            sib(4 * st + q, 0).wait_recv()

    def even(k):
        return lax.rem(k, 2) == 0

    def both(k, f):
        when(even(k), lambda: f(0))
        unless(even(k), lambda: f(1))

    def diag(st, k, y):
        return remote(mine(4 * st + dg, k), o.rr.at[st, k], o.sxy.at[0, st, k], o.rrr.at[st, k], TO[Y if y else X])

    def straight(kind, st, k, y):
        return remote(mine(4 * st + (yn if y else xn), k), (o.oy if y else o.ox).at[st, k], o.sxy.at[kind, st, k],
                      (o.roy if y else o.rox).at[st, k], TO[Y if y else X])

    def first(st, k):
        for q in (dg, xn, yn, p):
            m = mine(4 * st + q, k)
            m[...] = bf16(f32(m[...]) + f32(o.sr[4 * st + q, pl.ds(pl.multiple_of(k * R, R), R), :]))

        def f(odd):
            diag(st, k, not odd).start()
            straight(1, st, k, not odd).start()

        both(k, f)

    def second(st, k):
        diag(st, k, True).wait_recv()

        def f(odd):
            m = mine(4 * st + (yn if odd else xn), k)
            m[...] = bf16(f32(m[...]) + f32(o.rr[st, k]))
            straight(2, st, k, odd).start()

        both(k, f)

    def up(st, k):
        return remote(mine(4 * st + p, k), o.zd.at[st - 1, k], o.sz.at[st, k], o.rzd.at[st, k], TO[UP])

    def down(st, k):
        return remote(mine(4 * st + p, k), o.zu.at[st, k], o.sz.at[st, k], o.rzu.at[st, k], TO[DOWN])

    def third(st, k):
        straight(1, st, k, True).wait_recv()
        straight(1, st, k, False).wait_recv()
        m = mine(4 * st + p, k)
        return m, f32(m[...]) + f32(o.ox[st, k]) + f32(o.oy[st, k])

    def out_rows(jj, half, k):
        return o.dw.at[jj, pl.ds(pl.multiple_of(half * HALF + k * R, R), R), :]

    def fin_local(b, jj, k):
        return local(mine(b, k), out_rows(jj, c, k), o.sfin.at[jj, k, 0])

    def fin_sib(b, jj, k):
        return remote(mine(b, k), out_rows(jj, c, k), o.sfin.at[jj, k, 1], o.rfin.at[jj, k, 0], SIB)

    def fin_sib_in(jj, k):
        return remote(out_rows(jj, 1 - c, k), out_rows(jj, 1 - c, k), o.sfin.at[jj, k, 1], o.rfin.at[jj, k, 0], SIB)

    def fin_y(k, cross):
        to = dev(s, yn, 1 - c) if cross else TO[Y]
        return remote(mine(p, k), out_rows(1, c, k), o.sfin.at[1, k, 1 + cross], o.rfin.at[1, k, cross], to)

    def fin_y_in(k, cross):
        half = 1 - c if cross else c
        return remote(out_rows(1, half, k), out_rows(1, half, k), o.sfin.at[1, k, 1 + cross], o.rfin.at[1, k, cross], SIB)

    def last1(st, k):
        m, total = third(st, k)

        @pl.when(is3 | is0)
        def _():
            m[...] = bf16(total)
            when(is3, lambda: down(st, k).start())
            when(is0, lambda: up(st, k).start())

        @pl.when(is2)
        def _():
            down(st, k).wait_recv()
            m[...] = bf16(total + f32(o.zu[st, k]))
            down(st, k).start()

        @pl.when(is1)
        def _():
            down(st, k).wait_recv()
            up(st, k).wait_recv()
            m[...] = bf16(total + f32(o.zu[st, k]) + f32(o.zd[st - 1, k]))
            fin_local(4 * st + p, st - 1, k).start()
            fin_sib(4 * st + p, st - 1, k).start()

    def last0(k):
        m, total = third(0, k)

        @pl.when(is3)
        def _():
            m[...] = bf16(total)
            down(0, k).start()

        @pl.when(is1 | is2)
        def _():
            down(0, k).wait_recv()
            m[...] = bf16(total + f32(o.zu[0, k]))
            down(0, k).start()

        @pl.when(is0)
        def _():
            down(0, k).wait_recv()
            m[...] = bf16(total + f32(o.zu[0, k]))

            @pl.when(p < 2)
            def _():
                fin_local(p, 0, k).start()
                fin_sib(p, 0, k).start()

            @pl.when(p >= 2)
            def _():
                fin_y(k, 0).start()
                fin_y(k, 1).start()

    lag1 = (3 - s) - 3 * ((3 - s) // 3)
    lag0 = 3 - s

    N2 = 6

    def item(t):
        st = jnp.where(t < K, 1, jnp.where((t >= K + N2) & (t < 2 * K + N2), 0, 2))
        k = t - jnp.where(t < K, 0, jnp.where(t < K + N2, K, jnp.where(t < 2 * K + N2, K + N2, 2 * K)))
        return st, k

    def zstep(n):
        t1 = n - lag1
        st1, k1 = item(t1)
        when((t1 >= 0) & (t1 < 3 * K) & (st1 > 0), lambda: last1(st1, k1))
        t0 = n - lag0
        st0, k0 = item(t0)
        when((t0 >= 0) & (t0 < 3 * K) & (st0 == 0), lambda: last0(k0))

    L2, L3 = 2, 5

    def rstep(t):
        @pl.when(t < 3 * K)
        def _():
            st, k = item(t)
            when(k == 0, lambda: arrived(st))
            first(st, k)

        u = t - L2
        when((u >= 0) & (u < 3 * K), lambda: second(*item(u)))
        when(t >= L3, lambda: zstep(t - L3))

    def rsteps(a, b):
        loop(b, rstep, a)

    gg11 = jnp.zeros((1, D), F32)
    for rows in QUARTERS:
        g_enc = f32(bf16(tn(both_l[:, rows], both_r)))
        gm, part11 = norm_back(o.mid[rows, :], gain(1, 1), g_enc)
        o.mid[rows, :] = gm
        enc[rows, :] = bf16(gm)
        gg11 = gg11 + part11
    turned(enc, T.at[0])
    turned(A.at[fnorm_], T.at[1])

    def slopes(i):
        for cols in HALVES:
            a, slope = gelu_both(f32(B[i, :, cols]))
            A[act_, :, cols] = bf16(a)
            B[i, :, cols] = bf16(slope * nn(enc[...], W[HID[i][1], :, cols]))

    def back_out(i, begin=False):
        for cols in HALVES:
            back = nt(B[i], W[HID[i][0], cols, :])
            o.gfn[:, cols] = back if begin else o.gfn[:, cols] + back

    def emits(i):
        emit(HID[i][1], T.at[0], A.at[act_])
        emit(HID[i][0], T.at[1], B.at[i])

    for head in range(3):
        fetch(head).start()
    slopes(0)
    emits(0)
    slopes(2)
    emits(2)
    rsteps(0, 2)
    slopes(1)
    emits(1)
    rsteps(2, 4)
    slopes(3)
    emits(3)
    rsteps(4, 5)
    back_out(0, True)
    back_out(2)
    rsteps(5, 6)
    back_out(1)
    back_out(3)

    gg10 = jnp.zeros((1, D), F32)
    for rows in QUARTERS:
        gp, part10 = norm_back(f32(A[enc0_, rows, :]), gain(1, 0), o.gfn[rows, :])
        A[fnorm_, rows, :] = bf16(o.mid[rows, :] + gp)
        gg10 = gg10 + part10

    for cols in HALVES:
        B[0, :, cols] = bf16(nn(A[fnorm_], W[3, :, cols]))
    rsteps(6, 7)
    o.gg[1] = jnp.concatenate([gg10, gg11], axis=1)
    send_gain(1)
    turned(A.at[fnorm_], T.at[0])
    emit(3, T.at[0], A.at[att_])
    turned(B.at[0], T.at[1])
    turned(A.at[k_], T.at[2])
    rsteps(7, 8)

    lane_half = iota((L, 128), 1) // HEAD

    def attend_back(i):
        vp, qp, gp = A[v_, :, lanes(i)], A[q_, :, lanes(i)], B[0, :, lanes(i)]
        g_v = jnp.zeros((L, 128), F32)
        g_k = jnp.zeros((L, 128), F32)
        zero = jnp.zeros((), BF)
        for hh in range(2):
            head = 2 * i + hh
            fetch(head).wait()
            pr = o.ring[lax.rem(head, 3)]
            prf = f32(pr)
            g_p = nn(vp, padded(T.at[1], i, hh))
            g_s = bf16(prf * (g_p - jnp.sum(prf * g_p, axis=0, keepdims=True)))
            g_v = g_v + nn(pr, jnp.where(lane_half == hh, gp, zero))
            g_k = g_k + nn(g_s, jnp.where(lane_half == hh, qp, zero))
            T[0, half_rows(i, hh), :] = bf16(nn(T[2, half_rows(i, hh), :], g_s) * 0.125)
            when(head < 9, lambda: fetch(head + 3).start())
        B[1, :, lanes(i)] = bf16(g_v)
        B[2, :, lanes(i)] = bf16(g_k)

    def attend_back_step(i):
        attend_back(i)
        rstep(8 + i)

    loop(6, attend_back_step)
    turned_back(T.at[0], B.at[3])

    for rows in QUARTERS:
        A[att_, rows, :] = bf16(norm(f32(A[x_, rows, :]), gain(0, 0)))

    turned(A.at[att_], T.at[1])
    emit(1, T.at[1], B.at[1])
    emit(2, T.at[1], B.at[2])
    emit(0, T.at[1], B.at[3])
    rsteps(K + N2, K + N2 + 4)
    gg00 = jnp.zeros((1, D), F32)

    for cols in HALVES:
        o.gfn[:, cols] = nt(B[3], W[0, cols, :]) + nt(B[2], W[2, cols, :]) + nt(B[1], W[1, cols, :])
    for rows in QUARTERS:
        gp, part00 = norm_back(f32(A[x_, rows, :]), gain(0, 0), o.gfn[rows, :])
        A[act_, rows, :] = bf16(f32(A[fnorm_, rows, :]) + gp)
        gg00 = gg00 + part00
    out_enc = local(A.at[act_], o.enc_grad, o.lsem.at[3])
    out_enc.start()
    o.gg[0] = jnp.concatenate([gg00, jnp.zeros((1, D), F32)], axis=1)
    send_gain(0)
    rsteps(K + N2 + 4, 3 * K + L3 + 3)
    weights_sent()

    @pl.when(is2 & (p < 2))
    def _():
        load_again(0).start()
        load_again(1).start()

    def dw_out(jj):
        return local(W.at[4 + jj], o.dw.at[jj], o.lsem.at[4 + jj])

    def dw_done():
        dw_out(0).start()
        dw_out(1).start()

    def outer(jj, left, right):
        for t in range(3):
            cols = slice(t * 256, (t + 1) * 256)
            W[4 + jj, cols, :] = bf16(tn(left[:, cols], right))

    def both_cores(buf, left):
        for cc in range(2):
            outer(cc, left, buf[cc])
        dw_done()

    @pl.when(up_dev)
    def _():
        gh_sib().wait_send()
        pltpu.make_async_copy(o.GH.at[1 - c], o.GH.at[1 - c], o.rgh.at[1]).wait()
        both_cores(o.GH, o.keep[0])

    @pl.when(down_dev)
    def _():
        ab_sib().wait_send()
        pltpu.make_async_copy(o.AB.at[1 - c], o.AB.at[1 - c], o.ract.at[2]).wait()
        both_cores(o.AB, o.keep[0])

    factor_dev = is2 & ((p == 1) | (p == 2))

    def fs_copy():
        return remote(o.FB.at[c], o.FB.at[c], o.sfs.at[0], o.rfs.at[0], SIB)

    @pl.when(factor_dev)
    def _():
        local(o.FB.at[c], o.FB.at[c], o.rfb.at[0]).wait()
        fs_copy().start()

    def gd_copy():
        return remote(o.GD, o.GD, o.sgd.at[0], o.rgd.at[0], dev(2, 0, c))

    def gain2(slot):
        def go(i):
            when(i == p, lambda: local(o.gg.at[2], o.GB.at[slot], o.rgb.at[0]).start())
            unless(i == p, lambda: gain2_copy(slot, i).start())

        loop(4, go)

    def gain2_copy(slot, i):
        return remote(o.gg.at[2], o.GB.at[slot], o.sgb.at[2, i], o.rgb.at[0], dev(2, i, c))

    def all_factors():
        fs_copy().wait_send()
        pltpu.make_async_copy(o.FB.at[1 - c], o.FB.at[1 - c], o.rfs.at[0]).wait()
        return o.FB[...].reshape(L, D)

    @pl.when(is2 & (p == 1))
    def _():
        load_again(0).wait()
        load_again(1).wait()
        ys = all_factors()
        g_q = bf16(nn(gather16(), bf16(jnp.where(head_mask(L), nn(ys, W[13]), 0.0))))
        gp, gg21 = norm_back(o.DM[:, 0, :], gain(2, 1), nt(g_q, W[12]))
        o.GD[...] = nn(pick(13), ys) + gp
        gd_copy().start()
        o.gg[2] = jnp.concatenate([jnp.zeros((1, D), F32), gg21], axis=1)
        gain2(1)
        outer(0, o.keep[0], g_q)
        outer(1, ys, spread(o.keep[1]))
        dw_done()

    @pl.when(is2 & (p == 2))
    def _():
        zs = all_factors()
        g_ca = bf16(nn(pick(12), zs))
        outer(0, zs, spread(g_ca))
        outer(1, bf16(nn(pick(13), zs)), bf16(nn(pick(14), zs)))
        dw_done()


    def dg_copy(i, s_, p_):
        return remote(o.ROWS.at[c * 16 + p_ * 4 + s_], o.dgrow, o.sdg.at[i], o.rdg.at[0], dev(s_, p_, c))

    @pl.when(is2 & (p == 0))
    def _():
        load_again(0).wait()
        load_again(1).wait()
        gd_copy().wait_recv()
        g_sb = bf16(o.GD[...])
        g_sv = bf16(nn(g_sb, W[13]))
        gp, gg20 = norm_back(o.DI[:, 0, :], gain(2, 0), nt(g_sv, W[12]))
        o.ROWS[:, 0, :] = o.GD[...] + gp

        def go(i, s_, p_):
            me = (s_ == s) & (p_ == p)
            when(me, lambda: local(o.ROWS.at[row], o.dgrow, o.rdg.at[0]).start())
            unless(me, lambda: dg_copy(i, s_, p_).start())

        to_core(go)
        o.gg[2] = jnp.concatenate([gg20, jnp.zeros((1, D), F32)], axis=1)
        gain2(0)
        outer(0, o.keep[0], g_sv)
        outer(1, g_sb, o.keep[1])
        dw_done()


    @pl.when(is1)
    def _():
        def go(t):
            jj, k = t // K, lax.rem(t, K)
            b = 4 * (1 + jj) + p
            fin_local(b, jj, k).wait()
            fin_sib(b, jj, k).wait_send()
            fin_sib_in(jj, k).wait_recv()

        loop(2 * K, go)

    @pl.when(is0 & (p < 2))
    def _():
        def go(k):
            fin_local(p, 0, k).wait()
            fin_sib(p, 0, k).wait_send()
            fin_sib_in(0, k).wait_recv()
            fin_y_in(k, 0).wait_recv()
            fin_y_in(k, 1).wait_recv()

        loop(K, go)

    @pl.when(is0 & (p >= 2))
    def _():
        def go(k):
            fin_y(k, 0).wait_send()
            fin_y(k, 1).wait_send()

        loop(K, go)

    @pl.when(is3 | (is2 & (p < 3)))
    def _():
        dw_out(0).wait()
        dw_out(1).wait()

    local(o.dgrow, o.dgrow, o.rdg.at[0]).wait()
    o.dec_grad[...] = bf16(o.dgrow[...])
    out_enc.wait()

    def share(total):
        wide = D // 4
        for i in range(4):
            @pl.when(p == i)
            def _(i=i):
                for r in range(2):
                    o.gain_out[r:r + 1, :] = total[:, r * D + i * wide:r * D + (i + 1) * wide]

    @pl.when(s != 2)
    def _():
        local(o.GB, o.GB, o.rgb.at[0]).wait()
        share(jnp.sum(o.GB[:, 0, :], axis=0, keepdims=True))

    @pl.when(is2)
    def _():
        two = o.GB.at[pl.ds(0, 2)]
        local(two, two, o.rgb.at[0]).wait()
        share(o.GB[0] + o.GB[1])

    loop(4, lambda i: unless(i == s, lambda: remote(gains, o.gall.at[s], o.sg.at[i], o.rg.at[0], dev(i, p, c)).wait_send()))
    when(is2, lambda: loop(2, lambda i: unless((p == 0) & (i == c), lambda: remote(
        dec, o.DI.at[four], o.spre.at[i], o.rdi.at[0], dev(2, 0, i)).wait_send())))
    when(is3, lambda: loop(4, lambda i: unless((p == 2 + i // 2) & (lax.rem(i, 2) == c), lambda: remote(
        cot, o.CR.at[four], o.scr.at[i], o.rcr.at[0], dev(3, 2 + i // 2, lax.rem(i, 2))).wait_send())))

    @pl.when(is2 & (p == 0))
    def _():
        remote(o.DM, o.DM, o.sdm.at[16], o.rdm.at[1], dev(2, 1, c)).wait_send()
        others(lambda i, s_, p_: remote(o.DM.at[0], o.dmrow, o.sdm.at[i], o.rdm.at[0], dev(s_, p_, c)))
        others(dg_copy)
        loop(4, lambda i: unless(i == p, lambda: gain2_copy(0, i).wait_send()))

    @pl.when(is2 & (p == 1))
    def _():
        gd_copy().wait_send()
        loop(4, lambda i: unless(i == p, lambda: gain2_copy(1, i).wait_send()))

    loop(8, lambda i: unless(is3 & (i == p * 2 + c), lambda: remote(
        o.drow, o.DR.at[row], o.sd1.at[i], o.rdr.at[0], dev(3, i // 2, lax.rem(i, 2))).wait_send()))

    @pl.when(up_dev)
    def _():
        act_copy().wait_send()
        gp_copy().wait_send()
        loop(32, lambda i: unless(i == lin, lambda: gt_copy(i).wait_send()))

    @pl.when(down_dev)
    def _():
        gh_copy().wait_send()
        loop(4, lambda i: unless(i == j, lambda: pb_copy(i).wait_send()))

        def go(i):
            far, me, _ = out_copy(i)
            unless(me, lambda: far.wait_send())

        loop(8, go)

    for i in range(2):
        unless(is2 & (p == 1 + i), lambda i=i: fb_copy(i).wait_send())
    for sec in (0, 1, 3):
        loop(8, lambda i, sec=sec: unless((s == sec) & (i == p * 2 + c), lambda: gain_copy(sec, i).wait_send()))

    for n in (10, 11):
        sib(ORDER[n], n % 2).wait_send()

    def spent(t):
        st, k = t // K, lax.rem(t, K)
        diag(st, k, True).wait_send()
        straight(1, st, k, True).wait_send()
        straight(2, st, k, True).wait_send()
        when((st > 0) & (s != 1), lambda: down(st, k).wait_send())
        when((st == 0) & (s > 0), lambda: down(st, k).wait_send())

    loop(3 * K, spent)


OUTS = dict(dw=(2, D, D), enc_grad=(L, D), probs=(HEADS, L, L))
ROWS_OUT = dict(dec_out=((1, D), BF), dec_grad=((1, D), BF), gain_out=((2, D // 4), F32))


def fused(w, xall, dec8, gains):
    names = [*OUTS, *ROWS_OUT, *SCRATCH, *SEMS]
    hbm, vmem = pl.BlockSpec(memory_space=pl.ANY), pl.BlockSpec(memory_space=pltpu.VMEM)
    return pl.pallas_call(
        functools.partial(kernel, names),
        out_shape=[jax.ShapeDtypeStruct(v, BF) for v in OUTS.values()] + [jax.ShapeDtypeStruct(*v) for v in ROWS_OUT.values()],
        in_specs=[hbm, hbm, vmem, vmem],
        out_specs=[hbm] * len(OUTS) + [vmem] * len(ROWS_OUT),
        scratch_shapes=[pltpu.VMEM(*v) for v in SCRATCH.values()] + [pltpu.SemaphoreType.DMA(v) for v in SEMS.values()],
        compiler_params=pltpu.CompilerParams(collective_id=0, has_side_effects=True, vmem_limit_bytes=(64 << 20) - (128 << 10)),
        name="fused",
    )(w, xall, dec8, gains)


def body(enc_in, dec_in, lengths, weights, gains, dec_cot):
    s, p = lax.axis_index("section"), lax.axis_index("pair")
    dps = lax.axis_size("dp")
    dec8 = jnp.concatenate([f32(dec_in[:, 0]), f32(dec_cot[:, 0]), jnp.broadcast_to(f32(lengths), (4, D)), jnp.zeros((4, D), F32)], axis=0)
    dw, enc_grad, _, dec_out, dec_grad, gg = fused(weights[0], enc_in, dec8, gains[0])
    if dps > 2:
        groups = [[i for i in range(dps) if i % 2 == c] for c in range(2)]
        dw = bf16(lax.psum(dw, "dp", axis_index_groups=groups))
        gg = lax.psum(gg, "dp", axis_index_groups=groups)
    unused = (p >= 2) & (s == 0) | (p == 3) & (s == 2)
    dw = jnp.where(unused, 0.0, f32(jnp.concatenate([dw[0], dw[1]], axis=1)))
    return dec_out[None], enc_grad[None], dec_grad[None], dw[None], gg[None]


def solution(mesh):
    rows, both = P(None, ("pair", "dp"), None), P("section", ("pair", "dp"), None)
    return jax.shard_map(
        body, mesh=mesh,
        in_specs=(rows, rows, P(None, ("pair", "dp")), P("section", None, "pair"), P("section", None, None), rows),
        out_specs=(both, both, both, P("section", None, "pair"), P("section", None, "pair")),
        check_vma=False)
```
